32 devices in a mesh: dp: 4 (over x, core), fsdp: 8 (over z, y).
Axes of the slice: x: 2, y: 2, z: 4, core: 2. Of those that a mesh axis runs over, the one named last changes fastest.
Arguments:
- tokens: bfloat16 [4096, 2048], P(('dp', 'fsdp')), may hold values from -6 to 6
- triple_weight: bfloat16 [2048, 6144], P(('dp', 'fsdp')), may hold values from -0.125 to 0.125
- output_weight: bfloat16 [2048, 2048], P(('dp', 'fsdp')), may hold values from -1 to 1
- up_weight: bfloat16 [2048, 8192], P(('dp', 'fsdp')), may hold values from -0.125 to 0.125
- down_weight: bfloat16 [8192, 2048], P(('dp', 'fsdp')), may hold values from -0.0625 to 0.0625
- first_gain: bfloat16 [2048], P(('dp', 'fsdp')), may hold values from 0.5 to 1.5
- second_gain: bfloat16 [2048], P(('dp', 'fsdp')), may hold values from 0.5 to 1.5
- cotangent: bfloat16 [4096, 2048], P(('dp', 'fsdp')), may hold values from -6 to 6
- frame_counts: int32 [4, 2], P('dp'), may hold values from 1 to 4
- text_counts: int32 [4, 2, 4], P('dp'), may hold values from 0 to 32
- action_counts: int32 [4, 2, 4], P('dp'), may hold values from 0 to 2
Outputs:
- layer_output: bfloat16 [4096, 2048], P(('dp', 'fsdp'))
- token_grad: bfloat16 [4096, 2048], P(('dp', 'fsdp'))
- triple_grad: float32 [2048, 6144], P(('dp', 'fsdp'))
- output_grad: float32 [2048, 2048], P(('dp', 'fsdp'))
- up_grad: float32 [2048, 8192], P(('dp', 'fsdp'))
- down_grad: float32 [8192, 2048], P(('dp', 'fsdp'))
- first_gain_grad: float32 [2048], P(('dp', 'fsdp'))
- second_gain_grad: float32 [2048], P(('dp', 'fsdp'))
The draws below stay inside these ranges and needn't reach their ends.
All inputs are finite; a program needn't handle non-finite values.
Results may differ from the reference program's by a relative error of at most 0.015.
Values may be sent and summed in bfloat16 or wider, within the bound.
No kernel may reach another device: no remote copies, remote signals or barrier semaphores. Data moves between devices by JAX's collectives and lax.ppermute only.
A program may use at most 512 MiB of HBM per device.

```python
import math
import jax
import jax.numpy as jnp
from jax import lax

D = 2048
HEADS = 16
HEAD = 128
FF = 8192
IMG = 576
TEXT = 32
ACTION = 2
MAXF = 4
PACK = 1024
TOKENS = 4096
N_DP = 4


def place_ends(values, rng, smallest, high):
    longest = values.shape.index(max(values.shape))
    spots = []
    for shift in (0, 1):
        where = [jax.random.randint(jax.random.fold_in(rng, axis), (), 0, length) for axis, length in enumerate(values.shape)]
        where[longest] = (where[longest] + shift) % values.shape[longest]
        spots.append(tuple(where))
    return values.at[spots[0]].set(smallest).at[spots[1]].set(high)


def levels(key, extent, cuts, low, largest):
    factor_of = 1.0
    for dim, blocks in cuts:
        steps = jax.random.uniform(jax.random.fold_in(jax.random.fold_in(key, 6), dim), (blocks,), jnp.float32, low / len(cuts), largest / len(cuts))
        factor_of = factor_of * jnp.repeat(jnp.exp(steps), extent[dim] // blocks).reshape((-1,) + (1,) * (len(extent) - 1 - dim))
    return factor_of


def normal_values(rng, extent, scale, reach, split=(), kind=jnp.bfloat16):
    entries = scale * jax.random.normal(rng, extent, jnp.float32)
    if split:
        entries = entries * levels(rng, extent, split, -0.22, 0.18)
    return jnp.clip(entries, -reach, reach).astype(kind)


def setup_inputs(seed: int = 0) -> dict:
    keys = jax.random.split(jax.random.key(seed), 12)
    tokens = normal_values(keys[0], (TOKENS, D), 1.0, 6.0, ((0, 32),))
    triple_weight = normal_values(keys[1], (D, 3 * D), D ** -0.5, 0.125, ((0, 32),))
    output_weight = normal_values(keys[2], (D, D), (max(1, D // 64)) ** -0.5, 1.0, ((0, 32),))
    up_weight = normal_values(keys[3], (D, FF), D ** -0.5, 0.125, ((0, 32),))
    down_weight = normal_values(keys[4], (FF, D), FF ** -0.5, 0.0625, ((0, 32),))
    first_gain = jnp.clip(1.0 + 0.1 * jax.random.normal(keys[5], (D,), jnp.float32), 0.5, 1.5).astype(jnp.bfloat16)
    second_gain = jnp.clip(1.0 + 0.1 * jax.random.normal(keys[6], (D,), jnp.float32), 0.5, 1.5).astype(jnp.bfloat16)
    cotangent = normal_values(keys[7], (TOKENS, D), 1.0, 6.0, ((0, 32),))
    frame_counts = place_ends(jax.random.randint(keys[8], (N_DP, 2), 1, MAXF + 1), jax.random.fold_in(keys[8], 1), 1, MAXF).astype(jnp.int32)
    text_counts = place_ends(jax.random.randint(keys[9], (N_DP, 2, MAXF), 0, TEXT + 1), jax.random.fold_in(keys[9], 1), 0, TEXT).astype(jnp.int32)
    action_counts = place_ends(jax.random.randint(keys[10], (N_DP, 2, MAXF), 0, ACTION + 1), jax.random.fold_in(keys[10], 1), 0, ACTION).astype(jnp.int32)
    return dict(tokens=tokens, triple_weight=triple_weight, output_weight=output_weight, up_weight=up_weight, down_weight=down_weight, first_gain=first_gain, second_gain=second_gain, cotangent=cotangent, frame_counts=frame_counts, text_counts=text_counts, action_counts=action_counts)


EPSILON = 1e-05
MASKED = -1e+30
HIGHEST = lax.Precision.HIGHEST

@jax.custom_vjp
def low(v):
    return lax.optimization_barrier(v.astype(jnp.bfloat16)).astype(jnp.float32)

@jax.custom_vjp
def low_back(v):
    return v

def low_keep(v):
    return (low(v), None)

def low_pass(kept, grad):
    return (grad,)

def back_keep(v):
    return (v, None)

def back_low(kept, grad):
    return (low(grad),)
low.defvjp(low_keep, low_pass)
low_back.defvjp(back_keep, back_low)

def clip_layout(frame_counts, text_counts, action_counts, pack_length):
    frame_slot = jnp.arange(text_counts.shape[-1], dtype=jnp.int32)
    frame_live = frame_slot < frame_counts[..., None]
    frame_sizes = jnp.where(frame_live, IMG + text_counts + action_counts, 0)
    clip_lengths = lax.optimization_barrier(jnp.sum(frame_sizes, axis=-1))
    first_end = clip_lengths[..., 0:1]
    second_end = first_end + clip_lengths[..., 1:2]
    places = jnp.arange(pack_length, dtype=jnp.int32)
    segment = (places >= first_end).astype(jnp.int32) + (places >= second_end).astype(jnp.int32)
    starts = jnp.where(segment == 0, 0, jnp.where(segment == 1, first_end, second_end))
    return (segment, (places - starts).astype(jnp.int32))

def rotary_tables(position):
    half_width = HEAD // 2
    frequency = jnp.exp(jnp.arange(half_width, dtype=jnp.float32) * (-2.0 * math.log(10000.0) / HEAD))
    angles = position.astype(jnp.float32)[:, None] * frequency[None, :]
    return (jnp.cos(angles)[:, None, :], jnp.sin(angles)[:, None, :])

def rotate(vectors, cosine, sine_table):
    half_width = vectors.shape[-1] // 2
    former = vectors[..., :half_width]
    latter = vectors[..., half_width:]
    return jnp.concatenate([former * cosine - latter * sine_table, latter * cosine + former * sine_table], axis=-1)

def norm_rows(values, gain_vector):
    centred = values - lax.optimization_barrier(jnp.mean(values, axis=-1, keepdims=True))
    variance = lax.optimization_barrier(jnp.mean(centred * centred, axis=-1, keepdims=True))
    return centred * lax.rsqrt(variance + EPSILON) * gain_vector

def attention(queries, keys_all, values_all, segment):
    block_rows = min(512, PACK)
    block_count = PACK // block_rows
    places = jnp.arange(PACK, dtype=jnp.int32)
    score_scale = HEAD ** (-0.5)

    def one_block(block_index):
        pack_index = block_index // block_count
        start_row = block_index % block_count * block_rows
        query_block = lax.dynamic_slice_in_dim(queries[pack_index], start_row, block_rows, 0)
        pack_segment = segment[pack_index]
        query_segment = lax.dynamic_slice_in_dim(pack_segment, start_row, block_rows, 0)
        query_places = start_row + jnp.arange(block_rows, dtype=jnp.int32)
        allowed = (query_segment[:, None] == pack_segment[None, :]) & (places[None, :] <= query_places[:, None])
        scores = jnp.einsum('qhd,khd->hqk', query_block, keys_all[pack_index], precision=HIGHEST) * score_scale
        scores = low_back(jnp.where(allowed[None], scores, MASKED))
        row_max = lax.optimization_barrier(jnp.max(scores, axis=-1, keepdims=True))
        weights = jnp.exp(scores - row_max)
        probs = low(weights / lax.optimization_barrier(jnp.sum(weights, axis=-1, keepdims=True)))
        return jnp.einsum('hqk,khd->qhd', probs, values_all[pack_index], precision=HIGHEST)
    blocks = lax.map(jax.checkpoint(one_block), jnp.arange(N_DP * block_count, dtype=jnp.int32))
    return blocks.reshape(N_DP * PACK, HEADS * HEAD)

def layer(inputs, triple_weight, output_weight, up_weight, down_weight, first_gain, second_gain, segment, position):
    width = HEADS * HEAD
    token_count = inputs.shape[0]
    cosine, sine_table = rotary_tables(position)
    normed = low(norm_rows(inputs, first_gain))
    mixed = jnp.dot(normed, triple_weight, precision=HIGHEST)
    queries = low_back(mixed[:, :width]).reshape(token_count, HEADS, HEAD)
    keys_all = low_back(mixed[:, width:2 * width]).reshape(token_count, HEADS, HEAD)
    values_all = low(low_back(mixed[:, 2 * width:])).reshape(token_count, HEADS, HEAD)
    queries = low(rotate(queries, cosine, sine_table))
    keys_all = low(rotate(keys_all, cosine, sine_table))
    block_shape = (N_DP, PACK, HEADS, HEAD)
    attended = attention(queries.reshape(block_shape), keys_all.reshape(block_shape), values_all.reshape(block_shape), segment)
    attended = low(low_back(attended))
    middle = inputs + low_back(jnp.dot(attended, output_weight, precision=HIGHEST))
    normed_two = low(norm_rows(middle, second_gain))
    hidden = low_back(jnp.dot(normed_two, up_weight, precision=HIGHEST))
    activation = low(jax.nn.gelu(hidden))
    return middle + jnp.dot(activation, down_weight, precision=HIGHEST)

def reference(tokens, triple_weight, output_weight, up_weight, down_weight, first_gain, second_gain, cotangent, frame_counts, text_counts, action_counts):
    segment, position = clip_layout(frame_counts, text_counts, action_counts, PACK)
    position = position.reshape(-1)

    def forward(inputs, triple_f, output_f, up_f, down_f, gain_a, gain_b):
        return layer(inputs, triple_f, output_f, up_f, down_f, gain_a, gain_b, segment, position)
    output, pullback = jax.vjp(forward, tokens.astype(jnp.float32), triple_weight.astype(jnp.float32), output_weight.astype(jnp.float32), up_weight.astype(jnp.float32), down_weight.astype(jnp.float32), first_gain.astype(jnp.float32), second_gain.astype(jnp.float32))
    grads = pullback(cotangent.astype(jnp.float32))
    return (output.astype(jnp.bfloat16), grads[0].astype(jnp.bfloat16), grads[1], grads[2], grads[3], grads[4], grads[5], grads[6])
```

```python
import math

import jax
import jax.numpy as jnp
from jax import lax
from jax.experimental import pallas as pl
from jax.experimental.pallas import tpu as pltpu
from jax.sharding import PartitionSpec as P

HEADS = 16
HEAD = 128
IMG = 576


EPSILON = 1e-05
MASKED = -1e30


def clip_layout(frame_counts, text_counts, action_counts, pack_length):
    frame_slot = jnp.arange(text_counts.shape[-1], dtype=jnp.int32)
    frame_live = frame_slot < frame_counts[..., None]
    frame_sizes = jnp.where(frame_live, IMG + text_counts + action_counts, 0)
    clip_lengths = jnp.sum(frame_sizes, axis=-1)
    first_end = clip_lengths[..., 0:1]
    second_end = first_end + clip_lengths[..., 1:2]
    places = jnp.arange(pack_length, dtype=jnp.int32)
    segment = (places >= first_end).astype(jnp.int32) + (places >= second_end).astype(jnp.int32)
    starts = jnp.where(segment == 0, 0, jnp.where(segment == 1, first_end, second_end))
    return (segment, places - starts)


def rotary_tables(position):
    half_width = HEAD // 2
    frequency = jnp.exp(
        jnp.arange(half_width, dtype=jnp.float32) * (-2.0 * math.log(10000.0) / HEAD)
    )
    angles = position.astype(jnp.float32)[:, None] * frequency[None, :]
    return (jnp.cos(angles)[:, None, :], jnp.sin(angles)[:, None, :])


def rotate(vectors, cosine, sine_table):
    half_width = vectors.shape[-1] // 2
    former = vectors[..., :half_width]
    latter = vectors[..., half_width:]
    return jnp.concatenate(
        [former * cosine - latter * sine_table, latter * cosine + former * sine_table], axis=-1
    )


def unrotate(gradient, cosine, sine_table):
    half_width = gradient.shape[-1] // 2
    former = gradient[..., :half_width]
    latter = gradient[..., half_width:]
    return jnp.concatenate(
        [former * cosine + latter * sine_table, latter * cosine - former * sine_table], axis=-1
    )


def norm_rows(values, gain_vector):
    centred = values - jnp.mean(values, axis=-1, keepdims=True)
    variance = jnp.mean(centred * centred, axis=-1, keepdims=True)
    return centred * lax.rsqrt(variance + EPSILON) * gain_vector


def block_allowed(query_segment, query_places, key_segment, key_place):
    return (query_segment[:, None] == key_segment[None, :]) & (
        key_place[None, :] <= query_places[:, None]
    )


def block_scores(queries, key_block, allowed):
    scores = jnp.einsum(
        "qhd,khd->hqk", queries, key_block, preferred_element_type=jnp.float32
    ) * HEAD ** (-0.5)
    return jnp.where(allowed[None], scores, MASKED)


def block_probs(queries, key_block, allowed, row_max, row_sum):
    scores = block_scores(queries, key_block, allowed)
    return jnp.where(allowed[None], jnp.exp(scores - row_max[..., None]) / row_sum[..., None], 0.0)


def softmax_stats(queries, key_blocks, layout_parts):
    query_segment, query_places, key_segments, key_places = layout_parts
    row_count, head_count = (queries.shape[0], queries.shape[1])
    start_state = (
        jnp.full((head_count, row_count), MASKED, jnp.float32),
        jnp.zeros((head_count, row_count), jnp.float32),
    )

    def advance(state, block_inputs):
        key_block, key_segment, key_place = block_inputs
        allowed = block_allowed(query_segment, query_places, key_segment, key_place)

        def update(current):
            row_max, row_sum = current
            scores = block_scores(queries, key_block, allowed)
            new_max = jnp.maximum(row_max, jnp.max(scores, axis=-1))
            weights = jnp.where(allowed[None], jnp.exp(scores - new_max[..., None]), 0.0)
            return (new_max, row_sum * jnp.exp(row_max - new_max) + jnp.sum(weights, axis=-1))

        return (lax.cond(jnp.any(allowed), update, lambda current: current, state), None)

    final_state, unused = lax.scan(advance, start_state, (key_blocks, key_segments, key_places))
    return final_state


def attention_output(queries, key_blocks, value_blocks, layout_parts, row_max, row_sum):
    query_segment, query_places, key_segments, key_places = layout_parts

    def advance(accum, block_inputs):
        key_block, value_block, key_segment, key_place = block_inputs
        allowed = block_allowed(query_segment, query_places, key_segment, key_place)

        def update(current):
            probs = block_probs(queries, key_block, allowed, row_max, row_sum).astype(jnp.bfloat16)
            return current + jnp.einsum(
                "hqk,khd->qhd", probs, value_block, preferred_element_type=jnp.float32
            )

        return (lax.cond(jnp.any(allowed), update, lambda current: current, accum), None)

    attended, unused = lax.scan(
        advance,
        jnp.zeros(queries.shape, jnp.float32),
        (key_blocks, value_blocks, key_segments, key_places),
    )
    return attended


def attention_backward(
    queries, grad_attended, delta_rows, key_blocks, value_blocks, layout_parts, row_max, row_sum
):
    query_segment, query_places, key_segments, key_places = layout_parts
    score_scale = HEAD ** (-0.5)

    def advance(grad_query, block_inputs):
        key_block, value_block, key_segment, key_place = block_inputs
        allowed = block_allowed(query_segment, query_places, key_segment, key_place)

        def update(current):
            probs = block_probs(queries, key_block, allowed, row_max, row_sum)
            grad_probs = jnp.einsum(
                "qhd,khd->hqk", grad_attended, value_block, preferred_element_type=jnp.float32
            )
            grad_scores = (probs * (grad_probs - delta_rows[..., None])).astype(jnp.bfloat16)
            new_query = (
                current
                + jnp.einsum(
                    "hqk,khd->qhd", grad_scores, key_block, preferred_element_type=jnp.float32
                )
                * score_scale
            )
            return (new_query, ())

        def bypass(current):
            return (current, ())

        return lax.cond(jnp.any(allowed), update, bypass, grad_query)

    grad_query, terms = lax.scan(
        advance,
        jnp.zeros(queries.shape, jnp.float32),
        (key_blocks, value_blocks, key_segments, key_places),
    )
    return (grad_query, None, None)


def project_front(inputs, triple_full, gain_full, cosine, sine_table):
    row_count, width = inputs.shape
    normed = norm_rows(inputs, gain_full.astype(jnp.float32)).astype(jnp.bfloat16)
    mixed = jnp.dot(normed, triple_full, preferred_element_type=jnp.float32)
    queries = rotate(mixed[:, :width].reshape(row_count, HEADS, HEAD), cosine, sine_table).astype(
        jnp.bfloat16
    )
    keys_local = (
        rotate(mixed[:, width : 2 * width].reshape(row_count, HEADS, HEAD), cosine, sine_table)
        .astype(jnp.bfloat16)
        .reshape(row_count, width)
    )
    values_local = mixed[:, 2 * width :].astype(jnp.bfloat16)
    return (normed, queries, keys_local, values_local)


def run_attention(queries, gathered, layout_parts):
    block_count = layout_parts[2].shape[0]
    key_blocks = gathered[0].reshape(block_count, -1, HEADS, HEAD)
    value_blocks = gathered[1].reshape(block_count, -1, HEADS, HEAD)
    row_max, row_sum = softmax_stats(queries, key_blocks, layout_parts)
    attended = attention_output(queries, key_blocks, value_blocks, layout_parts, row_max, row_sum)
    return (attended, key_blocks, value_blocks, row_max, row_sum)


def finish_layer(inputs, attended, output_full, up_full, down_full, second_full):
    row_count, width = inputs.shape
    attended_low = attended.reshape(row_count, width).astype(jnp.bfloat16)
    middle = inputs + jnp.dot(attended_low, output_full, preferred_element_type=jnp.float32)
    normed_two = norm_rows(middle, second_full.astype(jnp.float32)).astype(jnp.bfloat16)
    hidden = jnp.dot(normed_two, up_full, preferred_element_type=jnp.float32)
    activation = jax.nn.gelu(hidden).astype(jnp.bfloat16)
    result = middle + jnp.dot(activation, down_full, preferred_element_type=jnp.float32)
    return (result, attended_low, middle, normed_two, hidden, activation)


def whole_rows_body(
    tokens,
    triple_weight,
    output_weight,
    up_weight,
    down_weight,
    first_gain,
    second_gain,
    cotangent,
    frame_counts,
    text_counts,
    action_counts,
):
    row_count, width = tokens.shape
    pack_length = row_count * lax.axis_size("fsdp")
    first_place = lax.axis_index("fsdp") * row_count
    segment, position = clip_layout(frame_counts[0], text_counts[0], action_counts[0], pack_length)
    block_rows = min(1024, pack_length)
    block_count = pack_length // block_rows
    query_places = first_place + jnp.arange(row_count, dtype=jnp.int32)
    own_segment = lax.dynamic_slice_in_dim(segment, first_place, row_count, 0)
    layout_parts = (
        own_segment,
        query_places,
        segment.reshape(block_count, block_rows),
        jnp.arange(pack_length, dtype=jnp.int32).reshape(block_count, block_rows),
    )
    cosine, sine_table = rotary_tables(
        lax.dynamic_slice_in_dim(position, first_place, row_count, 0)
    )
    inputs = tokens.astype(jnp.float32)
    attention_set = (
        lax.all_gather(triple_weight, ("dp", "fsdp"), axis=0, tiled=True),
        lax.all_gather(output_weight, ("dp", "fsdp"), axis=0, tiled=True),
        lax.all_gather(first_gain, ("dp", "fsdp"), axis=0, tiled=True),
    )
    normed, queries, keys_local, values_local = project_front(
        inputs, attention_set[0], attention_set[2], cosine, sine_table
    )
    gathered = (
        lax.all_gather(keys_local, "fsdp", axis=0, tiled=True),
        lax.all_gather(values_local, "fsdp", axis=0, tiled=True),
    )
    attended, key_blocks, value_blocks, row_max, row_sum = run_attention(
        queries, gathered, layout_parts
    )
    feedforward_set = (
        lax.all_gather(up_weight, ("dp", "fsdp"), axis=0, tiled=True),
        lax.all_gather(down_weight, ("dp", "fsdp"), axis=0, tiled=True),
        lax.all_gather(second_gain, ("dp", "fsdp"), axis=0, tiled=True),
    )
    kept_parts = finish_layer(
        inputs,
        attended,
        attention_set[1],
        feedforward_set[0],
        feedforward_set[1],
        feedforward_set[2],
    )
    layer_output = kept_parts[0].astype(jnp.bfloat16)
    attention_set = (
        lax.all_gather(triple_weight, ("dp", "fsdp"), axis=0, tiled=True),
        lax.all_gather(output_weight, ("dp", "fsdp"), axis=0, tiled=True),
        lax.all_gather(first_gain, ("dp", "fsdp"), axis=0, tiled=True),
    )
    normed, queries, keys_local, values_local = project_front(
        inputs, attention_set[0], attention_set[2], cosine, sine_table
    )
    gathered = (
        lax.all_gather(keys_local, "fsdp", axis=0, tiled=True),
        lax.all_gather(values_local, "fsdp", axis=0, tiled=True),
    )
    attended, key_blocks, value_blocks, row_max, row_sum = run_attention(
        queries, gathered, layout_parts
    )
    feedforward_set = (
        lax.all_gather(up_weight, ("dp", "fsdp"), axis=0, tiled=True),
        lax.all_gather(down_weight, ("dp", "fsdp"), axis=0, tiled=True),
        lax.all_gather(second_gain, ("dp", "fsdp"), axis=0, tiled=True),
    )
    kept_parts = finish_layer(
        inputs,
        attended,
        attention_set[1],
        feedforward_set[0],
        feedforward_set[1],
        feedforward_set[2],
    )
    unused_result, attended_low, middle, normed_two, hidden, activation = kept_parts
    down_term = jnp.einsum("rf,rd->fd", activation, cotangent, preferred_element_type=jnp.float32)
    grad_activation = jnp.einsum(
        "rd,fd->rf", cotangent, feedforward_set[1], preferred_element_type=jnp.float32
    )
    unused_gelu, gelu_pull = jax.vjp(jax.nn.gelu, hidden)
    grad_hidden = gelu_pull(grad_activation)[0].astype(jnp.bfloat16)
    up_term = jnp.einsum("rd,rf->df", normed_two, grad_hidden, preferred_element_type=jnp.float32)
    grad_normed_two = jnp.einsum(
        "rf,df->rd", grad_hidden, feedforward_set[0], preferred_element_type=jnp.float32
    )
    unused_second, second_pull = jax.vjp(norm_rows, middle, feedforward_set[2].astype(jnp.float32))
    grad_middle_norm, second_gain_term = second_pull(grad_normed_two)
    grad_middle = cotangent.astype(jnp.float32) + grad_middle_norm
    feedforward_sums = (
        lax.psum_scatter(up_term, ("dp", "fsdp"), scatter_dimension=0, tiled=True),
        lax.psum_scatter(down_term, ("dp", "fsdp"), scatter_dimension=0, tiled=True),
        lax.psum_scatter(second_gain_term, ("dp", "fsdp"), scatter_dimension=0, tiled=True),
    )
    grad_branch = grad_middle.astype(jnp.bfloat16)
    output_term = jnp.einsum(
        "rd,re->de", attended_low, grad_branch, preferred_element_type=jnp.float32
    )
    grad_attended = (
        jnp.einsum("re,de->rd", grad_branch, attention_set[1], preferred_element_type=jnp.float32)
        .astype(jnp.bfloat16)
        .reshape(row_count, HEADS, HEAD)
    )
    delta_rows = jnp.sum(grad_attended.astype(jnp.float32) * attended, axis=-1).T
    score_scale = HEAD ** (-0.5)
    grad_query = attention_backward(
        queries, grad_attended, delta_rows, key_blocks, value_blocks, layout_parts, row_max, row_sum
    )[0]
    pack_stats = (
        lax.all_gather(row_max.T, "fsdp", axis=0, tiled=True),
        lax.all_gather(row_sum.T, "fsdp", axis=0, tiled=True),
        lax.all_gather(delta_rows.T, "fsdp", axis=0, tiled=True),
    )
    own_keys = keys_local.reshape(row_count, HEADS, HEAD)
    own_values = values_local.reshape(row_count, HEADS, HEAD)
    empty_grads = jnp.zeros((row_count, HEADS, HEAD), jnp.float32)
    query_piece = lax.all_gather(queries, "fsdp", axis=0, tiled=True)
    grad_piece = lax.all_gather(grad_attended, "fsdp", axis=0, tiled=True)
    piece_rows = query_piece.shape[0]
    block_size = min(1024, piece_rows)
    block_total = piece_rows // block_size

    def advance(current, block_index):
        offset = block_index * block_size
        query_part = lax.dynamic_slice_in_dim(query_piece, offset, block_size, 0)
        grad_part = lax.dynamic_slice_in_dim(grad_piece, offset, block_size, 0)
        max_part = lax.dynamic_slice_in_dim(pack_stats[0], offset, block_size, 0).T
        sum_part = lax.dynamic_slice_in_dim(pack_stats[1], offset, block_size, 0).T
        delta_part = lax.dynamic_slice_in_dim(pack_stats[2], offset, block_size, 0).T
        part_segment = lax.dynamic_slice_in_dim(segment, offset, block_size, 0)
        part_places = offset + jnp.arange(block_size, dtype=jnp.int32)
        allowed = block_allowed(part_segment, part_places, own_segment, query_places)

        def update(pair):
            probs = block_probs(query_part, own_keys, allowed, max_part, sum_part)
            grad_probs = jnp.einsum(
                "qhd,khd->hqk", grad_part, own_values, preferred_element_type=jnp.float32
            )
            grad_scores = (probs * (grad_probs - delta_part[..., None])).astype(jnp.bfloat16)
            grad_key = (
                pair[0]
                + jnp.einsum(
                    "hqk,qhd->khd", grad_scores, query_part, preferred_element_type=jnp.float32
                )
                * score_scale
            )
            grad_value = pair[1] + jnp.einsum(
                "hqk,qhd->khd",
                probs.astype(jnp.bfloat16),
                grad_part,
                preferred_element_type=jnp.float32,
            )
            return (grad_key, grad_value)

        return (lax.cond(jnp.any(allowed), update, lambda pair: pair, current), None)

    result, unused = lax.scan(
        advance, (empty_grads, empty_grads), jnp.arange(block_total, dtype=jnp.int32)
    )
    key_grad_sum = result[0].reshape(row_count, width)
    value_grad_sum = result[1].reshape(row_count, width)
    grad_query_full = (
        unrotate(grad_query, cosine, sine_table).reshape(row_count, width).astype(jnp.bfloat16)
    )
    grad_key_full = (
        unrotate(key_grad_sum.reshape(row_count, HEADS, HEAD), cosine, sine_table)
        .reshape(row_count, width)
        .astype(jnp.bfloat16)
    )
    grad_value_full = value_grad_sum.astype(jnp.bfloat16)
    grad_mixed = jnp.concatenate([grad_query_full, grad_key_full, grad_value_full], axis=1)
    triple_term = jnp.einsum("rd,re->de", normed, grad_mixed, preferred_element_type=jnp.float32)
    grad_normed = jnp.einsum(
        "re,de->rd", grad_mixed, attention_set[0], preferred_element_type=jnp.float32
    )
    unused_first, first_pull = jax.vjp(norm_rows, inputs, attention_set[2].astype(jnp.float32))
    grad_input_norm, first_gain_term = first_pull(grad_normed)
    token_grad = (grad_middle + grad_input_norm).astype(jnp.bfloat16)
    attention_sums = (
        lax.psum_scatter(triple_term, ("dp", "fsdp"), scatter_dimension=0, tiled=True),
        lax.psum_scatter(output_term, ("dp", "fsdp"), scatter_dimension=0, tiled=True),
        lax.psum_scatter(first_gain_term, ("dp", "fsdp"), scatter_dimension=0, tiled=True),
    )
    return (
        layer_output,
        token_grad,
        attention_sums[0],
        attention_sums[1],
        feedforward_sums[0],
        feedforward_sums[1],
        attention_sums[2],
        feedforward_sums[2],
    )


AXES = ("dp", "fsdp")
DEVICES = 32
GROUPS = 4
MEMBERS = 8
CORE, ZL, Y = 8, 2, 1
X, ZH = 16, 4
BF16 = jnp.bfloat16
F32 = jnp.float32
SMEM = pl.BlockSpec(memory_space=pltpu.SMEM)
VMEM = pl.BlockSpec(memory_space=pltpu.VMEM)
HBM = pl.BlockSpec(memory_space=pltpu.HBM)


def swap(array, bits):
    return lax.ppermute(array, AXES, [(i, i ^ bits) for i in range(DEVICES)])


def member_bits(k):
    return (k >> 2) * CORE + ((k >> 1) & 1) * ZL + (k & 1) * Y


def regroup_pairs():
    def target(i):
        x, core, zh, low = i >> 4, (i >> 3) & 1, (i >> 2) & 1, i & 3
        return (x << 4) | (zh << 3) | (core << 2) | low

    return [(i, target(i)) for i in range(DEVICES)]


def regroup(array):
    return lax.ppermute(array, AXES, regroup_pairs())


def output_pairs(a, b):
    def target(i):
        x, core, zh, zl, y = i >> 4, (i >> 3) & 1, (i >> 2) & 1, (i >> 1) & 1, i & 1
        return ((y ^ a) << 4) | (core << 3) | ((zh ^ b) << 2) | (zl << 1) | x

    return [(i, target(i)) for i in range(DEVICES)]


def gather_members(own):
    near = [own, swap(own, Y), swap(own, ZL), swap(own, ZL | Y)]
    far = [swap(part, CORE) for part in near]
    return jnp.concatenate(near + far, axis=0)


def scatter_members(left, right):
    half = left.shape[0] // 2
    rows = half // 4
    far = jnp.dot(left[half:], right, preferred_element_type=F32).astype(BF16)
    far = swap(far, CORE)
    near = jnp.dot(left[:half], right, preferred_element_type=F32).astype(BF16)
    total = [
        near[i * rows : (i + 1) * rows].astype(F32) + far[i * rows : (i + 1) * rows].astype(F32)
        for i in range(4)
    ]
    sent = [swap(total[i].astype(BF16), member_bits(i)) for i in (3, 1, 2)]
    return total[0] + sent[0].astype(F32) + sent[1].astype(F32) + sent[2].astype(F32)


def hidden_columns(member, width):
    core, zl, y = (member >> 2) & 1, (member >> 1) & 1, member & 1
    return [
        ((gx * X + core * CORE + gz * ZH + zl * ZL + y) * width, width)
        for gx in range(2)
        for gz in range(2)
    ]


def head_columns(member, width):
    core, zl, y = (member >> 2) & 1, (member >> 1) & 1, member & 1
    return [
        (part * width + ((y * 2 + core) * 4 + half * 2 + zl) * HEAD, HEAD)
        for part in range(3)
        for half in range(2)
    ]


def deal_columns(member, own, columns):
    rows = own.shape[0]
    width = own.shape[1] // MEMBERS

    def kernel(member_ref, own_ref, *slabs):
        for k in range(MEMBERS):
            start = 0
            for place, size in columns(member_ref[0] ^ k):
                slabs[k][:, start : start + size] = own_ref[:, pl.ds(pl.multiple_of(place, 128), size)]
                start += size

    return pl.pallas_call(
        kernel,
        out_shape=[jax.ShapeDtypeStruct((rows, width), own.dtype)] * MEMBERS,
        in_specs=[SMEM, VMEM],
        out_specs=[VMEM] * MEMBERS,
    )(member, own)


def place_rows(places, pieces, blocks):
    rows = pieces[0].shape[0] // blocks
    width = pieces[0].shape[1]
    total = len(pieces) * blocks

    def kernel(places_ref, *rest):
        piece_refs, whole_ref, sems = rest[: len(pieces)], rest[len(pieces)], rest[len(pieces) + 1]
        copies = [
            pltpu.make_async_copy(
                piece_refs[i // blocks].at[pl.ds(i % blocks * rows, rows)],
                whole_ref.at[pl.ds(pl.multiple_of(places_ref[i] * rows, rows), rows)],
                sems.at[i],
            )
            for i in range(total)
        ]
        for copy in copies:
            copy.start()
        for copy in copies:
            copy.wait()

    return pl.pallas_call(
        kernel,
        out_shape=jax.ShapeDtypeStruct((total * rows, width), pieces[0].dtype),
        in_specs=[SMEM] + [HBM] * len(pieces),
        out_specs=VMEM,
        scratch_shapes=[pltpu.SemaphoreType.DMA((total,))],
        compiler_params=pltpu.CompilerParams(vmem_limit_bytes=16 << 20),
    )(places, *pieces)


def gather_columns(member, own, columns, places):
    slabs = deal_columns(member, own, columns)
    parts = [slabs[0]] + [swap(slabs[k], member_bits(k)) for k in range(1, MEMBERS)]
    group = jnp.concatenate(parts, axis=0)
    other = swap(group, ZH)
    return place_rows(places, [group, other, swap(group, X), swap(other, X)], MEMBERS)


def gather_gains(device, own):
    whole = own[None]
    for bits in (Y, ZL, CORE, ZH, X):
        other = swap(whole, bits)
        whole = jnp.where((device & bits) == 0, jnp.concatenate([whole, other]), jnp.concatenate([other, whole]))
    order = whole.reshape(2, 2, 2, 2, 2, 2, -1)
    return order.transpose(5, 0, 2, 1, 3, 4, 6).reshape(2, -1).astype(F32)


def deal_sums(member, kept, came):
    rows = kept.shape[0] // MEMBERS
    width = kept.shape[1]

    def kernel(member_ref, kept_ref, came_ref, *slabs):
        for k in range(MEMBERS):
            block = pl.ds(pl.multiple_of((member_ref[0] ^ k) * rows, rows), rows)
            slabs[k][...] = (kept_ref[block, :].astype(F32) + came_ref[block, :].astype(F32)).astype(BF16)

    return pl.pallas_call(
        kernel,
        out_shape=[jax.ShapeDtypeStruct((rows, width), BF16)] * MEMBERS,
        in_specs=[SMEM, VMEM, VMEM],
        out_specs=[VMEM] * MEMBERS,
        compiler_params=pltpu.CompilerParams(vmem_limit_bytes=32 << 20),
    )(member, kept, came)


def place_columns(member, parts, columns):
    rows, width = parts[0].shape

    def kernel(member_ref, *rest):
        part_refs, whole_ref = rest[:MEMBERS], rest[MEMBERS]
        for k in range(MEMBERS):
            start = 0
            for place, size in columns(member_ref[0] ^ k):
                whole_ref[:, pl.ds(pl.multiple_of(place, 128), size)] = part_refs[k][
                    :, start : start + size
                ].astype(F32)
                start += size

    return pl.pallas_call(
        kernel,
        out_shape=jax.ShapeDtypeStruct((rows, width * MEMBERS), F32),
        in_specs=[SMEM] + [VMEM] * MEMBERS,
        out_specs=VMEM,
        compiler_params=pltpu.CompilerParams(vmem_limit_bytes=32 << 20),
    )(member, *parts)


def scatter_columns(member, x, zh, grad, columns):
    width = grad.shape[1]
    quarter = grad.shape[0] // 8
    blocks = grad.reshape(2, 2, 2, quarter, width)
    came = swap(lax.dynamic_index_in_dim(blocks, 1 - x, 0, False), X)

    def half_sum(which):
        mine = lax.dynamic_slice(blocks, (x, 0, which, 0, 0), (1, 2, 1, quarter, width))
        theirs = lax.dynamic_slice(came, (0, which, 0, 0), (2, 1, quarter, width))
        total = mine.reshape(2 * quarter, width).astype(F32) + theirs.reshape(2 * quarter, width).astype(F32)
        return total.astype(BF16)

    far = swap(half_sum(1 - zh), ZH)
    slabs = deal_sums(member, half_sum(zh), far)
    parts = [slabs[0]] + [swap(slabs[k], member_bits(k)) for k in range(1, MEMBERS)]
    return place_columns(member, parts, columns)


def scatter_rows(x, zh, grad):
    rows, width = grad.shape[0] // 4, grad.shape[1]
    blocks = grad.reshape(2, 2, rows, width)
    came = swap(lax.dynamic_index_in_dim(blocks, 1 - x, 0, False), X)

    def half_sum(which):
        mine = lax.dynamic_slice(blocks, (x, which, 0, 0), (1, 1, rows, width)).reshape(rows, width)
        theirs = lax.dynamic_index_in_dim(came, which, 0, False)
        return mine.astype(F32) + theirs.astype(F32)

    return half_sum(zh) + swap(half_sum(1 - zh).astype(BF16), ZH).astype(F32)


def turn(vectors, cosine, sine):
    return vectors * cosine + pltpu.roll(vectors, HEAD // 2, 1) * sine


def key_place_row(member, rows):
    lane = lax.broadcasted_iota(jnp.int32, (1, rows), 1)
    return jnp.concatenate([lane + (member ^ k) * rows for k in range(MEMBERS)], axis=1)


def block_mask(layout_ref, block, block_rows, rows, key_place):
    member, first_end, second_end = layout_ref[0], layout_ref[1], layout_ref[2]
    per_block = block_rows // rows
    row = lax.broadcasted_iota(jnp.int32, (rows, 1), 0)
    place = jnp.concatenate(
        [row + (member ^ (block * per_block + i)) * rows for i in range(per_block)], axis=0
    )
    start = jnp.where(place < first_end, 0, jnp.where(place < second_end, first_end, second_end))
    return (key_place <= place) & (key_place >= start)


def masked_probs(queries, keys, allowed):
    scores = lax.dot_general(queries, keys, (((1,), (1,)), ((), ())), preferred_element_type=F32)
    scores = jnp.where(allowed, scores * HEAD ** (-0.5), MASKED)
    weights = jnp.exp(scores - jnp.max(scores, axis=-1, keepdims=True))
    return weights * (1.0 / jnp.sum(weights, axis=-1, keepdims=True))


BLOCK = 256


def attention_forward(layout, mixed, cosine, sine):
    count = mixed.shape[0]
    width = mixed.shape[1] // 3
    rows = count // MEMBERS

    def kernel(layout_ref, mixed_ref, cos_ref, sin_ref, q_ref, k_ref, v_ref, out_ref):
        key_place = key_place_row(layout_ref[0], rows)
        v_ref[...] = mixed_ref[:, 2 * width :].astype(BF16)
        for head in range(width // HEAD):
            span = slice(head * HEAD, (head + 1) * HEAD)
            key_span = slice(width + head * HEAD, width + (head + 1) * HEAD)
            q_ref[:, span] = turn(mixed_ref[:, span], cos_ref[...], sin_ref[...]).astype(BF16)
            k_ref[:, span] = turn(mixed_ref[:, key_span], cos_ref[...], sin_ref[...]).astype(BF16)

        @pl.loop(0, count // BLOCK)
        def _(block):
            here = pl.ds(pl.multiple_of(block * BLOCK, BLOCK), BLOCK)
            allowed = block_mask(layout_ref, block, BLOCK, rows, key_place)
            for head in range(width // HEAD):
                span = slice(head * HEAD, (head + 1) * HEAD)
                probs = masked_probs(q_ref[here, span], k_ref[:, span], allowed)
                out_ref[here, span] = jnp.dot(
                    probs.astype(BF16), v_ref[:, span], preferred_element_type=F32
                ).astype(BF16)

    return pl.pallas_call(
        kernel,
        out_shape=[jax.ShapeDtypeStruct((count, width), BF16)] * 4,
        in_specs=[SMEM, VMEM, VMEM, VMEM],
        out_specs=[VMEM] * 4,
        compiler_params=pltpu.CompilerParams(vmem_limit_bytes=48 << 20),
    )(layout, mixed, cosine, sine)


def attention_backward_heads(layout, queries, keys, values, grad_out, cosine, sine):
    count, width = queries.shape
    rows = count // MEMBERS

    def kernel(layout_ref, q_ref, k_ref, v_ref, g_ref, cos_ref, sin_ref, out_ref, gk_ref, gv_ref):
        key_place = key_place_row(layout_ref[0], rows)
        gk_ref[...] = jnp.zeros_like(gk_ref)
        gv_ref[...] = jnp.zeros_like(gv_ref)

        @pl.loop(0, count // BLOCK)
        def _(block):
            here = pl.ds(pl.multiple_of(block * BLOCK, BLOCK), BLOCK)
            allowed = block_mask(layout_ref, block, BLOCK, rows, key_place)
            for head in range(width // HEAD):
                span = slice(head * HEAD, (head + 1) * HEAD)
                q, g = q_ref[here, span], g_ref[here, span]
                probs = masked_probs(q, k_ref[:, span], allowed)
                grad_probs = lax.dot_general(
                    g, v_ref[:, span], (((1,), (1,)), ((), ())), preferred_element_type=F32
                )
                delta = jnp.sum(probs * grad_probs, axis=-1, keepdims=True)
                grad_scores = (probs * (grad_probs - delta)).astype(BF16)
                grad_query = jnp.dot(grad_scores, k_ref[:, span], preferred_element_type=F32)
                out_ref[here, span] = turn(
                    grad_query * HEAD ** (-0.5), cos_ref[here, :], -sin_ref[here, :]
                ).astype(BF16)
                over_rows = (((0,), (0,)), ((), ()))
                gk_ref[:, span] += lax.dot_general(grad_scores, q, over_rows, preferred_element_type=F32)
                gv_ref[:, span] += lax.dot_general(
                    probs.astype(BF16), g, over_rows, preferred_element_type=F32
                )

        out_ref[:, 2 * width :] = gv_ref[...].astype(BF16)
        for head in range(width // HEAD):
            span = slice(head * HEAD, (head + 1) * HEAD)
            out_ref[:, width + head * HEAD : width + (head + 1) * HEAD] = turn(
                gk_ref[:, span] * HEAD ** (-0.5), cos_ref[...], -sin_ref[...]
            ).astype(BF16)

    return pl.pallas_call(
        kernel,
        out_shape=jax.ShapeDtypeStruct((count, 3 * width), BF16),
        in_specs=[SMEM] + [VMEM] * 6,
        out_specs=VMEM,
        scratch_shapes=[pltpu.VMEM((count, width), F32), pltpu.VMEM((count, width), F32)],
        compiler_params=pltpu.CompilerParams(vmem_limit_bytes=48 << 20),
    )(layout, queries, keys, values, grad_out, cosine, sine)


def norm_parts(values):
    centred = values - jnp.mean(values, axis=-1, keepdims=True)
    inverse = lax.rsqrt(jnp.mean(centred * centred, axis=-1, keepdims=True) + EPSILON)
    return centred * inverse, inverse


def norm_backward(values, gain, grad):
    normal, inverse = norm_parts(values)
    scaled = grad * gain
    return inverse * (
        scaled
        - jnp.mean(scaled, axis=-1, keepdims=True)
        - normal * jnp.mean(scaled * normal, axis=-1, keepdims=True)
    )


def contract_rows(left, right):
    return lax.dot_general(left, right, (((0,), (0,)), ((), ())), preferred_element_type=F32)


def dot_transposed(left, right):
    return lax.dot_general(left, right, (((1,), (1,)), ((), ())), preferred_element_type=F32)


def grouped_body(
    tokens,
    triple_weight,
    output_weight,
    up_weight,
    down_weight,
    first_gain,
    second_gain,
    cotangent,
    frame_counts,
    text_counts,
    action_counts,
):
    rows, width = tokens.shape
    count = rows * MEMBERS
    dp, fsdp = lax.axis_index("dp"), lax.axis_index("fsdp")
    x, core = dp >> 1, dp & 1
    zh, low = fsdp >> 2, fsdp & 3
    device = dp * 8 + fsdp
    member = core * 4 + low
    member_array = member.reshape(1)

    hidden_width = up_weight.shape[1] // DEVICES
    source_bits = jnp.array(
        [group ^ member_bits(k) for group in (0, ZH, X, X | ZH) for k in range(MEMBERS)], jnp.int32
    )
    row_places = device ^ source_bits
    group_index = x * 2 + zh
    group_places = group_index ^ jnp.arange(GROUPS, dtype=jnp.int32)
    triple_columns = lambda m: head_columns(m, width)
    up_columns = lambda m: hidden_columns(m, hidden_width)

    tokens = regroup(tokens)
    triple = gather_columns(member_array, triple_weight, triple_columns, row_places)
    all_tokens = gather_members(tokens)
    gains = gather_gains(device, jnp.stack([first_gain, second_gain]))

    output_parts = [lax.ppermute(output_weight, AXES, output_pairs(a, b)) for a in (0, 1) for b in (0, 1)]
    output_places = jnp.stack([(zh ^ b) * 2 + (x ^ a) for a in (0, 1) for b in (0, 1)])
    output = place_rows(output_places, output_parts, 1)

    up = gather_columns(member_array, up_weight, up_columns, row_places)
    down_other = swap(down_weight, ZH)
    down = place_rows(
        group_places, [down_weight, down_other, swap(down_weight, X), swap(down_other, X)], 1
    )
    cotangent = regroup(cotangent)
    all_cotangent = gather_members(cotangent)

    counts = jnp.concatenate(
        [frame_counts.reshape(-1), text_counts.reshape(-1), action_counts.reshape(-1)]
    )
    counts = jnp.where(core == zh, counts, swap(counts, CORE))
    frames = counts[:2]
    slots = text_counts.shape[-1]
    texts = counts[2 : 2 + 2 * slots].reshape(2, slots)
    actions = counts[2 + 2 * slots :].reshape(2, slots)
    live = jnp.arange(slots, dtype=jnp.int32) < frames[:, None]
    lengths = jnp.sum(jnp.where(live, IMG + texts + actions, 0), axis=-1)
    first_end = lengths[0]
    second_end = lengths[0] + lengths[1]
    layout = jnp.stack([member, first_end, second_end]).astype(jnp.int32)
    block_order = member ^ jnp.arange(MEMBERS, dtype=jnp.int32)
    places = (block_order[:, None] * rows + jnp.arange(rows, dtype=jnp.int32)[None, :]).reshape(-1)
    starts = jnp.where(places < first_end, 0, jnp.where(places < second_end, first_end, second_end))
    cosine, sine = rotary_tables(places - starts)
    cosine = jnp.concatenate([cosine[:, 0], cosine[:, 0]], axis=1)
    sine = jnp.concatenate([-sine[:, 0], sine[:, 0]], axis=1)

    normed = norm_rows(all_tokens.astype(F32), gains[0]).astype(BF16)
    mixed = jnp.dot(normed, triple, preferred_element_type=F32)
    queries, keys, values, attended = attention_forward(layout, mixed, cosine, sine)
    inputs = tokens.astype(F32)
    middle = inputs + scatter_members(attended, output)
    normed_two = gather_members(norm_rows(middle, gains[1]).astype(BF16))
    hidden = jnp.dot(normed_two, up, preferred_element_type=F32)
    activation, gelu_pull = jax.vjp(jax.nn.gelu, hidden)
    activation = activation.astype(BF16)
    grad_hidden = gelu_pull(dot_transposed(all_cotangent, down))[0].astype(BF16)

    grad_normed_two = scatter_members(grad_hidden, up.T)
    grad_middle = cotangent.astype(F32) + norm_backward(middle, gains[1], grad_normed_two)
    grad_branch = gather_members(grad_middle.astype(BF16))
    grad_attended = dot_transposed(grad_branch, output).astype(BF16)
    grad_mixed = attention_backward_heads(layout, queries, keys, values, grad_attended, cosine, sine)
    grad_normed = scatter_members(grad_mixed, triple.T)
    token_grad = grad_middle + norm_backward(inputs, gains[0], grad_normed)
    token_grad = regroup(token_grad.astype(BF16))

    layer_output = middle + scatter_members(activation, down)
    layer_output = regroup(layer_output.astype(BF16))

    down_grad = scatter_rows(x, zh, contract_rows(activation, all_cotangent).astype(BF16))
    up_grad = scatter_columns(
        member_array, x, zh, contract_rows(normed_two, grad_hidden).astype(BF16), up_columns
    )
    output_term = contract_rows(attended, grad_branch).astype(BF16).reshape(GROUPS, -1, width)
    output_grad = 0.0
    for a in (0, 1):
        for b in (0, 1):
            piece = lax.dynamic_index_in_dim(output_term, (zh ^ b) * 2 + (x ^ a), 0, False)
            back = [(target, source) for source, target in output_pairs(a, b)]
            output_grad = output_grad + lax.ppermute(piece, AXES, back).astype(F32)
    triple_grad = scatter_columns(
        member_array, x, zh, contract_rows(normed, grad_mixed).astype(BF16), triple_columns
    )
    first_gain_grad = jnp.sum(triple_grad * triple_weight.astype(F32), axis=-1) / first_gain.astype(F32)
    second_gain_grad = jnp.sum(up_grad * up_weight.astype(F32), axis=-1) / second_gain.astype(F32)
    return (
        layer_output,
        token_grad,
        triple_grad,
        output_grad,
        up_grad,
        down_grad,
        first_gain_grad,
        second_gain_grad,
    )


def solution(mesh):
    grouped = mesh.shape["dp"] * 2 == mesh.shape["fsdp"] == MEMBERS
    rows = P(AXES, None)
    return jax.shard_map(
        grouped_body if grouped else whole_rows_body,
        mesh=mesh,
        in_specs=(rows,) * 5 + (P(AXES),) * 2 + (rows, P("dp", None), P("dp", None, None), P("dp", None, None)),
        out_specs=(rows,) * 6 + (P(AXES),) * 2,
        check_vma=False,
    )
```

```python
import math

import jax
import jax.numpy as jnp
from jax import lax
from jax.experimental import pallas as pl
from jax.experimental.pallas import tpu as pltpu
from jax.sharding import PartitionSpec as P

HEADS = 16
HEAD = 128
IMG = 576


EPSILON = 1e-05
MASKED = -1e30


def clip_layout(frame_counts, text_counts, action_counts, pack_length):
    frame_slot = jnp.arange(text_counts.shape[-1], dtype=jnp.int32)
    frame_live = frame_slot < frame_counts[..., None]
    frame_sizes = jnp.where(frame_live, IMG + text_counts + action_counts, 0)
    clip_lengths = jnp.sum(frame_sizes, axis=-1)
    first_end = clip_lengths[..., 0:1]
    second_end = first_end + clip_lengths[..., 1:2]
    places = jnp.arange(pack_length, dtype=jnp.int32)
    segment = (places >= first_end).astype(jnp.int32) + (places >= second_end).astype(jnp.int32)
    starts = jnp.where(segment == 0, 0, jnp.where(segment == 1, first_end, second_end))
    return (segment, places - starts)


def rotary_tables(position):
    half_width = HEAD // 2
    frequency = jnp.exp(
        jnp.arange(half_width, dtype=jnp.float32) * (-2.0 * math.log(10000.0) / HEAD)
    )
    angles = position.astype(jnp.float32)[:, None] * frequency[None, :]
    return (jnp.cos(angles)[:, None, :], jnp.sin(angles)[:, None, :])


def rotate(vectors, cosine, sine_table):
    half_width = vectors.shape[-1] // 2
    former = vectors[..., :half_width]
    latter = vectors[..., half_width:]
    return jnp.concatenate(
        [former * cosine - latter * sine_table, latter * cosine + former * sine_table], axis=-1
    )


def unrotate(gradient, cosine, sine_table):
    half_width = gradient.shape[-1] // 2
    former = gradient[..., :half_width]
    latter = gradient[..., half_width:]
    return jnp.concatenate(
        [former * cosine + latter * sine_table, latter * cosine - former * sine_table], axis=-1
    )


def norm_rows(values, gain_vector):
    centred = values - jnp.mean(values, axis=-1, keepdims=True)
    variance = jnp.mean(centred * centred, axis=-1, keepdims=True)
    return centred * lax.rsqrt(variance + EPSILON) * gain_vector


def block_allowed(query_segment, query_places, key_segment, key_place):
    return (query_segment[:, None] == key_segment[None, :]) & (
        key_place[None, :] <= query_places[:, None]
    )


def block_scores(queries, key_block, allowed):
    scores = jnp.einsum(
        "qhd,khd->hqk", queries, key_block, preferred_element_type=jnp.float32
    ) * HEAD ** (-0.5)
    return jnp.where(allowed[None], scores, MASKED)


def block_probs(queries, key_block, allowed, row_max, row_sum):
    scores = block_scores(queries, key_block, allowed)
    return jnp.where(allowed[None], jnp.exp(scores - row_max[..., None]) / row_sum[..., None], 0.0)


def softmax_stats(queries, key_blocks, layout_parts):
    query_segment, query_places, key_segments, key_places = layout_parts
    row_count, head_count = (queries.shape[0], queries.shape[1])
    start_state = (
        jnp.full((head_count, row_count), MASKED, jnp.float32),
        jnp.zeros((head_count, row_count), jnp.float32),
    )

    def advance(state, block_inputs):
        key_block, key_segment, key_place = block_inputs
        allowed = block_allowed(query_segment, query_places, key_segment, key_place)

        def update(current):
            row_max, row_sum = current
            scores = block_scores(queries, key_block, allowed)
            new_max = jnp.maximum(row_max, jnp.max(scores, axis=-1))
            weights = jnp.where(allowed[None], jnp.exp(scores - new_max[..., None]), 0.0)
            return (new_max, row_sum * jnp.exp(row_max - new_max) + jnp.sum(weights, axis=-1))

        return (lax.cond(jnp.any(allowed), update, lambda current: current, state), None)

    final_state, unused = lax.scan(advance, start_state, (key_blocks, key_segments, key_places))
    return final_state


def attention_output(queries, key_blocks, value_blocks, layout_parts, row_max, row_sum):
    query_segment, query_places, key_segments, key_places = layout_parts

    def advance(accum, block_inputs):
        key_block, value_block, key_segment, key_place = block_inputs
        allowed = block_allowed(query_segment, query_places, key_segment, key_place)

        def update(current):
            probs = block_probs(queries, key_block, allowed, row_max, row_sum).astype(jnp.bfloat16)
            return current + jnp.einsum(
                "hqk,khd->qhd", probs, value_block, preferred_element_type=jnp.float32
            )

        return (lax.cond(jnp.any(allowed), update, lambda current: current, accum), None)

    attended, unused = lax.scan(
        advance,
        jnp.zeros(queries.shape, jnp.float32),
        (key_blocks, value_blocks, key_segments, key_places),
    )
    return attended


def attention_backward(
    queries, grad_attended, delta_rows, key_blocks, value_blocks, layout_parts, row_max, row_sum
):
    query_segment, query_places, key_segments, key_places = layout_parts
    score_scale = HEAD ** (-0.5)

    def advance(grad_query, block_inputs):
        key_block, value_block, key_segment, key_place = block_inputs
        allowed = block_allowed(query_segment, query_places, key_segment, key_place)

        def update(current):
            probs = block_probs(queries, key_block, allowed, row_max, row_sum)
            grad_probs = jnp.einsum(
                "qhd,khd->hqk", grad_attended, value_block, preferred_element_type=jnp.float32
            )
            grad_scores = (probs * (grad_probs - delta_rows[..., None])).astype(jnp.bfloat16)
            new_query = (
                current
                + jnp.einsum(
                    "hqk,khd->qhd", grad_scores, key_block, preferred_element_type=jnp.float32
                )
                * score_scale
            )
            return (new_query, ())

        def bypass(current):
            return (current, ())

        return lax.cond(jnp.any(allowed), update, bypass, grad_query)

    grad_query, terms = lax.scan(
        advance,
        jnp.zeros(queries.shape, jnp.float32),
        (key_blocks, value_blocks, key_segments, key_places),
    )
    return (grad_query, None, None)


def project_front(inputs, triple_full, gain_full, cosine, sine_table):
    row_count, width = inputs.shape
    normed = norm_rows(inputs, gain_full.astype(jnp.float32)).astype(jnp.bfloat16)
    mixed = jnp.dot(normed, triple_full, preferred_element_type=jnp.float32)
    queries = rotate(mixed[:, :width].reshape(row_count, HEADS, HEAD), cosine, sine_table).astype(
        jnp.bfloat16
    )
    keys_local = (
        rotate(mixed[:, width : 2 * width].reshape(row_count, HEADS, HEAD), cosine, sine_table)
        .astype(jnp.bfloat16)
        .reshape(row_count, width)
    )
    values_local = mixed[:, 2 * width :].astype(jnp.bfloat16)
    return (normed, queries, keys_local, values_local)


def run_attention(queries, gathered, layout_parts):
    block_count = layout_parts[2].shape[0]
    key_blocks = gathered[0].reshape(block_count, -1, HEADS, HEAD)
    value_blocks = gathered[1].reshape(block_count, -1, HEADS, HEAD)
    row_max, row_sum = softmax_stats(queries, key_blocks, layout_parts)
    attended = attention_output(queries, key_blocks, value_blocks, layout_parts, row_max, row_sum)
    return (attended, key_blocks, value_blocks, row_max, row_sum)


def finish_layer(inputs, attended, output_full, up_full, down_full, second_full):
    row_count, width = inputs.shape
    attended_low = attended.reshape(row_count, width).astype(jnp.bfloat16)
    middle = inputs + jnp.dot(attended_low, output_full, preferred_element_type=jnp.float32)
    normed_two = norm_rows(middle, second_full.astype(jnp.float32)).astype(jnp.bfloat16)
    hidden = jnp.dot(normed_two, up_full, preferred_element_type=jnp.float32)
    activation = jax.nn.gelu(hidden).astype(jnp.bfloat16)
    result = middle + jnp.dot(activation, down_full, preferred_element_type=jnp.float32)
    return (result, attended_low, middle, normed_two, hidden, activation)


def whole_rows_body(
    tokens,
    triple_weight,
    output_weight,
    up_weight,
    down_weight,
    first_gain,
    second_gain,
    cotangent,
    frame_counts,
    text_counts,
    action_counts,
):
    row_count, width = tokens.shape
    pack_length = row_count * lax.axis_size("fsdp")
    first_place = lax.axis_index("fsdp") * row_count
    segment, position = clip_layout(frame_counts[0], text_counts[0], action_counts[0], pack_length)
    block_rows = min(1024, pack_length)
    block_count = pack_length // block_rows
    query_places = first_place + jnp.arange(row_count, dtype=jnp.int32)
    own_segment = lax.dynamic_slice_in_dim(segment, first_place, row_count, 0)
    layout_parts = (
        own_segment,
        query_places,
        segment.reshape(block_count, block_rows),
        jnp.arange(pack_length, dtype=jnp.int32).reshape(block_count, block_rows),
    )
    cosine, sine_table = rotary_tables(
        lax.dynamic_slice_in_dim(position, first_place, row_count, 0)
    )
    inputs = tokens.astype(jnp.float32)
    attention_set = (
        lax.all_gather(triple_weight, ("dp", "fsdp"), axis=0, tiled=True),
        lax.all_gather(output_weight, ("dp", "fsdp"), axis=0, tiled=True),
        lax.all_gather(first_gain, ("dp", "fsdp"), axis=0, tiled=True),
    )
    normed, queries, keys_local, values_local = project_front(
        inputs, attention_set[0], attention_set[2], cosine, sine_table
    )
    gathered = (
        lax.all_gather(keys_local, "fsdp", axis=0, tiled=True),
        lax.all_gather(values_local, "fsdp", axis=0, tiled=True),
    )
    attended, key_blocks, value_blocks, row_max, row_sum = run_attention(
        queries, gathered, layout_parts
    )
    feedforward_set = (
        lax.all_gather(up_weight, ("dp", "fsdp"), axis=0, tiled=True),
        lax.all_gather(down_weight, ("dp", "fsdp"), axis=0, tiled=True),
        lax.all_gather(second_gain, ("dp", "fsdp"), axis=0, tiled=True),
    )
    kept_parts = finish_layer(
        inputs,
        attended,
        attention_set[1],
        feedforward_set[0],
        feedforward_set[1],
        feedforward_set[2],
    )
    layer_output = kept_parts[0].astype(jnp.bfloat16)
    attention_set = (
        lax.all_gather(triple_weight, ("dp", "fsdp"), axis=0, tiled=True),
        lax.all_gather(output_weight, ("dp", "fsdp"), axis=0, tiled=True),
        lax.all_gather(first_gain, ("dp", "fsdp"), axis=0, tiled=True),
    )
    normed, queries, keys_local, values_local = project_front(
        inputs, attention_set[0], attention_set[2], cosine, sine_table
    )
    gathered = (
        lax.all_gather(keys_local, "fsdp", axis=0, tiled=True),
        lax.all_gather(values_local, "fsdp", axis=0, tiled=True),
    )
    attended, key_blocks, value_blocks, row_max, row_sum = run_attention(
        queries, gathered, layout_parts
    )
    feedforward_set = (
        lax.all_gather(up_weight, ("dp", "fsdp"), axis=0, tiled=True),
        lax.all_gather(down_weight, ("dp", "fsdp"), axis=0, tiled=True),
        lax.all_gather(second_gain, ("dp", "fsdp"), axis=0, tiled=True),
    )
    kept_parts = finish_layer(
        inputs,
        attended,
        attention_set[1],
        feedforward_set[0],
        feedforward_set[1],
        feedforward_set[2],
    )
    unused_result, attended_low, middle, normed_two, hidden, activation = kept_parts
    down_term = jnp.einsum("rf,rd->fd", activation, cotangent, preferred_element_type=jnp.float32)
    grad_activation = jnp.einsum(
        "rd,fd->rf", cotangent, feedforward_set[1], preferred_element_type=jnp.float32
    )
    unused_gelu, gelu_pull = jax.vjp(jax.nn.gelu, hidden)
    grad_hidden = gelu_pull(grad_activation)[0].astype(jnp.bfloat16)
    up_term = jnp.einsum("rd,rf->df", normed_two, grad_hidden, preferred_element_type=jnp.float32)
    grad_normed_two = jnp.einsum(
        "rf,df->rd", grad_hidden, feedforward_set[0], preferred_element_type=jnp.float32
    )
    unused_second, second_pull = jax.vjp(norm_rows, middle, feedforward_set[2].astype(jnp.float32))
    grad_middle_norm, second_gain_term = second_pull(grad_normed_two)
    grad_middle = cotangent.astype(jnp.float32) + grad_middle_norm
    feedforward_sums = (
        lax.psum_scatter(up_term, ("dp", "fsdp"), scatter_dimension=0, tiled=True),
        lax.psum_scatter(down_term, ("dp", "fsdp"), scatter_dimension=0, tiled=True),
        lax.psum_scatter(second_gain_term, ("dp", "fsdp"), scatter_dimension=0, tiled=True),
    )
    grad_branch = grad_middle.astype(jnp.bfloat16)
    output_term = jnp.einsum(
        "rd,re->de", attended_low, grad_branch, preferred_element_type=jnp.float32
    )
    grad_attended = (
        jnp.einsum("re,de->rd", grad_branch, attention_set[1], preferred_element_type=jnp.float32)
        .astype(jnp.bfloat16)
        .reshape(row_count, HEADS, HEAD)
    )
    delta_rows = jnp.sum(grad_attended.astype(jnp.float32) * attended, axis=-1).T
    score_scale = HEAD ** (-0.5)
    grad_query = attention_backward(
        queries, grad_attended, delta_rows, key_blocks, value_blocks, layout_parts, row_max, row_sum
    )[0]
    pack_stats = (
        lax.all_gather(row_max.T, "fsdp", axis=0, tiled=True),
        lax.all_gather(row_sum.T, "fsdp", axis=0, tiled=True),
        lax.all_gather(delta_rows.T, "fsdp", axis=0, tiled=True),
    )
    own_keys = keys_local.reshape(row_count, HEADS, HEAD)
    own_values = values_local.reshape(row_count, HEADS, HEAD)
    empty_grads = jnp.zeros((row_count, HEADS, HEAD), jnp.float32)
    query_piece = lax.all_gather(queries, "fsdp", axis=0, tiled=True)
    grad_piece = lax.all_gather(grad_attended, "fsdp", axis=0, tiled=True)
    piece_rows = query_piece.shape[0]
    block_size = min(1024, piece_rows)
    block_total = piece_rows // block_size

    def advance(current, block_index):
        offset = block_index * block_size
        query_part = lax.dynamic_slice_in_dim(query_piece, offset, block_size, 0)
        grad_part = lax.dynamic_slice_in_dim(grad_piece, offset, block_size, 0)
        max_part = lax.dynamic_slice_in_dim(pack_stats[0], offset, block_size, 0).T
        sum_part = lax.dynamic_slice_in_dim(pack_stats[1], offset, block_size, 0).T
        delta_part = lax.dynamic_slice_in_dim(pack_stats[2], offset, block_size, 0).T
        part_segment = lax.dynamic_slice_in_dim(segment, offset, block_size, 0)
        part_places = offset + jnp.arange(block_size, dtype=jnp.int32)
        allowed = block_allowed(part_segment, part_places, own_segment, query_places)

        def update(pair):
            probs = block_probs(query_part, own_keys, allowed, max_part, sum_part)
            grad_probs = jnp.einsum(
                "qhd,khd->hqk", grad_part, own_values, preferred_element_type=jnp.float32
            )
            grad_scores = (probs * (grad_probs - delta_part[..., None])).astype(jnp.bfloat16)
            grad_key = (
                pair[0]
                + jnp.einsum(
                    "hqk,qhd->khd", grad_scores, query_part, preferred_element_type=jnp.float32
                )
                * score_scale
            )
            grad_value = pair[1] + jnp.einsum(
                "hqk,qhd->khd",
                probs.astype(jnp.bfloat16),
                grad_part,
                preferred_element_type=jnp.float32,
            )
            return (grad_key, grad_value)

        return (lax.cond(jnp.any(allowed), update, lambda pair: pair, current), None)

    result, unused = lax.scan(
        advance, (empty_grads, empty_grads), jnp.arange(block_total, dtype=jnp.int32)
    )
    key_grad_sum = result[0].reshape(row_count, width)
    value_grad_sum = result[1].reshape(row_count, width)
    grad_query_full = (
        unrotate(grad_query, cosine, sine_table).reshape(row_count, width).astype(jnp.bfloat16)
    )
    grad_key_full = (
        unrotate(key_grad_sum.reshape(row_count, HEADS, HEAD), cosine, sine_table)
        .reshape(row_count, width)
        .astype(jnp.bfloat16)
    )
    grad_value_full = value_grad_sum.astype(jnp.bfloat16)
    grad_mixed = jnp.concatenate([grad_query_full, grad_key_full, grad_value_full], axis=1)
    triple_term = jnp.einsum("rd,re->de", normed, grad_mixed, preferred_element_type=jnp.float32)
    grad_normed = jnp.einsum(
        "re,de->rd", grad_mixed, attention_set[0], preferred_element_type=jnp.float32
    )
    unused_first, first_pull = jax.vjp(norm_rows, inputs, attention_set[2].astype(jnp.float32))
    grad_input_norm, first_gain_term = first_pull(grad_normed)
    token_grad = (grad_middle + grad_input_norm).astype(jnp.bfloat16)
    attention_sums = (
        lax.psum_scatter(triple_term, ("dp", "fsdp"), scatter_dimension=0, tiled=True),
        lax.psum_scatter(output_term, ("dp", "fsdp"), scatter_dimension=0, tiled=True),
        lax.psum_scatter(first_gain_term, ("dp", "fsdp"), scatter_dimension=0, tiled=True),
    )
    return (
        layer_output,
        token_grad,
        attention_sums[0],
        attention_sums[1],
        feedforward_sums[0],
        feedforward_sums[1],
        attention_sums[2],
        feedforward_sums[2],
    )


AXES = ("dp", "fsdp")
DEVICES = 32
MEMBERS = 8
CORE, ZL, Y = 8, 2, 1
X, ZH = 16, 4
BF16 = jnp.bfloat16
F32 = jnp.float32
SMEM = pl.BlockSpec(memory_space=pltpu.SMEM)
VMEM = pl.BlockSpec(memory_space=pltpu.VMEM)
HBM = pl.BlockSpec(memory_space=pltpu.HBM)


def swap(array, bits):
    return lax.ppermute(array, AXES, [(i, i ^ bits) for i in range(DEVICES)])


def alike(*bits):
    groups = {}
    for i in range(DEVICES):
        groups.setdefault(i & ~sum(bits), []).append(i)
    return list(groups.values())


def exchange(array, *bits):
    return lax.all_to_all(array, AXES, 0, 0, tiled=True, axis_index_groups=alike(*bits))


def after(array, *others):
    return lax.optimization_barrier((array,) + others)[0]


def together(*arrays):
    return lax.optimization_barrier(arrays)


def regroup_pairs():
    def target(i):
        x, core, zh, low = i >> 4, (i >> 3) & 1, (i >> 2) & 1, i & 3
        return (x << 4) | (zh << 3) | (core << 2) | low

    return [(i, target(i)) for i in range(DEVICES)]


def regroup(array):
    return lax.ppermute(array, AXES, regroup_pairs())


def turn_pairs():
    return [(i, (i & 14) | (i & 1) << 4 | i >> 4) for i in range(DEVICES)]


def gather(own, *bits):
    return lax.all_gather(own, AXES, axis=0, tiled=True, axis_index_groups=alike(*bits))


def collect(parts):
    return exchange(parts.reshape(4, -1, parts.shape[1]), ZL, Y)


def row_product(half, left, right, transposed, came=None):
    count, depth = left.shape[0] // 2, left.shape[1]
    width = right.shape[0] if transposed else right.shape[1]
    tile = 512

    def kernel(half_ref, left_ref, right_ref, *rest):
        if transposed:
            total = dot_transposed(left_ref[...], right_ref[...])
        else:
            total = jnp.dot(left_ref[...], right_ref[...], preferred_element_type=F32)
        if came is not None:
            total = total + rest[0][...].astype(F32)
        rest[-1][...] = total.astype(BF16)

    columns = pl.BlockSpec((count, tile), lambda i, half_ref: (0, i))
    if transposed:
        right_spec = pl.BlockSpec((tile, depth), lambda i, half_ref: (i, 0))
    else:
        right_spec = pl.BlockSpec((depth, tile), lambda i, half_ref: (0, i))
    more = [] if came is None else [came]
    return pl.pallas_call(
        kernel,
        grid_spec=pltpu.PrefetchScalarGridSpec(
            num_scalar_prefetch=1,
            grid=(width // tile,),
            in_specs=[pl.BlockSpec((count, depth), lambda i, half_ref: (half_ref[0], 0)), right_spec]
            + [columns] * len(more),
            out_specs=columns,
        ),
        out_shape=jax.ShapeDtypeStruct((count, width), BF16),
        compiler_params=pltpu.CompilerParams(vmem_limit_bytes=32 << 20),
    )(half, left, right, *more)


def product_sums(core, rows, right, transposed=False):
    near, far = core.reshape(1), (1 - core).reshape(1)
    came = swap(row_product(far, rows, right, transposed), CORE)
    return row_product(near, rows, right, transposed, came)


def hidden_columns(member, width):
    core, zl, y = (member >> 2) & 1, (member >> 1) & 1, member & 1
    return [
        ((gx * X + core * CORE + gz * ZH + zl * ZL + y) * width, width)
        for gx in range(2)
        for gz in range(2)
    ]


def head_columns(member, width):
    core, zl, y = (member >> 2) & 1, (member >> 1) & 1, member & 1
    return [
        (part * width + ((y * 2 + core) * 4 + half * 2 + zl) * HEAD, HEAD)
        for part in range(3)
        for half in range(2)
    ]


def deal_columns(own, columns, extra=None):
    rows = own.shape[0]
    width = own.shape[1] // MEMBERS
    more = 0 if extra is None else 16

    def kernel(*refs):
        own_ref, slabs_ref = refs[0], refs[-1]
        for member in range(MEMBERS):
            start = 0
            for place, size in columns(member):
                slabs_ref[member, :rows, start : start + size] = own_ref[:, place : place + size]
                start += size
            if more:
                slabs_ref[member, rows:, :] = jnp.zeros((more, width), own.dtype)
                slabs_ref[member, rows:, : extra.shape[1]] = jnp.broadcast_to(refs[1][...], (more, extra.shape[1]))

    arrays = [own] if extra is None else [own, extra]
    return pl.pallas_call(
        kernel,
        out_shape=jax.ShapeDtypeStruct((MEMBERS, rows + more, width), own.dtype),
        in_specs=[VMEM] * len(arrays),
        out_specs=VMEM,
    )(*arrays)


def pair_up(index, mine, theirs):
    return jnp.where(index == 0, jnp.stack([mine, theirs]), jnp.stack([theirs, mine]))


def row_copies(places_ref, pieces, whole_ref, sems, rows):
    sources = [(piece, start) for piece in pieces for start in range(0, piece.shape[0], rows)]
    return [
        pltpu.make_async_copy(
            piece.at[pl.ds(start, rows)],
            whole_ref.at[pl.ds(pl.multiple_of(places_ref[n] * rows, rows), rows)],
            sems.at[n],
        )
        for n, (piece, start) in enumerate(sources)
    ]


def place_rows(places, pieces, rows):
    count = sum(piece.shape[0] for piece in pieces)

    def kernel(places_ref, *rest):
        whole_ref, sems = rest[-2:]
        copies = row_copies(places_ref, rest[:-2], whole_ref, sems, rows)
        for copy in copies:
            copy.start()
        for copy in copies:
            copy.wait()

    return pl.pallas_call(
        kernel,
        out_shape=jax.ShapeDtypeStruct((count, pieces[0].shape[1]), BF16),
        in_specs=[SMEM] + [HBM] * len(pieces),
        out_specs=VMEM,
        scratch_shapes=[pltpu.SemaphoreType.DMA((count // rows,))],
        compiler_params=pltpu.CompilerParams(vmem_limit_bytes=16 << 20),
    )(places, *pieces)


def place_columns(slabs, own, gain, columns):
    rows = own.shape[0]

    def kernel(slabs_ref, own_ref, gain_ref, whole_ref, sum_ref):
        total = jnp.zeros((rows, HEAD), F32)
        for member in range(MEMBERS):
            start = 0
            for place, size in columns(member):
                part = slabs_ref[member, :, start : start + size].astype(F32)
                whole_ref[:, place : place + size] = part
                product = part * own_ref[:, place : place + size].astype(F32)
                for lane in range(0, size, HEAD):
                    total = total + product[:, lane : lane + HEAD]
                start += size
        sum_ref[...] = jnp.sum(total, axis=1, keepdims=True) / gain_ref[...]

    return pl.pallas_call(
        kernel,
        out_shape=[jax.ShapeDtypeStruct(own.shape, F32), jax.ShapeDtypeStruct((rows, 1), F32)],
        in_specs=[VMEM] * 3,
        out_specs=[VMEM] * 2,
        compiler_params=pltpu.CompilerParams(vmem_limit_bytes=32 << 20),
    )(slabs, own, gain)


def give(index, bits, grad):
    return swap(lax.dynamic_index_in_dim(grad, 1 - index, 0, False), bits)


def half_sum(first, second, grad, came):
    outer, inner, width = grad.shape[1], grad.shape[3], grad.shape[4]
    mine = lax.dynamic_slice(grad, (first, 0, second, 0, 0), (1, outer, 1, inner, width))
    theirs = lax.dynamic_slice(came, (0, second, 0, 0), (outer, 1, inner, width))
    shape = (outer, inner, width)
    return mine.reshape(shape).astype(F32) + theirs.reshape(shape).astype(F32)


def give_sum(first, second, bits, grad, came):
    return swap(half_sum(first, 1 - second, grad, came).astype(BF16), bits)


def keep_sum(first, second, grad, came, far):
    return half_sum(first, second, grad, came) + far.astype(F32)


def turn(vectors, cosine, sine):
    return vectors * cosine + pltpu.roll(vectors, HEAD // 2, 1) * sine


def block_mask(ends_ref, block, block_rows, count):
    first_end, second_end = ends_ref[0], ends_ref[1]
    place = lax.broadcasted_iota(jnp.int32, (block_rows, 1), 0) + block * block_rows
    key_place = lax.broadcasted_iota(jnp.int32, (1, count), 1)
    start = jnp.where(place < first_end, 0, jnp.where(place < second_end, first_end, second_end))
    return (key_place <= place) & (key_place >= start)


def masked_probs(queries, keys, allowed):
    scores = lax.dot_general(queries, keys, (((1,), (1,)), ((), ())), preferred_element_type=F32)
    scores = jnp.where(allowed, scores * HEAD ** (-0.5), MASKED)
    weights = jnp.exp(scores - jnp.max(scores, axis=-1, keepdims=True))
    return weights * (1.0 / jnp.sum(weights, axis=-1, keepdims=True))


BLOCK = 256


def attention_forward(ends, places, normal, pieces, cosine, sine):
    count, depth = normal.shape
    width = pieces[0].shape[1] // 3
    block_rows = depth // 8

    def kernel(ends_ref, places_ref, normal_ref, cos_ref, sin_ref, *rest):
        piece_refs, (q_ref, k_ref, v_ref, out_ref, weight_ref, sems) = rest[: len(pieces)], rest[len(pieces) :]
        copies = row_copies(places_ref, piece_refs, weight_ref, sems, block_rows)
        for copy in copies:
            copy.start()
        for copy in copies:
            copy.wait()

        @pl.loop(0, count // BLOCK)
        def _(block):
            here = pl.ds(pl.multiple_of(block * BLOCK, BLOCK), BLOCK)
            mixed = jnp.dot(normal_ref[here, :], weight_ref[...], preferred_element_type=F32)
            cos, sin = cos_ref[here, :], sin_ref[here, :]
            v_ref[here, :] = mixed[:, 2 * width :].astype(BF16)
            for head in range(width // HEAD):
                span = slice(head * HEAD, (head + 1) * HEAD)
                key_span = slice(width + head * HEAD, width + (head + 1) * HEAD)
                q_ref[here, span] = turn(mixed[:, span], cos, sin).astype(BF16)
                k_ref[here, span] = turn(mixed[:, key_span], cos, sin).astype(BF16)

        @pl.loop(0, count // BLOCK)
        def _(block):
            here = pl.ds(pl.multiple_of(block * BLOCK, BLOCK), BLOCK)
            allowed = block_mask(ends_ref, block, BLOCK, count)
            for head in range(width // HEAD):
                span = slice(head * HEAD, (head + 1) * HEAD)
                probs = masked_probs(q_ref[here, span], k_ref[:, span], allowed)
                out_ref[here, span] = jnp.dot(
                    probs.astype(BF16), v_ref[:, span], preferred_element_type=F32
                ).astype(BF16)

    return pl.pallas_call(
        kernel,
        out_shape=[jax.ShapeDtypeStruct((count, width), BF16)] * 4
        + [jax.ShapeDtypeStruct((depth, 3 * width), BF16)],
        in_specs=[SMEM] * 2 + [VMEM] * 3 + [HBM] * len(pieces),
        out_specs=[VMEM] * 5,
        scratch_shapes=[pltpu.SemaphoreType.DMA((8,))],
        compiler_params=pltpu.CompilerParams(vmem_limit_bytes=48 << 20),
    )(ends, places, normal, cosine, sine, *pieces)


def attention_backward_heads(ends, queries, keys, values, grad_out, cosine, sine):
    count, width = queries.shape

    def kernel(ends_ref, q_ref, k_ref, v_ref, g_ref, cos_ref, sin_ref, out_ref, gk_ref, gv_ref):
        gk_ref[...] = jnp.zeros_like(gk_ref)
        gv_ref[...] = jnp.zeros_like(gv_ref)

        @pl.loop(0, count // BLOCK)
        def _(block):
            here = pl.ds(pl.multiple_of(block * BLOCK, BLOCK), BLOCK)
            allowed = block_mask(ends_ref, block, BLOCK, count)
            for head in range(width // HEAD):
                span = slice(head * HEAD, (head + 1) * HEAD)
                q, g = q_ref[here, span], g_ref[here, span]
                probs = masked_probs(q, k_ref[:, span], allowed)
                grad_probs = lax.dot_general(
                    g, v_ref[:, span], (((1,), (1,)), ((), ())), preferred_element_type=F32
                )
                delta = jnp.sum(probs * grad_probs, axis=-1, keepdims=True)
                grad_scores = (probs * (grad_probs - delta)).astype(BF16)
                grad_query = jnp.dot(grad_scores, k_ref[:, span], preferred_element_type=F32)
                out_ref[here, span] = turn(
                    grad_query * HEAD ** (-0.5), cos_ref[here, :], -sin_ref[here, :]
                ).astype(BF16)
                over_rows = (((0,), (0,)), ((), ()))
                gk_ref[:, span] += lax.dot_general(grad_scores, q, over_rows, preferred_element_type=F32)
                gv_ref[:, span] += lax.dot_general(
                    probs.astype(BF16), g, over_rows, preferred_element_type=F32
                )

        out_ref[:, 2 * width :] = gv_ref[...].astype(BF16)
        for head in range(width // HEAD):
            span = slice(head * HEAD, (head + 1) * HEAD)
            out_ref[:, width + head * HEAD : width + (head + 1) * HEAD] = turn(
                gk_ref[:, span] * HEAD ** (-0.5), cos_ref[...], -sin_ref[...]
            ).astype(BF16)

    return pl.pallas_call(
        kernel,
        out_shape=jax.ShapeDtypeStruct((count, 3 * width), BF16),
        in_specs=[SMEM] + [VMEM] * 6,
        out_specs=VMEM,
        scratch_shapes=[pltpu.VMEM((count, width), F32), pltpu.VMEM((count, width), F32)],
        compiler_params=pltpu.CompilerParams(vmem_limit_bytes=48 << 20),
    )(ends, queries, keys, values, grad_out, cosine, sine)


def norm_parts(values):
    centred = values - jnp.mean(values, axis=-1, keepdims=True)
    inverse = lax.rsqrt(jnp.mean(centred * centred, axis=-1, keepdims=True) + EPSILON)
    return centred * inverse, inverse


def norm_backward(values, scaled):
    normal, inverse = norm_parts(values)
    return inverse * (
        scaled
        - jnp.mean(scaled, axis=-1, keepdims=True)
        - normal * jnp.mean(scaled * normal, axis=-1, keepdims=True)
    )


ROWS = 64


def norm_of(values, gain):
    def kernel(values_ref, gain_ref, out_ref):
        out_ref[...] = (norm_parts(values_ref[...].astype(F32))[0] * gain_ref[...]).astype(BF16)

    count, width = values.shape
    return pl.pallas_call(
        kernel,
        grid=(count // ROWS,),
        out_shape=jax.ShapeDtypeStruct(values.shape, BF16),
        in_specs=[pl.BlockSpec((ROWS, width), lambda i: (i, 0)), pl.BlockSpec((1, width), lambda i: (0, 0))],
        out_specs=pl.BlockSpec((ROWS, width), lambda i: (i, 0)),
    )(values, gain)


def row_kernel(kernel, parts, arrays, gain, outs):
    rows, width = parts.shape[1:]
    whole = pl.BlockSpec((4, ROWS, width), lambda i: (0, i, 0))
    single = pl.BlockSpec((ROWS, width), lambda i: (i, 0))
    return pl.pallas_call(
        kernel,
        grid=(rows // ROWS,),
        out_shape=[jax.ShapeDtypeStruct((rows, width), kind) for kind in outs],
        in_specs=[whole] + [single] * len(arrays) + [pl.BlockSpec((1, width), lambda i: (0, 0))],
        out_specs=[single] * len(outs),
    )(parts, *arrays, gain)


def add_parts(parts_ref):
    total = parts_ref[0].astype(F32)
    for i in range(1, 4):
        total = total + parts_ref[i].astype(F32)
    return total


def middle_rows(parts, inputs, gain):
    def kernel(parts_ref, inputs_ref, gain_ref, middle_ref, normal_ref):
        middle = inputs_ref[...].astype(F32) + add_parts(parts_ref)
        middle_ref[...] = middle
        normal_ref[...] = (norm_parts(middle)[0] * gain_ref[...]).astype(BF16)

    return row_kernel(kernel, parts, [inputs], gain, [F32, BF16])


def grad_middle_rows(parts, middle, cotangent, gain):
    def kernel(parts_ref, middle_ref, cotangent_ref, gain_ref, grad_ref, branch_ref):
        grad = cotangent_ref[...].astype(F32) + norm_backward(middle_ref[...], add_parts(parts_ref) * gain_ref[...])
        grad_ref[...] = grad
        branch_ref[...] = grad.astype(BF16)

    return row_kernel(kernel, parts, [middle, cotangent], gain, [F32, BF16])


def token_grad_rows(parts, inputs, grad_middle, gain):
    def kernel(parts_ref, inputs_ref, middle_ref, gain_ref, grad_ref):
        grad = norm_backward(inputs_ref[...].astype(F32), add_parts(parts_ref) * gain_ref[...])
        grad_ref[...] = (middle_ref[...] + grad).astype(BF16)

    return row_kernel(kernel, parts, [inputs, grad_middle], gain, [BF16])[0]


def feed_forward(normal, grad_activation, places, pieces, piece_rows):
    count, width = normal.shape
    hidden_width = pieces[0].shape[1]
    step_rows = 256
    steps = count // step_rows

    def kernel(places_ref, normal_ref, grad_activation_ref, *rest):
        act_ref, grad_ref, up_out, up_ref, sems, out_sem = rest[len(pieces) :]
        step = pl.program_id(0)
        copies = row_copies(places_ref, rest[: len(pieces)], up_ref, sems, piece_rows)
        back = pltpu.make_async_copy(up_ref, up_out, out_sem)

        @pl.when(step == 0)
        def _():
            for copy in copies:
                copy.start()
            for copy in copies:
                copy.wait()
            back.start()

        hidden = jnp.dot(normal_ref[...], up_ref[...], preferred_element_type=F32)
        scale = math.sqrt(2.0 / math.pi)
        square = hidden * hidden
        tanh = jnp.tanh(scale * hidden * (1.0 + 0.044715 * square))
        act_ref[...] = (0.5 * hidden * (1.0 + tanh)).astype(BF16)
        slope = 0.5 * (1.0 + tanh) + (0.5 * scale) * hidden * (1.0 - tanh * tanh) * (
            1.0 + (3.0 * 0.044715) * square
        )
        grad_ref[...] = (grad_activation_ref[...] * slope).astype(BF16)

        @pl.when(step == steps - 1)
        def _():
            back.wait()

    row_spec = pl.BlockSpec((step_rows, width), lambda i: (i, 0))
    hidden_spec = pl.BlockSpec((step_rows, hidden_width), lambda i: (i, 0))
    return pl.pallas_call(
        kernel,
        grid=(steps,),
        out_shape=[jax.ShapeDtypeStruct((count, hidden_width), BF16)] * 2
        + [jax.ShapeDtypeStruct((width, hidden_width), BF16)],
        in_specs=[SMEM, row_spec, hidden_spec] + [HBM] * len(pieces),
        out_specs=[hidden_spec, hidden_spec, HBM],
        scratch_shapes=[
            pltpu.VMEM((width, hidden_width), BF16),
            pltpu.SemaphoreType.DMA((width // piece_rows,)),
            pltpu.SemaphoreType.DMA,
        ],
        compiler_params=pltpu.CompilerParams(vmem_limit_bytes=48 << 20),
    )(places, normal, grad_activation, *pieces)


def contract_rows(left, right):
    return lax.dot_general(left, right, (((0,), (0,)), ((), ())), preferred_element_type=F32)


def dot_transposed(left, right):
    return lax.dot_general(left, right, (((1,), (1,)), ((), ())), preferred_element_type=F32)


def grouped_body(
    tokens,
    triple_weight,
    output_weight,
    up_weight,
    down_weight,
    first_gain,
    second_gain,
    cotangent,
    frame_counts,
    text_counts,
    action_counts,
):
    rows, width = tokens.shape
    count = rows * MEMBERS
    dp, fsdp = lax.axis_index("dp"), lax.axis_index("fsdp")
    x, core = dp >> 1, dp & 1
    zh = fsdp >> 2

    counts = jnp.concatenate(
        [frame_counts.reshape(-1), text_counts.reshape(-1), action_counts.reshape(-1)]
    )
    counts = jnp.where(core == zh, counts, swap(counts, CORE))
    frames = counts[:2]
    slots = text_counts.shape[-1]
    texts = counts[2 : 2 + 2 * slots].reshape(2, slots)
    actions = counts[2 + 2 * slots :].reshape(2, slots)
    live = jnp.arange(slots, dtype=jnp.int32) < frames[:, None]
    lengths = jnp.sum(jnp.where(live, IMG + texts + actions, 0), axis=-1)
    first_end = lengths[0]
    second_end = lengths[0] + lengths[1]
    ends = jnp.stack([first_end, second_end]).astype(jnp.int32)
    places = jnp.arange(count, dtype=jnp.int32)
    starts = jnp.where(places < first_end, 0, jnp.where(places < second_end, first_end, second_end))
    cosine, sine = rotary_tables(places - starts)
    cosine = jnp.concatenate([cosine[:, 0], cosine[:, 0]], axis=1)
    sine = jnp.concatenate([-sine[:, 0], sine[:, 0]], axis=1)

    hidden_width = up_weight.shape[1] // DEVICES
    triple_columns = lambda m: head_columns(m, width)
    up_columns = lambda m: hidden_columns(m, hidden_width)
    first_column = first_gain.astype(F32)[:, None]
    second_column = second_gain.astype(F32)[:, None]
    sides = ((0, 0), (0, 1), (1, 0), (1, 1))
    rows_of_weight = triple_weight.shape[0]
    block = rows_of_weight * 4
    half_block = down_weight.shape[0] // 4

    def places_of(pieces):
        return jnp.stack([place for a, b, parts in pieces for place in parts(x ^ a, zh ^ b)]).astype(jnp.int32)

    def column_places(*which):
        return lambda sx, sz: [sx * 4 + c * 2 + sz for c in which]

    def down_places(*which):
        return lambda sx, sz: [(sx * 2 + sz) * 4 + q for q in which]

    triple_own = deal_columns(triple_weight, triple_columns, jnp.concatenate([first_gain, second_gain])[None])
    triple_own = exchange(triple_own, CORE, ZL, Y)
    inputs = regroup(tokens)
    down_x = swap(down_weight, X)
    turned = lax.ppermute(output_weight, AXES, turn_pairs())
    cotangent = regroup(cotangent)
    quarters = [down_weight[q * half_block : (q + 1) * half_block] for q in range(4)]
    up_dealt = deal_columns(up_weight, up_columns)
    gains = triple_own[:, rows_of_weight, : 2 * rows_of_weight]
    triple_own = triple_own[:, :rows_of_weight].reshape(-1, triple_own.shape[-1])
    triple_own, inputs, down_x, turned, gains, cotangent, ends, quarters, up_dealt = together(
        triple_own, inputs, down_x, turned, gains, cotangent, ends, quarters, up_dealt
    )
    all_inputs = gather(inputs, CORE, ZL, Y)
    triple_zh = swap(triple_own, ZH)
    triple_x = swap(triple_own, X)
    gains = pair_up(zh, gains, swap(gains, ZH))
    gains = pair_up(x, gains, swap(gains, X))
    gains = gains.reshape(2, 2, 2, 4, 2, -1).transpose(4, 0, 2, 1, 3, 5).reshape(2, -1).astype(F32)
    all_inputs, triple_zh, triple_x, gains, cosine, sine, turned, cotangent, up_dealt, quarters = together(
        all_inputs, triple_zh, triple_x, gains, cosine, sine, turned, cotangent, up_dealt, quarters
    )
    triple_xz = swap(triple_zh, X)
    all_cotangent = gather(cotangent, CORE, ZL, Y)
    turned_zh = swap(turned, ZH)
    down_zh = [swap(quarters[0], ZH)]
    normal = norm_of(all_inputs, gains[:1])
    pair = pair_up(zh, turned, turned_zh)
    triple_xz, normal, pair, down_zh, quarters, up_dealt = together(
        triple_xz, normal, pair, down_zh, quarters, up_dealt
    )
    up_own = exchange(up_dealt, CORE, ZL, Y)
    up_own = up_own.reshape(-1, up_own.shape[-1])
    up_halves = [up_own[:block], up_own[block:]]
    pair_x = swap(pair, X)
    down_zh += [swap(quarters[1], ZH), swap(quarters[2], ZH)]
    down_xz = [swap(down_zh[0], X)]
    queries, keys, values, attended, triple = attention_forward(
        ends,
        places_of([(a, b, column_places(0, 1)) for a, b in sides]),
        normal,
        [triple_own, triple_zh, triple_x, triple_xz],
        cosine,
        sine,
    )
    output = jnp.where(x == 0, jnp.stack([pair, pair_x], axis=1), jnp.stack([pair_x, pair], axis=1))
    output = output.reshape(-1, width)
    down_zh, down_xz, attended, output, up_own, up_halves, quarters = together(
        down_zh, down_xz, attended, output, up_own, up_halves, quarters
    )
    sums = product_sums(core, attended, output)
    sums, up_own, up_halves, quarters, down_zh = together(sums, up_own, up_halves, quarters, down_zh)
    sums = collect(sums)
    up_zh = [swap(up_halves[0], ZH)]
    up_x = swap(up_own, X)
    down_zh.append(swap(quarters[3], ZH))
    down_xz += [swap(down_zh[1], X), swap(down_zh[2], X)]
    sums, up_zh, up_x, up_halves, down_zh, down_xz, all_cotangent = together(
        sums, up_zh, up_x, up_halves, down_zh, down_xz, all_cotangent
    )
    middle, normal_two = middle_rows(sums, inputs, gains[1:])
    normal_two = gather(normal_two, CORE, ZL, Y)
    up_zh.append(swap(up_halves[1], ZH))
    up_xz = [swap(up_zh[0], X)]
    down_xz.append(swap(down_zh[3], X))
    normal_two, up_zh, up_xz, down_xz = together(normal_two, up_zh, up_xz, down_xz)
    up_xz.append(swap(up_zh[1], X))
    down = place_rows(
        places_of(
            [(0, 0, down_places(0, 1, 2, 3))]
            + [(0, 1, down_places(q)) for q in range(4)]
            + [(1, 0, down_places(0, 1, 2, 3))]
            + [(1, 1, down_places(q)) for q in range(4)]
        ),
        [down_weight, *down_zh, down_x, *down_xz],
        half_block,
    )
    grad_activation = dot_transposed(all_cotangent, down)
    activation, grad_hidden, up = feed_forward(
        normal_two,
        grad_activation,
        places_of(
            [(0, 0, column_places(0, 1)), (0, 1, column_places(0)), (0, 1, column_places(1))]
            + [(1, 0, column_places(0, 1)), (1, 1, column_places(0)), (1, 1, column_places(1))]
        ),
        [up_own, *up_zh, up_x, *up_xz],
        block,
    )

    def columns(left, right, start, stop, shape):
        return contract_rows(left, right[:, start:stop]).astype(BF16).reshape(*shape, -1, stop - start)

    cut = width * 3 // 4
    partial = product_sums(core, grad_hidden, up, True)
    down_most = columns(activation, all_cotangent, 0, cut, (2, 1, 2))
    partial, activation, grad_hidden, down_most = together(partial, activation, grad_hidden, down_most)
    sums = collect(partial)
    down_rest = columns(activation, all_cotangent, cut, width, (2, 1, 2)).swapaxes(0, 2)
    down_most_came = give(x, X, down_most)
    down_rest_came = give(zh, ZH, down_rest)
    middle_hidden = grad_hidden.shape[1] // 2
    up_first = columns(normal_two, grad_hidden, 0, middle_hidden, (2, 2, 2))
    sums, down_most_came, down_rest_came, up_first = together(sums, down_most_came, down_rest_came, up_first)
    grad_middle, grad_branch = grad_middle_rows(sums, middle, cotangent, gains[1:])
    grad_branch = gather(grad_branch, CORE, ZL, Y)
    up_first_came = give(x, X, up_first)
    down_rest_far = give_sum(zh, x, X, down_rest, down_rest_came)
    down_most_far = give_sum(x, zh, ZH, down_most, down_most_came)
    up_last = columns(normal_two, grad_hidden, middle_hidden, 2 * middle_hidden, (2, 2, 2))
    output_partial = jnp.dot(activation, down, preferred_element_type=F32).astype(BF16)
    grad_branch, down_rest_far, down_most_far, up_first_came, up_last, output_partial = together(
        grad_branch, down_rest_far, down_most_far, up_first_came, up_last, output_partial
    )
    output_sums = lax.psum_scatter(
        output_partial, AXES, scatter_dimension=0, tiled=True, axis_index_groups=alike(CORE, ZL, Y)
    )
    up_last_came = give(x, X, up_last)
    up_first_far = give_sum(x, zh, ZH, up_first, up_first_came)
    grad_attended = dot_transposed(grad_branch, output).astype(BF16)
    grad_mixed = attention_backward_heads(ends, queries, keys, values, grad_attended, cosine, sine)
    output_term = contract_rows(attended, grad_branch).astype(BF16)
    output_term = output_term.reshape(2, 2, -1, width).swapaxes(0, 1)[:, None]
    triple_term = columns(normal, grad_mixed, 0, grad_mixed.shape[1], (2, 2, 2))
    grad_mixed, up_last_came, up_first_far, output_term, triple_term = together(
        grad_mixed, up_last_came, up_first_far, output_term, triple_term
    )
    partial = product_sums(core, grad_mixed, triple, True)
    triple_sent = lax.dynamic_index_in_dim(triple_term, 1 - x, 0, False)
    partial, triple_sent, up_last_came = together(partial, triple_sent, up_last_came)
    sums = collect(partial)
    triple_came = swap(triple_sent, X)
    up_last_far = give_sum(x, zh, ZH, up_last, up_last_came)
    sums, triple_came, up_last_far, output_term, up_first_far = together(
        sums, triple_came, up_last_far, output_term, up_first_far
    )
    triple_far = give_sum(x, zh, ZH, triple_term, triple_came)
    output_came = give(x, X, output_term)
    up_parts = [
        keep_sum(x, zh, up_first, up_first_came, up_first_far),
        keep_sum(x, zh, up_last, up_last_came, up_last_far),
    ]
    up_parts = [part.astype(BF16).reshape(MEMBERS, -1, middle_hidden) for part in up_parts]
    up_slabs = exchange(jnp.concatenate(up_parts, axis=2), CORE, ZL, Y)
    token_grad = token_grad_rows(sums, inputs, grad_middle, gains[:1])
    triple_far, output_came, output_sums, token_grad, up_slabs = together(
        triple_far, output_came, output_sums, token_grad, up_slabs
    )
    triple_sum = keep_sum(x, zh, triple_term, triple_came, triple_far).astype(BF16)
    triple_sum = triple_sum.reshape(MEMBERS, -1, triple_sum.shape[-1])
    triple_slabs = exchange(triple_sum, CORE, ZL, Y)
    token_grad = regroup(token_grad)
    layer_output = regroup((middle + output_sums.astype(F32)).astype(BF16))
    output_far = give_sum(x, zh, ZH, output_term, output_came)
    output_sum = keep_sum(x, zh, output_term, output_came, output_far)[0]
    output_grad = lax.ppermute(output_sum.astype(BF16), AXES, turn_pairs()).astype(F32)
    down_grad = jnp.concatenate(
        [
            keep_sum(x, zh, down_most, down_most_came, down_most_far)[0],
            keep_sum(zh, x, down_rest, down_rest_came, down_rest_far)[0],
        ],
        axis=1,
    )
    triple_grad, first_gain_grad = place_columns(triple_slabs, triple_weight, first_column, triple_columns)
    up_grad, second_gain_grad = place_columns(up_slabs, up_weight, second_column, up_columns)
    return (
        layer_output,
        token_grad,
        triple_grad,
        output_grad,
        up_grad,
        down_grad,
        first_gain_grad[:, 0],
        second_gain_grad[:, 0],
    )


def solution(mesh):
    grouped = mesh.shape["dp"] * 2 == mesh.shape["fsdp"] == MEMBERS
    rows = P(AXES, None)
    return jax.shard_map(
        grouped_body if grouped else whole_rows_body,
        mesh=mesh,
        in_specs=(rows,) * 5 + (P(AXES),) * 2 + (rows, P("dp", None), P("dp", None, None), P("dp", None, None)),
        out_specs=(rows,) * 6 + (P(AXES),) * 2,
        check_vma=False,
    )
```

```python
import math

import jax
import jax.numpy as jnp
from jax import lax
from jax.experimental import pallas as pl
from jax.experimental.pallas import tpu as pltpu
from jax.sharding import PartitionSpec as P

HEADS = 16
HEAD = 128
IMG = 576


EPSILON = 1e-05
MASKED = -1e30


def clip_layout(frame_counts, text_counts, action_counts, pack_length):
    frame_slot = jnp.arange(text_counts.shape[-1], dtype=jnp.int32)
    frame_live = frame_slot < frame_counts[..., None]
    frame_sizes = jnp.where(frame_live, IMG + text_counts + action_counts, 0)
    clip_lengths = jnp.sum(frame_sizes, axis=-1)
    first_end = clip_lengths[..., 0:1]
    second_end = first_end + clip_lengths[..., 1:2]
    places = jnp.arange(pack_length, dtype=jnp.int32)
    segment = (places >= first_end).astype(jnp.int32) + (places >= second_end).astype(jnp.int32)
    starts = jnp.where(segment == 0, 0, jnp.where(segment == 1, first_end, second_end))
    return (segment, places - starts)


def rotary_tables(position):
    half_width = HEAD // 2
    frequency = jnp.exp(
        jnp.arange(half_width, dtype=jnp.float32) * (-2.0 * math.log(10000.0) / HEAD)
    )
    angles = position.astype(jnp.float32)[:, None] * frequency[None, :]
    return (jnp.cos(angles)[:, None, :], jnp.sin(angles)[:, None, :])


def rotate(vectors, cosine, sine_table):
    half_width = vectors.shape[-1] // 2
    former = vectors[..., :half_width]
    latter = vectors[..., half_width:]
    return jnp.concatenate(
        [former * cosine - latter * sine_table, latter * cosine + former * sine_table], axis=-1
    )


def unrotate(gradient, cosine, sine_table):
    half_width = gradient.shape[-1] // 2
    former = gradient[..., :half_width]
    latter = gradient[..., half_width:]
    return jnp.concatenate(
        [former * cosine + latter * sine_table, latter * cosine - former * sine_table], axis=-1
    )


def norm_rows(values, gain_vector):
    centred = values - jnp.mean(values, axis=-1, keepdims=True)
    variance = jnp.mean(centred * centred, axis=-1, keepdims=True)
    return centred * lax.rsqrt(variance + EPSILON) * gain_vector


def block_allowed(query_segment, query_places, key_segment, key_place):
    return (query_segment[:, None] == key_segment[None, :]) & (
        key_place[None, :] <= query_places[:, None]
    )


def block_scores(queries, key_block, allowed):
    scores = jnp.einsum(
        "qhd,khd->hqk", queries, key_block, preferred_element_type=jnp.float32
    ) * HEAD ** (-0.5)
    return jnp.where(allowed[None], scores, MASKED)


def block_probs(queries, key_block, allowed, row_max, row_sum):
    scores = block_scores(queries, key_block, allowed)
    return jnp.where(allowed[None], jnp.exp(scores - row_max[..., None]) / row_sum[..., None], 0.0)


def softmax_stats(queries, key_blocks, layout_parts):
    query_segment, query_places, key_segments, key_places = layout_parts
    row_count, head_count = (queries.shape[0], queries.shape[1])
    start_state = (
        jnp.full((head_count, row_count), MASKED, jnp.float32),
        jnp.zeros((head_count, row_count), jnp.float32),
    )

    def advance(state, block_inputs):
        key_block, key_segment, key_place = block_inputs
        allowed = block_allowed(query_segment, query_places, key_segment, key_place)

        def update(current):
            row_max, row_sum = current
            scores = block_scores(queries, key_block, allowed)
            new_max = jnp.maximum(row_max, jnp.max(scores, axis=-1))
            weights = jnp.where(allowed[None], jnp.exp(scores - new_max[..., None]), 0.0)
            return (new_max, row_sum * jnp.exp(row_max - new_max) + jnp.sum(weights, axis=-1))

        return (lax.cond(jnp.any(allowed), update, lambda current: current, state), None)

    final_state, unused = lax.scan(advance, start_state, (key_blocks, key_segments, key_places))
    return final_state


def attention_output(queries, key_blocks, value_blocks, layout_parts, row_max, row_sum):
    query_segment, query_places, key_segments, key_places = layout_parts

    def advance(accum, block_inputs):
        key_block, value_block, key_segment, key_place = block_inputs
        allowed = block_allowed(query_segment, query_places, key_segment, key_place)

        def update(current):
            probs = block_probs(queries, key_block, allowed, row_max, row_sum).astype(jnp.bfloat16)
            return current + jnp.einsum(
                "hqk,khd->qhd", probs, value_block, preferred_element_type=jnp.float32
            )

        return (lax.cond(jnp.any(allowed), update, lambda current: current, accum), None)

    attended, unused = lax.scan(
        advance,
        jnp.zeros(queries.shape, jnp.float32),
        (key_blocks, value_blocks, key_segments, key_places),
    )
    return attended


def attention_backward(
    queries, grad_attended, delta_rows, key_blocks, value_blocks, layout_parts, row_max, row_sum
):
    query_segment, query_places, key_segments, key_places = layout_parts
    score_scale = HEAD ** (-0.5)

    def advance(grad_query, block_inputs):
        key_block, value_block, key_segment, key_place = block_inputs
        allowed = block_allowed(query_segment, query_places, key_segment, key_place)

        def update(current):
            probs = block_probs(queries, key_block, allowed, row_max, row_sum)
            grad_probs = jnp.einsum(
                "qhd,khd->hqk", grad_attended, value_block, preferred_element_type=jnp.float32
            )
            grad_scores = (probs * (grad_probs - delta_rows[..., None])).astype(jnp.bfloat16)
            new_query = (
                current
                + jnp.einsum(
                    "hqk,khd->qhd", grad_scores, key_block, preferred_element_type=jnp.float32
                )
                * score_scale
            )
            return (new_query, ())

        def bypass(current):
            return (current, ())

        return lax.cond(jnp.any(allowed), update, bypass, grad_query)

    grad_query, terms = lax.scan(
        advance,
        jnp.zeros(queries.shape, jnp.float32),
        (key_blocks, value_blocks, key_segments, key_places),
    )
    return (grad_query, None, None)


def project_front(inputs, triple_full, gain_full, cosine, sine_table):
    row_count, width = inputs.shape
    normed = norm_rows(inputs, gain_full.astype(jnp.float32)).astype(jnp.bfloat16)
    mixed = jnp.dot(normed, triple_full, preferred_element_type=jnp.float32)
    queries = rotate(mixed[:, :width].reshape(row_count, HEADS, HEAD), cosine, sine_table).astype(
        jnp.bfloat16
    )
    keys_local = (
        rotate(mixed[:, width : 2 * width].reshape(row_count, HEADS, HEAD), cosine, sine_table)
        .astype(jnp.bfloat16)
        .reshape(row_count, width)
    )
    values_local = mixed[:, 2 * width :].astype(jnp.bfloat16)
    return (normed, queries, keys_local, values_local)


def run_attention(queries, gathered, layout_parts):
    block_count = layout_parts[2].shape[0]
    key_blocks = gathered[0].reshape(block_count, -1, HEADS, HEAD)
    value_blocks = gathered[1].reshape(block_count, -1, HEADS, HEAD)
    row_max, row_sum = softmax_stats(queries, key_blocks, layout_parts)
    attended = attention_output(queries, key_blocks, value_blocks, layout_parts, row_max, row_sum)
    return (attended, key_blocks, value_blocks, row_max, row_sum)


def finish_layer(inputs, attended, output_full, up_full, down_full, second_full):
    row_count, width = inputs.shape
    attended_low = attended.reshape(row_count, width).astype(jnp.bfloat16)
    middle = inputs + jnp.dot(attended_low, output_full, preferred_element_type=jnp.float32)
    normed_two = norm_rows(middle, second_full.astype(jnp.float32)).astype(jnp.bfloat16)
    hidden = jnp.dot(normed_two, up_full, preferred_element_type=jnp.float32)
    activation = jax.nn.gelu(hidden).astype(jnp.bfloat16)
    result = middle + jnp.dot(activation, down_full, preferred_element_type=jnp.float32)
    return (result, attended_low, middle, normed_two, hidden, activation)


def whole_rows_body(
    tokens,
    triple_weight,
    output_weight,
    up_weight,
    down_weight,
    first_gain,
    second_gain,
    cotangent,
    frame_counts,
    text_counts,
    action_counts,
):
    row_count, width = tokens.shape
    pack_length = row_count * lax.axis_size("fsdp")
    first_place = lax.axis_index("fsdp") * row_count
    segment, position = clip_layout(frame_counts[0], text_counts[0], action_counts[0], pack_length)
    block_rows = min(1024, pack_length)
    block_count = pack_length // block_rows
    query_places = first_place + jnp.arange(row_count, dtype=jnp.int32)
    own_segment = lax.dynamic_slice_in_dim(segment, first_place, row_count, 0)
    layout_parts = (
        own_segment,
        query_places,
        segment.reshape(block_count, block_rows),
        jnp.arange(pack_length, dtype=jnp.int32).reshape(block_count, block_rows),
    )
    cosine, sine_table = rotary_tables(
        lax.dynamic_slice_in_dim(position, first_place, row_count, 0)
    )
    inputs = tokens.astype(jnp.float32)
    attention_set = (
        lax.all_gather(triple_weight, ("dp", "fsdp"), axis=0, tiled=True),
        lax.all_gather(output_weight, ("dp", "fsdp"), axis=0, tiled=True),
        lax.all_gather(first_gain, ("dp", "fsdp"), axis=0, tiled=True),
    )
    normed, queries, keys_local, values_local = project_front(
        inputs, attention_set[0], attention_set[2], cosine, sine_table
    )
    gathered = (
        lax.all_gather(keys_local, "fsdp", axis=0, tiled=True),
        lax.all_gather(values_local, "fsdp", axis=0, tiled=True),
    )
    attended, key_blocks, value_blocks, row_max, row_sum = run_attention(
        queries, gathered, layout_parts
    )
    feedforward_set = (
        lax.all_gather(up_weight, ("dp", "fsdp"), axis=0, tiled=True),
        lax.all_gather(down_weight, ("dp", "fsdp"), axis=0, tiled=True),
        lax.all_gather(second_gain, ("dp", "fsdp"), axis=0, tiled=True),
    )
    kept_parts = finish_layer(
        inputs,
        attended,
        attention_set[1],
        feedforward_set[0],
        feedforward_set[1],
        feedforward_set[2],
    )
    layer_output = kept_parts[0].astype(jnp.bfloat16)
    attention_set = (
        lax.all_gather(triple_weight, ("dp", "fsdp"), axis=0, tiled=True),
        lax.all_gather(output_weight, ("dp", "fsdp"), axis=0, tiled=True),
        lax.all_gather(first_gain, ("dp", "fsdp"), axis=0, tiled=True),
    )
    normed, queries, keys_local, values_local = project_front(
        inputs, attention_set[0], attention_set[2], cosine, sine_table
    )
    gathered = (
        lax.all_gather(keys_local, "fsdp", axis=0, tiled=True),
        lax.all_gather(values_local, "fsdp", axis=0, tiled=True),
    )
    attended, key_blocks, value_blocks, row_max, row_sum = run_attention(
        queries, gathered, layout_parts
    )
    feedforward_set = (
        lax.all_gather(up_weight, ("dp", "fsdp"), axis=0, tiled=True),
        lax.all_gather(down_weight, ("dp", "fsdp"), axis=0, tiled=True),
        lax.all_gather(second_gain, ("dp", "fsdp"), axis=0, tiled=True),
    )
    kept_parts = finish_layer(
        inputs,
        attended,
        attention_set[1],
        feedforward_set[0],
        feedforward_set[1],
        feedforward_set[2],
    )
    unused_result, attended_low, middle, normed_two, hidden, activation = kept_parts
    down_term = jnp.einsum("rf,rd->fd", activation, cotangent, preferred_element_type=jnp.float32)
    grad_activation = jnp.einsum(
        "rd,fd->rf", cotangent, feedforward_set[1], preferred_element_type=jnp.float32
    )
    unused_gelu, gelu_pull = jax.vjp(jax.nn.gelu, hidden)
    grad_hidden = gelu_pull(grad_activation)[0].astype(jnp.bfloat16)
    up_term = jnp.einsum("rd,rf->df", normed_two, grad_hidden, preferred_element_type=jnp.float32)
    grad_normed_two = jnp.einsum(
        "rf,df->rd", grad_hidden, feedforward_set[0], preferred_element_type=jnp.float32
    )
    unused_second, second_pull = jax.vjp(norm_rows, middle, feedforward_set[2].astype(jnp.float32))
    grad_middle_norm, second_gain_term = second_pull(grad_normed_two)
    grad_middle = cotangent.astype(jnp.float32) + grad_middle_norm
    feedforward_sums = (
        lax.psum_scatter(up_term, ("dp", "fsdp"), scatter_dimension=0, tiled=True),
        lax.psum_scatter(down_term, ("dp", "fsdp"), scatter_dimension=0, tiled=True),
        lax.psum_scatter(second_gain_term, ("dp", "fsdp"), scatter_dimension=0, tiled=True),
    )
    grad_branch = grad_middle.astype(jnp.bfloat16)
    output_term = jnp.einsum(
        "rd,re->de", attended_low, grad_branch, preferred_element_type=jnp.float32
    )
    grad_attended = (
        jnp.einsum("re,de->rd", grad_branch, attention_set[1], preferred_element_type=jnp.float32)
        .astype(jnp.bfloat16)
        .reshape(row_count, HEADS, HEAD)
    )
    delta_rows = jnp.sum(grad_attended.astype(jnp.float32) * attended, axis=-1).T
    score_scale = HEAD ** (-0.5)
    grad_query = attention_backward(
        queries, grad_attended, delta_rows, key_blocks, value_blocks, layout_parts, row_max, row_sum
    )[0]
    pack_stats = (
        lax.all_gather(row_max.T, "fsdp", axis=0, tiled=True),
        lax.all_gather(row_sum.T, "fsdp", axis=0, tiled=True),
        lax.all_gather(delta_rows.T, "fsdp", axis=0, tiled=True),
    )
    own_keys = keys_local.reshape(row_count, HEADS, HEAD)
    own_values = values_local.reshape(row_count, HEADS, HEAD)
    empty_grads = jnp.zeros((row_count, HEADS, HEAD), jnp.float32)
    query_piece = lax.all_gather(queries, "fsdp", axis=0, tiled=True)
    grad_piece = lax.all_gather(grad_attended, "fsdp", axis=0, tiled=True)
    piece_rows = query_piece.shape[0]
    block_size = min(1024, piece_rows)
    block_total = piece_rows // block_size

    def advance(current, block_index):
        offset = block_index * block_size
        query_part = lax.dynamic_slice_in_dim(query_piece, offset, block_size, 0)
        grad_part = lax.dynamic_slice_in_dim(grad_piece, offset, block_size, 0)
        max_part = lax.dynamic_slice_in_dim(pack_stats[0], offset, block_size, 0).T
        sum_part = lax.dynamic_slice_in_dim(pack_stats[1], offset, block_size, 0).T
        delta_part = lax.dynamic_slice_in_dim(pack_stats[2], offset, block_size, 0).T
        part_segment = lax.dynamic_slice_in_dim(segment, offset, block_size, 0)
        part_places = offset + jnp.arange(block_size, dtype=jnp.int32)
        allowed = block_allowed(part_segment, part_places, own_segment, query_places)

        def update(pair):
            probs = block_probs(query_part, own_keys, allowed, max_part, sum_part)
            grad_probs = jnp.einsum(
                "qhd,khd->hqk", grad_part, own_values, preferred_element_type=jnp.float32
            )
            grad_scores = (probs * (grad_probs - delta_part[..., None])).astype(jnp.bfloat16)
            grad_key = (
                pair[0]
                + jnp.einsum(
                    "hqk,qhd->khd", grad_scores, query_part, preferred_element_type=jnp.float32
                )
                * score_scale
            )
            grad_value = pair[1] + jnp.einsum(
                "hqk,qhd->khd",
                probs.astype(jnp.bfloat16),
                grad_part,
                preferred_element_type=jnp.float32,
            )
            return (grad_key, grad_value)

        return (lax.cond(jnp.any(allowed), update, lambda pair: pair, current), None)

    result, unused = lax.scan(
        advance, (empty_grads, empty_grads), jnp.arange(block_total, dtype=jnp.int32)
    )
    key_grad_sum = result[0].reshape(row_count, width)
    value_grad_sum = result[1].reshape(row_count, width)
    grad_query_full = (
        unrotate(grad_query, cosine, sine_table).reshape(row_count, width).astype(jnp.bfloat16)
    )
    grad_key_full = (
        unrotate(key_grad_sum.reshape(row_count, HEADS, HEAD), cosine, sine_table)
        .reshape(row_count, width)
        .astype(jnp.bfloat16)
    )
    grad_value_full = value_grad_sum.astype(jnp.bfloat16)
    grad_mixed = jnp.concatenate([grad_query_full, grad_key_full, grad_value_full], axis=1)
    triple_term = jnp.einsum("rd,re->de", normed, grad_mixed, preferred_element_type=jnp.float32)
    grad_normed = jnp.einsum(
        "re,de->rd", grad_mixed, attention_set[0], preferred_element_type=jnp.float32
    )
    unused_first, first_pull = jax.vjp(norm_rows, inputs, attention_set[2].astype(jnp.float32))
    grad_input_norm, first_gain_term = first_pull(grad_normed)
    token_grad = (grad_middle + grad_input_norm).astype(jnp.bfloat16)
    attention_sums = (
        lax.psum_scatter(triple_term, ("dp", "fsdp"), scatter_dimension=0, tiled=True),
        lax.psum_scatter(output_term, ("dp", "fsdp"), scatter_dimension=0, tiled=True),
        lax.psum_scatter(first_gain_term, ("dp", "fsdp"), scatter_dimension=0, tiled=True),
    )
    return (
        layer_output,
        token_grad,
        attention_sums[0],
        attention_sums[1],
        feedforward_sums[0],
        feedforward_sums[1],
        attention_sums[2],
        feedforward_sums[2],
    )


AXES = ("dp", "fsdp")
DEVICES = 32
MEMBERS = 8
CORE, ZL, Y = 8, 2, 1
X, ZH = 16, 4
BF16 = jnp.bfloat16
F32 = jnp.float32
SMEM = pl.BlockSpec(memory_space=pltpu.SMEM)
VMEM = pl.BlockSpec(memory_space=pltpu.VMEM)
HBM = pl.BlockSpec(memory_space=pltpu.HBM)


def swap(array, bits):
    return lax.ppermute(array, AXES, [(i, i ^ bits) for i in range(DEVICES)])


def alike(*bits):
    groups = {}
    for i in range(DEVICES):
        groups.setdefault(i & ~sum(bits), []).append(i)
    return list(groups.values())


def exchange(array, *bits):
    return lax.all_to_all(array, AXES, 0, 0, tiled=True, axis_index_groups=alike(*bits))


def after(array, *others):
    return lax.optimization_barrier((array,) + others)[0]


def together(*arrays):
    return lax.optimization_barrier(arrays)


def regroup_pairs():
    def target(i):
        x, core, zh, low = i >> 4, (i >> 3) & 1, (i >> 2) & 1, i & 3
        return (x << 4) | (zh << 3) | (core << 2) | low

    return [(i, target(i)) for i in range(DEVICES)]


def regroup(array):
    return lax.ppermute(array, AXES, regroup_pairs())


def turn_pairs():
    return [(i, (i & 14) | (i & 1) << 4 | i >> 4) for i in range(DEVICES)]


def gather(own, *bits):
    return lax.all_gather(own, AXES, axis=0, tiled=True, axis_index_groups=alike(*bits))


def collect(parts):
    return exchange(parts.reshape(4, -1, parts.shape[1]), ZL, Y)


def row_product(half, left, right, transposed, came=None):
    count, depth = left.shape[0] // 2, left.shape[1]
    width = right.shape[0] if transposed else right.shape[1]
    tile = 512

    def kernel(half_ref, left_ref, right_ref, *rest):
        if transposed:
            total = dot_transposed(left_ref[...], right_ref[...])
        else:
            total = jnp.dot(left_ref[...], right_ref[...], preferred_element_type=F32)
        if came is not None:
            total = total + rest[0][...].astype(F32)
        rest[-1][...] = total.astype(BF16)

    columns = pl.BlockSpec((count, tile), lambda i, half_ref: (0, i))
    if transposed:
        right_spec = pl.BlockSpec((tile, depth), lambda i, half_ref: (i, 0))
    else:
        right_spec = pl.BlockSpec((depth, tile), lambda i, half_ref: (0, i))
    more = [] if came is None else [came]
    return pl.pallas_call(
        kernel,
        grid_spec=pltpu.PrefetchScalarGridSpec(
            num_scalar_prefetch=1,
            grid=(width // tile,),
            in_specs=[pl.BlockSpec((count, depth), lambda i, half_ref: (half_ref[0], 0)), right_spec]
            + [columns] * len(more),
            out_specs=columns,
        ),
        out_shape=jax.ShapeDtypeStruct((count, width), BF16),
        compiler_params=pltpu.CompilerParams(vmem_limit_bytes=32 << 20),
    )(half, left, right, *more)


def product_sums(core, rows, right, transposed=False):
    near, far = core.reshape(1), (1 - core).reshape(1)
    came = swap(row_product(far, rows, right, transposed), CORE)
    return row_product(near, rows, right, transposed, came)


def hidden_columns(member, width):
    core, zl, y = (member >> 2) & 1, (member >> 1) & 1, member & 1
    return [
        ((gx * X + core * CORE + gz * ZH + zl * ZL + y) * width, width)
        for gx in range(2)
        for gz in range(2)
    ]


def head_columns(member, width):
    core, zl, y = (member >> 2) & 1, (member >> 1) & 1, member & 1
    return [
        (part * width + ((y * 2 + core) * 4 + half * 2 + zl) * HEAD, HEAD)
        for part in range(3)
        for half in range(2)
    ]


def deal_columns(own, columns, extra=()):
    rows = own.shape[0]
    width = own.shape[1] // MEMBERS
    more = 16 if extra else 0

    def kernel(*refs):
        own_ref, slabs_ref = refs[0], refs[-1]
        for member in range(MEMBERS):
            start = 0
            for place, size in columns(member):
                slabs_ref[member, :rows, start : start + size] = own_ref[:, place : place + size]
                start += size
            if more:
                slabs_ref[member, rows:, :] = jnp.zeros((more, width), own.dtype)
                for i, extra_ref in enumerate(refs[1:-1]):
                    slabs_ref[member, rows:, i * HEAD : i * HEAD + rows] = jnp.broadcast_to(
                        extra_ref[...], (more, rows)
                    )

    arrays = [own, *extra]
    return pl.pallas_call(
        kernel,
        out_shape=jax.ShapeDtypeStruct((MEMBERS, rows + more, width), own.dtype),
        in_specs=[VMEM] * len(arrays),
        out_specs=VMEM,
    )(*arrays)


def pair_up(index, mine, theirs):
    return jnp.where(index == 0, jnp.stack([mine, theirs]), jnp.stack([theirs, mine]))


def row_copies(places_ref, pieces, whole_ref, sems, rows):
    sources = [(piece, start) for piece in pieces for start in range(0, piece.shape[0], rows)]
    return [
        pltpu.make_async_copy(
            piece.at[pl.ds(start, rows)],
            whole_ref.at[pl.ds(pl.multiple_of(places_ref[n] * rows, rows), rows)],
            sems.at[n],
        )
        for n, (piece, start) in enumerate(sources)
    ]


def place_rows(places, pieces, rows):
    count = sum(piece.shape[0] for piece in pieces)

    def kernel(places_ref, *rest):
        whole_ref, sems = rest[-2:]
        copies = row_copies(places_ref, rest[:-2], whole_ref, sems, rows)
        for copy in copies:
            copy.start()
        for copy in copies:
            copy.wait()

    return pl.pallas_call(
        kernel,
        out_shape=jax.ShapeDtypeStruct((count, pieces[0].shape[1]), BF16),
        in_specs=[SMEM] + [HBM] * len(pieces),
        out_specs=VMEM,
        scratch_shapes=[pltpu.SemaphoreType.DMA((count // rows,))],
        compiler_params=pltpu.CompilerParams(vmem_limit_bytes=16 << 20),
    )(places, *pieces)


def place_columns(slabs, own, gain, columns):
    rows = own.shape[0]
    sources = [(i, lane) for i, slab in enumerate(slabs) for lane in range(0, slab.shape[2], HEAD)]

    def kernel(*refs):
        slab_refs, (own_ref, gain_ref, whole_ref, sum_ref) = refs[: len(slabs)], refs[len(slabs) :]
        total = jnp.zeros((rows, HEAD), F32)
        for member in range(MEMBERS):
            places = [place + lane for place, size in columns(member) for lane in range(0, size, HEAD)]
            for place, (i, lane) in zip(places, sources):
                part = slab_refs[i][member, :, lane : lane + HEAD].astype(F32)
                whole_ref[:, place : place + HEAD] = part
                total = total + part * own_ref[:, place : place + HEAD].astype(F32)
        sum_ref[...] = jnp.sum(total, axis=1, keepdims=True) / gain_ref[...]

    return pl.pallas_call(
        kernel,
        out_shape=[jax.ShapeDtypeStruct(own.shape, F32), jax.ShapeDtypeStruct((rows, 1), F32)],
        in_specs=[VMEM] * (len(slabs) + 2),
        out_specs=[VMEM] * 2,
        compiler_params=pltpu.CompilerParams(vmem_limit_bytes=32 << 20),
    )(*slabs, own, gain)


def give(index, bits, grad):
    return swap(lax.dynamic_index_in_dim(grad, 1 - index, 0, False), bits)


def half_sum(first, second, grad, came):
    outer, inner, width = grad.shape[1], grad.shape[3], grad.shape[4]
    mine = lax.dynamic_slice(grad, (first, 0, second, 0, 0), (1, outer, 1, inner, width))
    theirs = lax.dynamic_slice(came, (0, second, 0, 0), (outer, 1, inner, width))
    shape = (outer, inner, width)
    return mine.reshape(shape).astype(F32) + theirs.reshape(shape).astype(F32)


def give_sum(first, second, bits, grad, came):
    return swap(half_sum(first, 1 - second, grad, came).astype(BF16), bits)


def keep_sum(first, second, grad, came, far):
    return half_sum(first, second, grad, came) + far.astype(F32)


def turn(vectors, cosine, sine):
    return vectors * cosine + pltpu.roll(vectors, HEAD // 2, 1) * sine


def block_mask(ends_ref, block):
    first_end, second_end = ends_ref[0], ends_ref[1]
    place = lax.broadcasted_iota(jnp.int32, (BLOCK, 1), 0) + block * BLOCK
    key_place = lax.broadcasted_iota(jnp.int32, (1, (block + 1) * BLOCK), 1)
    start = jnp.where(place < first_end, 0, jnp.where(place < second_end, first_end, second_end))
    return (key_place <= place) & (key_place >= start)


def masked_probs(queries, keys, allowed):
    scores = lax.dot_general(queries, keys, (((1,), (1,)), ((), ())), preferred_element_type=F32)
    scores = jnp.where(allowed, scores * HEAD ** (-0.5), MASKED)
    weights = jnp.exp(scores - jnp.max(scores, axis=-1, keepdims=True))
    return weights * (1.0 / jnp.sum(weights, axis=-1, keepdims=True))


BLOCK = 256


def attention_forward(ends, places, normal, pieces, cosine, sine):
    count, depth = normal.shape
    width = pieces[0].shape[1] // 3
    block_rows = depth // 8

    def kernel(ends_ref, places_ref, normal_ref, cos_ref, sin_ref, *rest):
        piece_refs, (q_ref, k_ref, v_ref, out_ref, weight_ref, sems) = rest[: len(pieces)], rest[len(pieces) :]
        copies = row_copies(places_ref, piece_refs, weight_ref, sems, block_rows)
        for copy in copies:
            copy.start()
        for copy in copies:
            copy.wait()

        @pl.loop(0, count // BLOCK)
        def _(block):
            here = pl.ds(pl.multiple_of(block * BLOCK, BLOCK), BLOCK)
            mixed = jnp.dot(normal_ref[here, :], weight_ref[...], preferred_element_type=F32)
            cos, sin = cos_ref[here, :], sin_ref[here, :]
            v_ref[here, :] = mixed[:, 2 * width :].astype(BF16)
            for head in range(width // HEAD):
                span = slice(head * HEAD, (head + 1) * HEAD)
                key_span = slice(width + head * HEAD, width + (head + 1) * HEAD)
                q_ref[here, span] = turn(mixed[:, span], cos, sin).astype(BF16)
                k_ref[here, span] = turn(mixed[:, key_span], cos, sin).astype(BF16)

        for block in range(count // BLOCK):
            here, keys = slice(block * BLOCK, (block + 1) * BLOCK), slice(0, (block + 1) * BLOCK)
            allowed = block_mask(ends_ref, block)
            for head in range(width // HEAD):
                span = slice(head * HEAD, (head + 1) * HEAD)
                probs = masked_probs(q_ref[here, span], k_ref[keys, span], allowed)
                out_ref[here, span] = jnp.dot(
                    probs.astype(BF16), v_ref[keys, span], preferred_element_type=F32
                ).astype(BF16)

    return pl.pallas_call(
        kernel,
        out_shape=[jax.ShapeDtypeStruct((count, width), BF16)] * 4
        + [jax.ShapeDtypeStruct((depth, 3 * width), BF16)],
        in_specs=[SMEM] * 2 + [VMEM] * 3 + [HBM] * len(pieces),
        out_specs=[VMEM] * 5,
        scratch_shapes=[pltpu.SemaphoreType.DMA((8,))],
        compiler_params=pltpu.CompilerParams(vmem_limit_bytes=48 << 20),
    )(ends, places, normal, cosine, sine, *pieces)


def attention_backward_heads(ends, queries, keys, values, grad_out, cosine, sine):
    count, width = queries.shape

    def kernel(ends_ref, q_ref, k_ref, v_ref, g_ref, cos_ref, sin_ref, out_ref, gk_ref, gv_ref):
        gk_ref[...] = jnp.zeros_like(gk_ref)
        gv_ref[...] = jnp.zeros_like(gv_ref)

        for block in range(count // BLOCK):
            here, keys = slice(block * BLOCK, (block + 1) * BLOCK), slice(0, (block + 1) * BLOCK)
            allowed = block_mask(ends_ref, block)
            for head in range(width // HEAD):
                span = slice(head * HEAD, (head + 1) * HEAD)
                q, g = q_ref[here, span], g_ref[here, span]
                probs = masked_probs(q, k_ref[keys, span], allowed)
                grad_probs = lax.dot_general(
                    g, v_ref[keys, span], (((1,), (1,)), ((), ())), preferred_element_type=F32
                )
                delta = jnp.sum(probs * grad_probs, axis=-1, keepdims=True)
                grad_scores = (probs * (grad_probs - delta)).astype(BF16)
                grad_query = jnp.dot(grad_scores, k_ref[keys, span], preferred_element_type=F32)
                out_ref[here, span] = turn(
                    grad_query * HEAD ** (-0.5), cos_ref[here, :], -sin_ref[here, :]
                ).astype(BF16)
                over_rows = (((0,), (0,)), ((), ()))
                gk_ref[keys, span] += lax.dot_general(grad_scores, q, over_rows, preferred_element_type=F32)
                gv_ref[keys, span] += lax.dot_general(
                    probs.astype(BF16), g, over_rows, preferred_element_type=F32
                )

        out_ref[:, 2 * width :] = gv_ref[...].astype(BF16)
        for head in range(width // HEAD):
            span = slice(head * HEAD, (head + 1) * HEAD)
            out_ref[:, width + head * HEAD : width + (head + 1) * HEAD] = turn(
                gk_ref[:, span] * HEAD ** (-0.5), cos_ref[...], -sin_ref[...]
            ).astype(BF16)

    return pl.pallas_call(
        kernel,
        out_shape=jax.ShapeDtypeStruct((count, 3 * width), BF16),
        in_specs=[SMEM] + [VMEM] * 6,
        out_specs=VMEM,
        scratch_shapes=[pltpu.VMEM((count, width), F32), pltpu.VMEM((count, width), F32)],
        compiler_params=pltpu.CompilerParams(vmem_limit_bytes=48 << 20),
    )(ends, queries, keys, values, grad_out, cosine, sine)


def norm_parts(values):
    centred = values - jnp.mean(values, axis=-1, keepdims=True)
    inverse = lax.rsqrt(jnp.mean(centred * centred, axis=-1, keepdims=True) + EPSILON)
    return centred * inverse, inverse


def norm_backward(values, scaled):
    normal, inverse = norm_parts(values)
    return inverse * (
        scaled
        - jnp.mean(scaled, axis=-1, keepdims=True)
        - normal * jnp.mean(scaled * normal, axis=-1, keepdims=True)
    )


ROWS = 64


def norm_of(values, gain):
    def kernel(values_ref, gain_ref, out_ref):
        out_ref[...] = (norm_parts(values_ref[...].astype(F32))[0] * gain_ref[...]).astype(BF16)

    count, width = values.shape
    return pl.pallas_call(
        kernel,
        grid=(count // ROWS,),
        out_shape=jax.ShapeDtypeStruct(values.shape, BF16),
        in_specs=[pl.BlockSpec((ROWS, width), lambda i: (i, 0)), pl.BlockSpec((1, width), lambda i: (0, 0))],
        out_specs=pl.BlockSpec((ROWS, width), lambda i: (i, 0)),
    )(values, gain)


def row_kernel(kernel, parts, arrays, gain, outs):
    rows, width = parts.shape[1:]
    whole = pl.BlockSpec((4, ROWS, width), lambda i: (0, i, 0))
    single = pl.BlockSpec((ROWS, width), lambda i: (i, 0))
    return pl.pallas_call(
        kernel,
        grid=(rows // ROWS,),
        out_shape=[jax.ShapeDtypeStruct((rows, width), kind) for kind in outs],
        in_specs=[whole] + [single] * len(arrays) + [pl.BlockSpec((1, width), lambda i: (0, 0))],
        out_specs=[single] * len(outs),
    )(parts, *arrays, gain)


def add_parts(parts_ref):
    total = parts_ref[0].astype(F32)
    for i in range(1, 4):
        total = total + parts_ref[i].astype(F32)
    return total


def middle_rows(parts, inputs, gain):
    def kernel(parts_ref, inputs_ref, gain_ref, middle_ref, normal_ref):
        middle = inputs_ref[...].astype(F32) + add_parts(parts_ref)
        middle_ref[...] = middle
        normal_ref[...] = (norm_parts(middle)[0] * gain_ref[...]).astype(BF16)

    return row_kernel(kernel, parts, [inputs], gain, [F32, BF16])


def grad_middle_rows(parts, middle, cotangent, gain):
    def kernel(parts_ref, middle_ref, cotangent_ref, gain_ref, grad_ref, branch_ref):
        grad = cotangent_ref[...].astype(F32) + norm_backward(middle_ref[...], add_parts(parts_ref) * gain_ref[...])
        grad_ref[...] = grad
        branch_ref[...] = grad.astype(BF16)

    return row_kernel(kernel, parts, [middle, cotangent], gain, [F32, BF16])


def token_grad_rows(parts, inputs, grad_middle, gain):
    def kernel(parts_ref, inputs_ref, middle_ref, gain_ref, grad_ref):
        grad = norm_backward(inputs_ref[...].astype(F32), add_parts(parts_ref) * gain_ref[...])
        grad_ref[...] = (middle_ref[...] + grad).astype(BF16)

    return row_kernel(kernel, parts, [inputs, grad_middle], gain, [BF16])[0]


def feed_forward(normal, grad_activation, places, pieces, piece_rows):
    count, width = normal.shape
    hidden_width = pieces[0].shape[1]
    step_rows = 256
    steps = count // step_rows

    def kernel(places_ref, normal_ref, grad_activation_ref, *rest):
        act_ref, grad_ref, up_out, up_ref, sems, out_sem = rest[len(pieces) :]
        step = pl.program_id(0)
        copies = row_copies(places_ref, rest[: len(pieces)], up_ref, sems, piece_rows)
        back = pltpu.make_async_copy(up_ref, up_out, out_sem)

        @pl.when(step == 0)
        def _():
            for copy in copies:
                copy.start()
            for copy in copies:
                copy.wait()
            back.start()

        hidden = jnp.dot(normal_ref[...], up_ref[...], preferred_element_type=F32)
        scale = math.sqrt(2.0 / math.pi)
        square = hidden * hidden
        tanh = jnp.tanh(scale * hidden * (1.0 + 0.044715 * square))
        act_ref[...] = (0.5 * hidden * (1.0 + tanh)).astype(BF16)
        slope = 0.5 * (1.0 + tanh) + (0.5 * scale) * hidden * (1.0 - tanh * tanh) * (
            1.0 + (3.0 * 0.044715) * square
        )
        grad_ref[...] = (grad_activation_ref[...] * slope).astype(BF16)

        @pl.when(step == steps - 1)
        def _():
            back.wait()

    row_spec = pl.BlockSpec((step_rows, width), lambda i: (i, 0))
    hidden_spec = pl.BlockSpec((step_rows, hidden_width), lambda i: (i, 0))
    return pl.pallas_call(
        kernel,
        grid=(steps,),
        out_shape=[jax.ShapeDtypeStruct((count, hidden_width), BF16)] * 2
        + [jax.ShapeDtypeStruct((width, hidden_width), BF16)],
        in_specs=[SMEM, row_spec, hidden_spec] + [HBM] * len(pieces),
        out_specs=[hidden_spec, hidden_spec, HBM],
        scratch_shapes=[
            pltpu.VMEM((width, hidden_width), BF16),
            pltpu.SemaphoreType.DMA((width // piece_rows,)),
            pltpu.SemaphoreType.DMA,
        ],
        compiler_params=pltpu.CompilerParams(vmem_limit_bytes=48 << 20),
    )(places, normal, grad_activation, *pieces)


def contract_rows(left, right):
    return lax.dot_general(left, right, (((0,), (0,)), ((), ())), preferred_element_type=F32)


def dot_transposed(left, right):
    return lax.dot_general(left, right, (((1,), (1,)), ((), ())), preferred_element_type=F32)


class Step:
    def __init__(self, function, *needs):
        self.function, self.needs, self.made = function, needs, None

    def get(self):
        if self.made is None:
            self.put(self.function(*[need.get() for need in self.needs]))
        return self.made[0]

    def put(self, value):
        self.made = (value,)


def grouped_body(
    tokens_own,
    triple_weight,
    output_weight,
    up_weight,
    down_weight,
    first_gain,
    second_gain,
    cotangent_own,
    frame_counts,
    text_counts,
    action_counts,
):
    rows, width = tokens_own.shape
    count = rows * MEMBERS
    dp, fsdp = lax.axis_index("dp"), lax.axis_index("fsdp")
    x, core = dp >> 1, dp & 1
    zh = fsdp >> 2

    counts = jnp.concatenate(
        [frame_counts.reshape(-1), text_counts.reshape(-1), action_counts.reshape(-1)]
    )
    counts = jnp.where(core == zh, counts, swap(counts, CORE))
    frames = counts[:2]
    slots = text_counts.shape[-1]
    texts = counts[2 : 2 + 2 * slots].reshape(2, slots)
    actions = counts[2 + 2 * slots :].reshape(2, slots)
    live = jnp.arange(slots, dtype=jnp.int32) < frames[:, None]
    lengths = jnp.sum(jnp.where(live, IMG + texts + actions, 0), axis=-1)
    first_end = lengths[0]
    second_end = lengths[0] + lengths[1]
    pack_ends = jnp.stack([first_end, second_end]).astype(jnp.int32)
    places = jnp.arange(count, dtype=jnp.int32)
    starts = jnp.where(places < first_end, 0, jnp.where(places < second_end, first_end, second_end))
    cosine_table, sine_table = rotary_tables(places - starts)
    cosine_table = jnp.concatenate([cosine_table[:, 0], cosine_table[:, 0]], axis=1)
    sine_table = jnp.concatenate([-sine_table[:, 0], sine_table[:, 0]], axis=1)

    sides = ((0, 0), (0, 1), (1, 0), (1, 1))
    rows_of_weight = triple_weight.shape[0]
    block = rows_of_weight * 4
    quarter = down_weight.shape[0] // 4
    hidden_width = up_weight.shape[1] // DEVICES
    triple_columns = lambda m: head_columns(m, width)
    up_columns = lambda m: hidden_columns(m, hidden_width)
    first_column = first_gain.astype(F32)[:, None]
    second_column = second_gain.astype(F32)[:, None]

    def places_of(pieces):
        return jnp.stack([place for a, b, parts in pieces for place in parts(x ^ a, zh ^ b)]).astype(jnp.int32)

    def column_places(*which):
        return lambda sx, sz: [sx * 4 + c * 2 + sz for c in which]

    def down_places(*which):
        return lambda sx, sz: [(sx * 2 + sz) * 4 + q for q in which]

    tokens, cotangent = Step(lambda: tokens_own), Step(lambda: cotangent_own)
    down_own, output_own = Step(lambda: down_weight), Step(lambda: output_weight)
    ends, cosine, sine = Step(lambda: pack_ends), Step(lambda: cosine_table), Step(lambda: sine_table)

    triple_dealt = Step(lambda: deal_columns(triple_weight, triple_columns, [first_gain[None], second_gain[None]]))
    triple_all = Step(lambda a: exchange(a, CORE, ZL, Y), triple_dealt)
    triple_own = Step(lambda a: a[:, :rows_of_weight].reshape(-1, a.shape[-1]), triple_all)
    triple_x = Step(lambda a: swap(a, X), triple_own)
    triple_half = [Step(lambda a, h=h: a[h * block : (h + 1) * block], triple_own) for h in range(2)]
    triple_zh = [Step(lambda a: swap(a, ZH), half) for half in triple_half]
    triple_xz = [Step(lambda a: swap(a, X), half) for half in triple_zh]
    inputs = Step(regroup, tokens)
    all_inputs = Step(lambda a: gather(a, CORE, ZL, Y), inputs)
    gains_own = Step(
        lambda a: jnp.concatenate(
            [a[:, rows_of_weight, i * HEAD : i * HEAD + rows_of_weight] for i in range(2)], axis=1
        ),
        triple_all,
    )
    gains_pair = Step(lambda a: pair_up(zh, a, swap(a, ZH)), gains_own)

    def whole_gains(pair):
        whole = pair_up(x, pair, swap(pair, X)).reshape(2, 2, 2, 4, 2, -1)
        return whole.transpose(4, 0, 2, 1, 3, 5).reshape(2, -1).astype(F32)

    gains = Step(whole_gains, gains_pair)
    normal = Step(lambda a, gains: norm_of(a, gains[:1]), all_inputs, gains)
    own_cotangent = Step(regroup, cotangent)
    all_cotangent = Step(lambda a: gather(a, CORE, ZL, Y), own_cotangent)
    turned = Step(lambda a: lax.ppermute(a, AXES, turn_pairs()), output_own)
    turned_zh = Step(lambda a: swap(a, ZH), turned)
    turned_pair = Step(lambda a, b: pair_up(zh, a, b), turned, turned_zh)
    turned_x = Step(lambda a: swap(a, X), turned_pair)

    def whole_output(pair, pair_x):
        whole = jnp.where(x == 0, jnp.stack([pair, pair_x], axis=1), jnp.stack([pair_x, pair], axis=1))
        return whole.reshape(-1, width)

    output = Step(whole_output, turned_pair, turned_x)
    down_x = Step(lambda a: swap(a, X), down_own)
    down_part = [Step(lambda a, q=q: a[q * quarter : (q + 1) * quarter], down_own) for q in range(4)]
    down_zh = [Step(lambda a: swap(a, ZH), part) for part in down_part]
    down_xz = [Step(lambda a: swap(a, X), part) for part in down_zh]

    def whole_down(own, own_x, *rest):
        places = [(0, 0, down_places(0, 1, 2, 3)), (1, 0, down_places(0, 1, 2, 3))]
        places += [(0, 1, down_places(q)) for q in range(4)] + [(1, 1, down_places(q)) for q in range(4)]
        return place_rows(places_of(places), [own, own_x, *rest], quarter)

    down = Step(whole_down, down_own, down_x, *down_zh, *down_xz)
    grad_activation = Step(dot_transposed, all_cotangent, down)
    up_dealt = Step(lambda: deal_columns(up_weight, up_columns))
    up_own = Step(lambda a: exchange(a, CORE, ZL, Y).reshape(-1, a.shape[-1]), up_dealt)
    up_x = Step(lambda a: swap(a, X), up_own)
    up_half = [Step(lambda a, h=h: a[h * block : (h + 1) * block], up_own) for h in range(2)]
    up_zh = [Step(lambda a: swap(a, ZH), half) for half in up_half]
    up_xz = [Step(lambda a: swap(a, X), half) for half in up_zh]

    halved = [(0, 0, column_places(0, 1)), (0, 1, column_places(0)), (0, 1, column_places(1))]
    halved += [(1, 0, column_places(0, 1)), (1, 1, column_places(0)), (1, 1, column_places(1))]

    def attend(ends, normal, cosine, sine, *pieces):
        return attention_forward(ends, places_of(halved), normal, list(pieces), cosine, sine)

    attention = Step(attend, ends, normal, cosine, sine, triple_own, *triple_zh, triple_x, *triple_xz)
    attended_partial = Step(lambda a, output: product_sums(core, a[3], output), attention, output)
    attended_sums = Step(collect, attended_partial)
    middle = Step(lambda a, inputs, gains: middle_rows(a, inputs, gains[1:]), attended_sums, inputs, gains)
    normal_two = Step(lambda a: gather(a[1], CORE, ZL, Y), middle)

    def feed(normal_two, grad_activation, *pieces):
        return feed_forward(normal_two, grad_activation, places_of(halved), list(pieces), block)

    forward = Step(feed, normal_two, grad_activation, up_own, *up_zh, up_x, *up_xz)

    def columns(left, right, start, stop, shape):
        return contract_rows(left, right[:, start:stop]).astype(BF16).reshape(*shape, -1, stop - start)

    class Reduction:
        def __init__(self, kept, one, two, sent=None, index=None):
            (side, bits), (other, other_bits) = one, two
            index = side if index is None else index
            self.kept = kept
            self.sent = sent or Step(lambda a: lax.dynamic_index_in_dim(a, 1 - side, 0, False), kept)
            self.came = Step(lambda a: swap(a, bits), self.sent)
            self.half = Step(lambda a, came: half_sum(index, 1 - other, a, came).astype(BF16), kept, self.came)
            self.far = Step(lambda a: swap(a, other_bits), self.half)
            self.total = Step(lambda a, came, far: keep_sum(index, other, a, came, far), kept, self.came, self.far)

    over_x, over_zh = (x, X), (zh, ZH)

    def x_first(left, right, pick, start, lanes, shape):
        def side(index):
            def product(a, b):
                whole, columns_of = pick(a, b)
                half = whole.shape[1] // 2
                own = lax.dynamic_slice_in_dim(whole, index * half, half, 1)
                return columns(own, columns_of, start * HEAD, (start + lanes) * HEAD, (1,) + shape)

            return product

        sent = Step(lambda a, b: side(1 - x)(a, b)[0], left, right)
        return Reduction(Step(side(x), left, right), over_x, over_zh, sent, 0)

    def zh_first(left, right, pick, start, lanes, shape):
        def product(a, b):
            return columns(*pick(a, b), start * HEAD, (start + lanes) * HEAD, (2,) + shape).swapaxes(0, 2)

        return Reduction(Step(product, left, right), over_zh, over_x)

    def slabs(parts):
        parts = [part.astype(BF16).reshape(MEMBERS, -1, part.shape[-1]) for part in parts]
        return exchange(jnp.concatenate(parts, axis=2), CORE, ZL, Y)

    hidden_partial = Step(lambda a: product_sums(core, a[1], a[2], True), forward)
    hidden_sums = Step(collect, hidden_partial)
    down_pick, down_shape = lambda a, b: (a[0], b), (1, 2)
    grad_down = [
        x_first(forward, all_cotangent, down_pick, 0, 12, down_shape),
        zh_first(forward, all_cotangent, down_pick, 12, 4, down_shape),
    ]
    down_out = Step(
        lambda *parts: jnp.concatenate([part[0] for part in parts], axis=1), *[part.total for part in grad_down]
    )
    up_pick, up_shape = lambda a, b: (a, b[1]), (2, 2)
    grad_up = [x_first(normal_two, forward, up_pick, start, 4, up_shape) for start in (0, 4)]
    up_slabs = Step(lambda *parts: slabs(parts), *[part.total for part in grad_up])
    up_out = Step(lambda a: place_columns([a], up_weight, second_column, up_columns), up_slabs)
    layer_partial = Step(lambda a, down: product_sums(core, a[0], down), forward, down)
    layer_sums = Step(collect, layer_partial)
    layer_rows = Step(
        lambda a, middle: (middle[0] + jnp.sum(a.astype(F32), axis=0)).astype(BF16), layer_sums, middle
    )
    layer_output = Step(regroup, layer_rows)
    grad_middle = Step(
        lambda a, middle, cot, gains: grad_middle_rows(a, middle[0], cot, gains[1:]),
        hidden_sums,
        middle,
        own_cotangent,
        gains,
    )
    grad_branch = Step(lambda a: gather(a[1], CORE, ZL, Y), grad_middle)
    grad_attended = Step(lambda a, output: dot_transposed(a, output).astype(BF16), grad_branch, output)
    grad_mixed = Step(
        lambda ends, a, grad, cosine, sine: attention_backward_heads(ends, a[0], a[1], a[2], grad, cosine, sine),
        ends,
        attention,
        grad_attended,
        cosine,
        sine,
    )
    output_term = Reduction(
        Step(
            lambda a, b: contract_rows(a[3], b).astype(BF16).reshape(2, 2, -1, width).swapaxes(0, 1)[:, None],
            attention,
            grad_branch,
        ),
        over_x,
        over_zh,
    )
    output_grad = Step(
        lambda a: lax.ppermute(a[0].astype(BF16), AXES, turn_pairs()).astype(F32), output_term.total
    )
    mixed_partial = Step(lambda a, b: product_sums(core, a, b[4], True), grad_mixed, attention)
    mixed_sums = Step(collect, mixed_partial)
    token_rows = Step(
        lambda a, inputs, middle, gains: token_grad_rows(a, inputs, middle[0], gains[:1]),
        mixed_sums,
        inputs,
        grad_middle,
        gains,
    )
    token_grad = Step(regroup, token_rows)
    grad_triple = [x_first(normal, grad_mixed, lambda a, b: (a, b), 0, 6, (2, 2))]
    triple_slabs = Step(lambda *parts: slabs(parts), *[part.total for part in grad_triple])
    triple_out = Step(lambda a: place_columns([a], triple_weight, first_column, triple_columns), triple_slabs)

    windows = [
        (
            [
                triple_own, triple_half[0], triple_half[1], gains_own, inputs, own_cotangent, down_x, turned,
                ends, down_part[0], down_part[1], down_part[2], down_part[3], up_dealt,
            ],
            [],
        ),
        (
            [all_inputs, triple_zh[0], triple_zh[1], triple_x, gains_pair, gains, cosine, sine],
            [down_part[0], turned],
        ),
        (
            [triple_xz[0], triple_xz[1], turned_zh, turned_pair, down_zh[0], normal],
            [
                cosine, down_part[1], down_part[2], ends, sine, triple_own, triple_x, triple_zh[0],
                triple_zh[1], up_dealt,
            ],
        ),
        (
            [up_own, up_half[0], up_half[1], turned_x, output, down_zh[1], down_zh[2], down_xz[0], attention],
            [down_part[3], own_cotangent],
        ),
        (
            [
                attended_partial, attended_sums, up_zh[0], up_x, down_zh[3], down_xz[1], down_xz[2],
                all_cotangent,
            ],
            [down_own, down_x, down_xz[0], down_zh[0], down_zh[1], down_zh[2], gains, inputs, up_half[1]],
        ),
        (
            [middle, normal_two, up_zh[1], up_xz[0], down_xz[3], up_xz[1], down, grad_activation],
            [up_own, up_x, up_zh[0]],
        ),
        (
            [forward],
            [all_cotangent],
        ),
        (
            [hidden_partial, grad_down[0].sent],
            [all_cotangent, forward, normal_two],
        ),
        (
            [
                hidden_sums, grad_down[1].kept, grad_down[0].came, grad_down[1].came, grad_up[0].sent,
                grad_down[0].kept,
            ],
            [down, forward, gains, middle, normal_two, own_cotangent],
        ),
        (
            [
                grad_middle, grad_branch, grad_up[0].came, grad_down[1].far, grad_down[0].far, grad_up[1].sent,
                grad_up[1].kept, layer_partial, grad_up[0].kept,
            ],
            [attention, cosine, ends, normal, output, sine],
        ),
        (
            [
                layer_sums, grad_up[1].came, grad_up[0].far, grad_attended, grad_mixed, mixed_partial,
                grad_triple[0].sent,
            ],
            [attention, grad_branch, normal],
        ),
        (
            [
                mixed_sums, grad_triple[0].came, grad_up[1].far, layer_output, grad_triple[0].kept,
                output_term.kept,
            ],
            [gains, grad_middle, inputs],
        ),
        (
            [grad_triple[0].far, output_term.came, token_rows, up_slabs],
            [],
        ),
    ]
    for made, held in windows:
        values = together(*[step.get() for step in made + held])
        for step, value in zip(made + held, values):
            step.put(value)
    return (
        layer_output.get(),
        token_grad.get(),
        triple_out.get()[0],
        output_grad.get(),
        up_out.get()[0],
        down_out.get(),
        triple_out.get()[1][:, 0],
        up_out.get()[1][:, 0],
    )


def solution(mesh):
    grouped = mesh.shape["dp"] * 2 == mesh.shape["fsdp"] == MEMBERS
    rows = P(AXES, None)
    return jax.shard_map(
        grouped_body if grouped else whole_rows_body,
        mesh=mesh,
        in_specs=(rows,) * 5 + (P(AXES),) * 2 + (rows, P("dp", None), P("dp", None, None), P("dp", None, None)),
        out_specs=(rows,) * 6 + (P(AXES),) * 2,
        check_vma=False,
    )
```

```python
import math

import jax
import jax.numpy as jnp
from jax import lax
from jax.experimental import pallas as pl
from jax.experimental.pallas import tpu as pltpu
from jax.sharding import PartitionSpec as P

HEADS = 16
HEAD = 128
IMG = 576


EPSILON = 1e-05
MASKED = -1e30


def clip_layout(frame_counts, text_counts, action_counts, pack_length):
    frame_slot = jnp.arange(text_counts.shape[-1], dtype=jnp.int32)
    frame_live = frame_slot < frame_counts[..., None]
    frame_sizes = jnp.where(frame_live, IMG + text_counts + action_counts, 0)
    clip_lengths = jnp.sum(frame_sizes, axis=-1)
    first_end = clip_lengths[..., 0:1]
    second_end = first_end + clip_lengths[..., 1:2]
    places = jnp.arange(pack_length, dtype=jnp.int32)
    segment = (places >= first_end).astype(jnp.int32) + (places >= second_end).astype(jnp.int32)
    starts = jnp.where(segment == 0, 0, jnp.where(segment == 1, first_end, second_end))
    return (segment, places - starts)


def rotary_tables(position):
    half_width = HEAD // 2
    frequency = jnp.exp(
        jnp.arange(half_width, dtype=jnp.float32) * (-2.0 * math.log(10000.0) / HEAD)
    )
    angles = position.astype(jnp.float32)[:, None] * frequency[None, :]
    return (jnp.cos(angles)[:, None, :], jnp.sin(angles)[:, None, :])


def rotate(vectors, cosine, sine_table):
    half_width = vectors.shape[-1] // 2
    former = vectors[..., :half_width]
    latter = vectors[..., half_width:]
    return jnp.concatenate(
        [former * cosine - latter * sine_table, latter * cosine + former * sine_table], axis=-1
    )


def unrotate(gradient, cosine, sine_table):
    half_width = gradient.shape[-1] // 2
    former = gradient[..., :half_width]
    latter = gradient[..., half_width:]
    return jnp.concatenate(
        [former * cosine + latter * sine_table, latter * cosine - former * sine_table], axis=-1
    )


def norm_rows(values, gain_vector):
    centred = values - jnp.mean(values, axis=-1, keepdims=True)
    variance = jnp.mean(centred * centred, axis=-1, keepdims=True)
    return centred * lax.rsqrt(variance + EPSILON) * gain_vector


def block_allowed(query_segment, query_places, key_segment, key_place):
    return (query_segment[:, None] == key_segment[None, :]) & (
        key_place[None, :] <= query_places[:, None]
    )


def block_scores(queries, key_block, allowed):
    scores = jnp.einsum(
        "qhd,khd->hqk", queries, key_block, preferred_element_type=jnp.float32
    ) * HEAD ** (-0.5)
    return jnp.where(allowed[None], scores, MASKED)


def block_probs(queries, key_block, allowed, row_max, row_sum):
    scores = block_scores(queries, key_block, allowed)
    return jnp.where(allowed[None], jnp.exp(scores - row_max[..., None]) / row_sum[..., None], 0.0)


def softmax_stats(queries, key_blocks, layout_parts):
    query_segment, query_places, key_segments, key_places = layout_parts
    row_count, head_count = (queries.shape[0], queries.shape[1])
    start_state = (
        jnp.full((head_count, row_count), MASKED, jnp.float32),
        jnp.zeros((head_count, row_count), jnp.float32),
    )

    def advance(state, block_inputs):
        key_block, key_segment, key_place = block_inputs
        allowed = block_allowed(query_segment, query_places, key_segment, key_place)

        def update(current):
            row_max, row_sum = current
            scores = block_scores(queries, key_block, allowed)
            new_max = jnp.maximum(row_max, jnp.max(scores, axis=-1))
            weights = jnp.where(allowed[None], jnp.exp(scores - new_max[..., None]), 0.0)
            return (new_max, row_sum * jnp.exp(row_max - new_max) + jnp.sum(weights, axis=-1))

        return (lax.cond(jnp.any(allowed), update, lambda current: current, state), None)

    final_state, unused = lax.scan(advance, start_state, (key_blocks, key_segments, key_places))
    return final_state


def attention_output(queries, key_blocks, value_blocks, layout_parts, row_max, row_sum):
    query_segment, query_places, key_segments, key_places = layout_parts

    def advance(accum, block_inputs):
        key_block, value_block, key_segment, key_place = block_inputs
        allowed = block_allowed(query_segment, query_places, key_segment, key_place)

        def update(current):
            probs = block_probs(queries, key_block, allowed, row_max, row_sum).astype(jnp.bfloat16)
            return current + jnp.einsum(
                "hqk,khd->qhd", probs, value_block, preferred_element_type=jnp.float32
            )

        return (lax.cond(jnp.any(allowed), update, lambda current: current, accum), None)

    attended, unused = lax.scan(
        advance,
        jnp.zeros(queries.shape, jnp.float32),
        (key_blocks, value_blocks, key_segments, key_places),
    )
    return attended


def attention_backward(
    queries, grad_attended, delta_rows, key_blocks, value_blocks, layout_parts, row_max, row_sum
):
    query_segment, query_places, key_segments, key_places = layout_parts
    score_scale = HEAD ** (-0.5)

    def advance(grad_query, block_inputs):
        key_block, value_block, key_segment, key_place = block_inputs
        allowed = block_allowed(query_segment, query_places, key_segment, key_place)

        def update(current):
            probs = block_probs(queries, key_block, allowed, row_max, row_sum)
            grad_probs = jnp.einsum(
                "qhd,khd->hqk", grad_attended, value_block, preferred_element_type=jnp.float32
            )
            grad_scores = (probs * (grad_probs - delta_rows[..., None])).astype(jnp.bfloat16)
            new_query = (
                current
                + jnp.einsum(
                    "hqk,khd->qhd", grad_scores, key_block, preferred_element_type=jnp.float32
                )
                * score_scale
            )
            return (new_query, ())

        def bypass(current):
            return (current, ())

        return lax.cond(jnp.any(allowed), update, bypass, grad_query)

    grad_query, terms = lax.scan(
        advance,
        jnp.zeros(queries.shape, jnp.float32),
        (key_blocks, value_blocks, key_segments, key_places),
    )
    return (grad_query, None, None)


def project_front(inputs, triple_full, gain_full, cosine, sine_table):
    row_count, width = inputs.shape
    normed = norm_rows(inputs, gain_full.astype(jnp.float32)).astype(jnp.bfloat16)
    mixed = jnp.dot(normed, triple_full, preferred_element_type=jnp.float32)
    queries = rotate(mixed[:, :width].reshape(row_count, HEADS, HEAD), cosine, sine_table).astype(
        jnp.bfloat16
    )
    keys_local = (
        rotate(mixed[:, width : 2 * width].reshape(row_count, HEADS, HEAD), cosine, sine_table)
        .astype(jnp.bfloat16)
        .reshape(row_count, width)
    )
    values_local = mixed[:, 2 * width :].astype(jnp.bfloat16)
    return (normed, queries, keys_local, values_local)


def run_attention(queries, gathered, layout_parts):
    block_count = layout_parts[2].shape[0]
    key_blocks = gathered[0].reshape(block_count, -1, HEADS, HEAD)
    value_blocks = gathered[1].reshape(block_count, -1, HEADS, HEAD)
    row_max, row_sum = softmax_stats(queries, key_blocks, layout_parts)
    attended = attention_output(queries, key_blocks, value_blocks, layout_parts, row_max, row_sum)
    return (attended, key_blocks, value_blocks, row_max, row_sum)


def finish_layer(inputs, attended, output_full, up_full, down_full, second_full):
    row_count, width = inputs.shape
    attended_low = attended.reshape(row_count, width).astype(jnp.bfloat16)
    middle = inputs + jnp.dot(attended_low, output_full, preferred_element_type=jnp.float32)
    normed_two = norm_rows(middle, second_full.astype(jnp.float32)).astype(jnp.bfloat16)
    hidden = jnp.dot(normed_two, up_full, preferred_element_type=jnp.float32)
    activation = jax.nn.gelu(hidden).astype(jnp.bfloat16)
    result = middle + jnp.dot(activation, down_full, preferred_element_type=jnp.float32)
    return (result, attended_low, middle, normed_two, hidden, activation)


def whole_rows_body(
    tokens,
    triple_weight,
    output_weight,
    up_weight,
    down_weight,
    first_gain,
    second_gain,
    cotangent,
    frame_counts,
    text_counts,
    action_counts,
):
    row_count, width = tokens.shape
    pack_length = row_count * lax.axis_size("fsdp")
    first_place = lax.axis_index("fsdp") * row_count
    segment, position = clip_layout(frame_counts[0], text_counts[0], action_counts[0], pack_length)
    block_rows = min(1024, pack_length)
    block_count = pack_length // block_rows
    query_places = first_place + jnp.arange(row_count, dtype=jnp.int32)
    own_segment = lax.dynamic_slice_in_dim(segment, first_place, row_count, 0)
    layout_parts = (
        own_segment,
        query_places,
        segment.reshape(block_count, block_rows),
        jnp.arange(pack_length, dtype=jnp.int32).reshape(block_count, block_rows),
    )
    cosine, sine_table = rotary_tables(
        lax.dynamic_slice_in_dim(position, first_place, row_count, 0)
    )
    inputs = tokens.astype(jnp.float32)
    attention_set = (
        lax.all_gather(triple_weight, ("dp", "fsdp"), axis=0, tiled=True),
        lax.all_gather(output_weight, ("dp", "fsdp"), axis=0, tiled=True),
        lax.all_gather(first_gain, ("dp", "fsdp"), axis=0, tiled=True),
    )
    normed, queries, keys_local, values_local = project_front(
        inputs, attention_set[0], attention_set[2], cosine, sine_table
    )
    gathered = (
        lax.all_gather(keys_local, "fsdp", axis=0, tiled=True),
        lax.all_gather(values_local, "fsdp", axis=0, tiled=True),
    )
    attended, key_blocks, value_blocks, row_max, row_sum = run_attention(
        queries, gathered, layout_parts
    )
    feedforward_set = (
        lax.all_gather(up_weight, ("dp", "fsdp"), axis=0, tiled=True),
        lax.all_gather(down_weight, ("dp", "fsdp"), axis=0, tiled=True),
        lax.all_gather(second_gain, ("dp", "fsdp"), axis=0, tiled=True),
    )
    kept_parts = finish_layer(
        inputs,
        attended,
        attention_set[1],
        feedforward_set[0],
        feedforward_set[1],
        feedforward_set[2],
    )
    layer_output = kept_parts[0].astype(jnp.bfloat16)
    attention_set = (
        lax.all_gather(triple_weight, ("dp", "fsdp"), axis=0, tiled=True),
        lax.all_gather(output_weight, ("dp", "fsdp"), axis=0, tiled=True),
        lax.all_gather(first_gain, ("dp", "fsdp"), axis=0, tiled=True),
    )
    normed, queries, keys_local, values_local = project_front(
        inputs, attention_set[0], attention_set[2], cosine, sine_table
    )
    gathered = (
        lax.all_gather(keys_local, "fsdp", axis=0, tiled=True),
        lax.all_gather(values_local, "fsdp", axis=0, tiled=True),
    )
    attended, key_blocks, value_blocks, row_max, row_sum = run_attention(
        queries, gathered, layout_parts
    )
    feedforward_set = (
        lax.all_gather(up_weight, ("dp", "fsdp"), axis=0, tiled=True),
        lax.all_gather(down_weight, ("dp", "fsdp"), axis=0, tiled=True),
        lax.all_gather(second_gain, ("dp", "fsdp"), axis=0, tiled=True),
    )
    kept_parts = finish_layer(
        inputs,
        attended,
        attention_set[1],
        feedforward_set[0],
        feedforward_set[1],
        feedforward_set[2],
    )
    unused_result, attended_low, middle, normed_two, hidden, activation = kept_parts
    down_term = jnp.einsum("rf,rd->fd", activation, cotangent, preferred_element_type=jnp.float32)
    grad_activation = jnp.einsum(
        "rd,fd->rf", cotangent, feedforward_set[1], preferred_element_type=jnp.float32
    )
    unused_gelu, gelu_pull = jax.vjp(jax.nn.gelu, hidden)
    grad_hidden = gelu_pull(grad_activation)[0].astype(jnp.bfloat16)
    up_term = jnp.einsum("rd,rf->df", normed_two, grad_hidden, preferred_element_type=jnp.float32)
    grad_normed_two = jnp.einsum(
        "rf,df->rd", grad_hidden, feedforward_set[0], preferred_element_type=jnp.float32
    )
    unused_second, second_pull = jax.vjp(norm_rows, middle, feedforward_set[2].astype(jnp.float32))
    grad_middle_norm, second_gain_term = second_pull(grad_normed_two)
    grad_middle = cotangent.astype(jnp.float32) + grad_middle_norm
    feedforward_sums = (
        lax.psum_scatter(up_term, ("dp", "fsdp"), scatter_dimension=0, tiled=True),
        lax.psum_scatter(down_term, ("dp", "fsdp"), scatter_dimension=0, tiled=True),
        lax.psum_scatter(second_gain_term, ("dp", "fsdp"), scatter_dimension=0, tiled=True),
    )
    grad_branch = grad_middle.astype(jnp.bfloat16)
    output_term = jnp.einsum(
        "rd,re->de", attended_low, grad_branch, preferred_element_type=jnp.float32
    )
    grad_attended = (
        jnp.einsum("re,de->rd", grad_branch, attention_set[1], preferred_element_type=jnp.float32)
        .astype(jnp.bfloat16)
        .reshape(row_count, HEADS, HEAD)
    )
    delta_rows = jnp.sum(grad_attended.astype(jnp.float32) * attended, axis=-1).T
    score_scale = HEAD ** (-0.5)
    grad_query = attention_backward(
        queries, grad_attended, delta_rows, key_blocks, value_blocks, layout_parts, row_max, row_sum
    )[0]
    pack_stats = (
        lax.all_gather(row_max.T, "fsdp", axis=0, tiled=True),
        lax.all_gather(row_sum.T, "fsdp", axis=0, tiled=True),
        lax.all_gather(delta_rows.T, "fsdp", axis=0, tiled=True),
    )
    own_keys = keys_local.reshape(row_count, HEADS, HEAD)
    own_values = values_local.reshape(row_count, HEADS, HEAD)
    empty_grads = jnp.zeros((row_count, HEADS, HEAD), jnp.float32)
    query_piece = lax.all_gather(queries, "fsdp", axis=0, tiled=True)
    grad_piece = lax.all_gather(grad_attended, "fsdp", axis=0, tiled=True)
    piece_rows = query_piece.shape[0]
    block_size = min(1024, piece_rows)
    block_total = piece_rows // block_size

    def advance(current, block_index):
        offset = block_index * block_size
        query_part = lax.dynamic_slice_in_dim(query_piece, offset, block_size, 0)
        grad_part = lax.dynamic_slice_in_dim(grad_piece, offset, block_size, 0)
        max_part = lax.dynamic_slice_in_dim(pack_stats[0], offset, block_size, 0).T
        sum_part = lax.dynamic_slice_in_dim(pack_stats[1], offset, block_size, 0).T
        delta_part = lax.dynamic_slice_in_dim(pack_stats[2], offset, block_size, 0).T
        part_segment = lax.dynamic_slice_in_dim(segment, offset, block_size, 0)
        part_places = offset + jnp.arange(block_size, dtype=jnp.int32)
        allowed = block_allowed(part_segment, part_places, own_segment, query_places)

        def update(pair):
            probs = block_probs(query_part, own_keys, allowed, max_part, sum_part)
            grad_probs = jnp.einsum(
                "qhd,khd->hqk", grad_part, own_values, preferred_element_type=jnp.float32
            )
            grad_scores = (probs * (grad_probs - delta_part[..., None])).astype(jnp.bfloat16)
            grad_key = (
                pair[0]
                + jnp.einsum(
                    "hqk,qhd->khd", grad_scores, query_part, preferred_element_type=jnp.float32
                )
                * score_scale
            )
            grad_value = pair[1] + jnp.einsum(
                "hqk,qhd->khd",
                probs.astype(jnp.bfloat16),
                grad_part,
                preferred_element_type=jnp.float32,
            )
            return (grad_key, grad_value)

        return (lax.cond(jnp.any(allowed), update, lambda pair: pair, current), None)

    result, unused = lax.scan(
        advance, (empty_grads, empty_grads), jnp.arange(block_total, dtype=jnp.int32)
    )
    key_grad_sum = result[0].reshape(row_count, width)
    value_grad_sum = result[1].reshape(row_count, width)
    grad_query_full = (
        unrotate(grad_query, cosine, sine_table).reshape(row_count, width).astype(jnp.bfloat16)
    )
    grad_key_full = (
        unrotate(key_grad_sum.reshape(row_count, HEADS, HEAD), cosine, sine_table)
        .reshape(row_count, width)
        .astype(jnp.bfloat16)
    )
    grad_value_full = value_grad_sum.astype(jnp.bfloat16)
    grad_mixed = jnp.concatenate([grad_query_full, grad_key_full, grad_value_full], axis=1)
    triple_term = jnp.einsum("rd,re->de", normed, grad_mixed, preferred_element_type=jnp.float32)
    grad_normed = jnp.einsum(
        "re,de->rd", grad_mixed, attention_set[0], preferred_element_type=jnp.float32
    )
    unused_first, first_pull = jax.vjp(norm_rows, inputs, attention_set[2].astype(jnp.float32))
    grad_input_norm, first_gain_term = first_pull(grad_normed)
    token_grad = (grad_middle + grad_input_norm).astype(jnp.bfloat16)
    attention_sums = (
        lax.psum_scatter(triple_term, ("dp", "fsdp"), scatter_dimension=0, tiled=True),
        lax.psum_scatter(output_term, ("dp", "fsdp"), scatter_dimension=0, tiled=True),
        lax.psum_scatter(first_gain_term, ("dp", "fsdp"), scatter_dimension=0, tiled=True),
    )
    return (
        layer_output,
        token_grad,
        attention_sums[0],
        attention_sums[1],
        feedforward_sums[0],
        feedforward_sums[1],
        attention_sums[2],
        feedforward_sums[2],
    )


AXES = ("dp", "fsdp")
DEVICES = 32
MEMBERS = 8
CORE, ZL, Y = 8, 2, 1
X, ZH = 16, 4
BF16 = jnp.bfloat16
F32 = jnp.float32
SMEM = pl.BlockSpec(memory_space=pltpu.SMEM)
VMEM = pl.BlockSpec(memory_space=pltpu.VMEM)
HBM = pl.BlockSpec(memory_space=pltpu.HBM)


def swap(array, bits):
    return lax.ppermute(array, AXES, [(i, i ^ bits) for i in range(DEVICES)])


def alike(*bits):
    groups = {}
    for i in range(DEVICES):
        groups.setdefault(i & ~sum(bits), []).append(i)
    return list(groups.values())


def exchange(array, *bits):
    return lax.all_to_all(array, AXES, 0, 0, tiled=True, axis_index_groups=alike(*bits))


def after(array, *others):
    return lax.optimization_barrier((array,) + others)[0]


def together(*arrays):
    return lax.optimization_barrier(arrays)


def regroup_pairs():
    def target(i):
        x, core, zh, low = i >> 4, (i >> 3) & 1, (i >> 2) & 1, i & 3
        return (x << 4) | (zh << 3) | (core << 2) | low

    return [(i, target(i)) for i in range(DEVICES)]


def regroup(array):
    return lax.ppermute(array, AXES, regroup_pairs())


def turn_pairs():
    return [(i, (i & 14) | (i & 1) << 4 | i >> 4) for i in range(DEVICES)]


def gather(own, *bits):
    return lax.all_gather(own, AXES, axis=0, tiled=True, axis_index_groups=alike(*bits))


def collect(parts):
    return exchange(parts.reshape(4, -1, parts.shape[1]), ZL, Y)


def row_product(half, left, right, transposed, came=None):
    count, depth = left.shape[0] // 2, left.shape[1]
    width = right.shape[0] if transposed else right.shape[1]
    tile = 512

    def kernel(half_ref, left_ref, right_ref, *rest):
        if transposed:
            total = dot_transposed(left_ref[...], right_ref[...])
        else:
            total = jnp.dot(left_ref[...], right_ref[...], preferred_element_type=F32)
        if came is not None:
            total = total + rest[0][...].astype(F32)
        rest[-1][...] = total.astype(BF16)

    columns = pl.BlockSpec((count, tile), lambda i, half_ref: (0, i))
    if transposed:
        right_spec = pl.BlockSpec((tile, depth), lambda i, half_ref: (i, 0))
    else:
        right_spec = pl.BlockSpec((depth, tile), lambda i, half_ref: (0, i))
    more = [] if came is None else [came]
    return pl.pallas_call(
        kernel,
        grid_spec=pltpu.PrefetchScalarGridSpec(
            num_scalar_prefetch=1,
            grid=(width // tile,),
            in_specs=[pl.BlockSpec((count, depth), lambda i, half_ref: (half_ref[0], 0)), right_spec]
            + [columns] * len(more),
            out_specs=columns,
        ),
        out_shape=jax.ShapeDtypeStruct((count, width), BF16),
        compiler_params=pltpu.CompilerParams(vmem_limit_bytes=32 << 20),
    )(half, left, right, *more)


def product_sums(core, rows, right, transposed=False):
    near, far = core.reshape(1), (1 - core).reshape(1)
    came = swap(row_product(far, rows, right, transposed), CORE)
    return row_product(near, rows, right, transposed, came)


def hidden_columns(member, width):
    core, zl, y = (member >> 2) & 1, (member >> 1) & 1, member & 1
    return [
        ((gx * X + core * CORE + gz * ZH + zl * ZL + y) * width, width)
        for gx in range(2)
        for gz in range(2)
    ]


def head_columns(member, width):
    core, zl, y = (member >> 2) & 1, (member >> 1) & 1, member & 1
    return [
        (part * width + ((y * 2 + core) * 4 + half * 2 + zl) * HEAD, HEAD)
        for part in range(3)
        for half in range(2)
    ]


def deal_columns(own, columns, extra=()):
    rows = own.shape[0]
    width = own.shape[1] // MEMBERS
    more = 16 if extra else 0

    def kernel(*refs):
        own_ref, slabs_ref = refs[0], refs[-1]
        for member in range(MEMBERS):
            start = 0
            for place, size in columns(member):
                slabs_ref[member, :rows, start : start + size] = own_ref[:, place : place + size]
                start += size
            if more:
                slabs_ref[member, rows:, :] = jnp.zeros((more, width), own.dtype)
                for i, extra_ref in enumerate(refs[1:-1]):
                    slabs_ref[member, rows:, i * HEAD : i * HEAD + rows] = jnp.broadcast_to(
                        extra_ref[...], (more, rows)
                    )

    arrays = [own, *extra]
    return pl.pallas_call(
        kernel,
        out_shape=jax.ShapeDtypeStruct((MEMBERS, rows + more, width), own.dtype),
        in_specs=[VMEM] * len(arrays),
        out_specs=VMEM,
    )(*arrays)


def pair_up(index, mine, theirs):
    return jnp.where(index == 0, jnp.stack([mine, theirs]), jnp.stack([theirs, mine]))


def row_copies(places_ref, pieces, whole_ref, sems, rows):
    sources = [(piece, start) for piece in pieces for start in range(0, piece.shape[0], rows)]
    return [
        pltpu.make_async_copy(
            piece.at[pl.ds(start, rows)],
            whole_ref.at[pl.ds(pl.multiple_of(places_ref[n] * rows, rows), rows)],
            sems.at[n],
        )
        for n, (piece, start) in enumerate(sources)
    ]


def place_rows(places, pieces, rows):
    count = sum(piece.shape[0] for piece in pieces)

    def kernel(places_ref, *rest):
        whole_ref, sems = rest[-2:]
        copies = row_copies(places_ref, rest[:-2], whole_ref, sems, rows)
        for copy in copies:
            copy.start()
        for copy in copies:
            copy.wait()

    return pl.pallas_call(
        kernel,
        out_shape=jax.ShapeDtypeStruct((count, pieces[0].shape[1]), BF16),
        in_specs=[SMEM] + [HBM] * len(pieces),
        out_specs=VMEM,
        scratch_shapes=[pltpu.SemaphoreType.DMA((count // rows,))],
        compiler_params=pltpu.CompilerParams(vmem_limit_bytes=16 << 20),
    )(places, *pieces)


def place_columns(slabs, own, gain, columns):
    rows = own.shape[0]
    sources = [(i, lane) for i, slab in enumerate(slabs) for lane in range(0, slab.shape[2], HEAD)]

    def kernel(*refs):
        slab_refs, (own_ref, gain_ref, whole_ref, sum_ref) = refs[: len(slabs)], refs[len(slabs) :]
        total = jnp.zeros((rows, HEAD), F32)
        for member in range(MEMBERS):
            places = [place + lane for place, size in columns(member) for lane in range(0, size, HEAD)]
            for place, (i, lane) in zip(places, sources):
                part = slab_refs[i][member, :, lane : lane + HEAD].astype(F32)
                whole_ref[:, place : place + HEAD] = part
                total = total + part * own_ref[:, place : place + HEAD].astype(F32)
        sum_ref[...] = jnp.sum(total, axis=1, keepdims=True) / gain_ref[...]

    return pl.pallas_call(
        kernel,
        out_shape=[jax.ShapeDtypeStruct(own.shape, F32), jax.ShapeDtypeStruct((rows, 1), F32)],
        in_specs=[VMEM] * (len(slabs) + 2),
        out_specs=[VMEM] * 2,
        compiler_params=pltpu.CompilerParams(vmem_limit_bytes=32 << 20),
    )(*slabs, own, gain)


def give(index, bits, grad):
    return swap(lax.dynamic_index_in_dim(grad, 1 - index, 0, False), bits)


def half_sum(first, second, grad, came):
    outer, inner, width = grad.shape[1], grad.shape[3], grad.shape[4]
    mine = lax.dynamic_slice(grad, (first, 0, second, 0, 0), (1, outer, 1, inner, width))
    theirs = lax.dynamic_slice(came, (0, second, 0, 0), (outer, 1, inner, width))
    shape = (outer, inner, width)
    return mine.reshape(shape).astype(F32) + theirs.reshape(shape).astype(F32)


def give_sum(first, second, bits, grad, came):
    return swap(half_sum(first, 1 - second, grad, came).astype(BF16), bits)


def keep_sum(first, second, grad, came, far):
    return half_sum(first, second, grad, came) + far.astype(F32)


def turn(vectors, cosine, sine):
    return vectors * cosine + pltpu.roll(vectors, HEAD // 2, 1) * sine


def block_mask(ends_ref, block):
    first_end, second_end = ends_ref[0], ends_ref[1]
    place = lax.broadcasted_iota(jnp.int32, (BLOCK, 1), 0) + block * BLOCK
    key_place = lax.broadcasted_iota(jnp.int32, (1, (block + 1) * BLOCK), 1)
    start = jnp.where(place < first_end, 0, jnp.where(place < second_end, first_end, second_end))
    return (key_place <= place) & (key_place >= start)


def masked_probs(queries, keys, allowed):
    scores = lax.dot_general(queries, keys, (((1,), (1,)), ((), ())), preferred_element_type=F32)
    scores = jnp.where(allowed, scores * HEAD ** (-0.5), MASKED)
    weights = jnp.exp(scores - jnp.max(scores, axis=-1, keepdims=True))
    return weights * (1.0 / jnp.sum(weights, axis=-1, keepdims=True))


BLOCK = 256


def attention_forward(ends, places, normal, pieces, cosine, sine):
    count, depth = normal.shape
    width = pieces[0].shape[1] // 3
    block_rows = depth // 8

    def kernel(ends_ref, places_ref, normal_ref, cos_ref, sin_ref, *rest):
        piece_refs, (q_ref, k_ref, v_ref, out_ref, weight_ref, sems) = rest[: len(pieces)], rest[len(pieces) :]
        copies = row_copies(places_ref, piece_refs, weight_ref, sems, block_rows)
        for copy in copies:
            copy.start()
        for copy in copies:
            copy.wait()

        @pl.loop(0, count // BLOCK)
        def _(block):
            here = pl.ds(pl.multiple_of(block * BLOCK, BLOCK), BLOCK)
            mixed = jnp.dot(normal_ref[here, :], weight_ref[...], preferred_element_type=F32)
            cos, sin = cos_ref[here, :], sin_ref[here, :]
            v_ref[here, :] = mixed[:, 2 * width :].astype(BF16)
            for head in range(width // HEAD):
                span = slice(head * HEAD, (head + 1) * HEAD)
                key_span = slice(width + head * HEAD, width + (head + 1) * HEAD)
                q_ref[here, span] = turn(mixed[:, span], cos, sin).astype(BF16)
                k_ref[here, span] = turn(mixed[:, key_span], cos, sin).astype(BF16)

        for block in range(count // BLOCK):
            here, keys = slice(block * BLOCK, (block + 1) * BLOCK), slice(0, (block + 1) * BLOCK)
            allowed = block_mask(ends_ref, block)
            for head in range(width // HEAD):
                span = slice(head * HEAD, (head + 1) * HEAD)
                probs = masked_probs(q_ref[here, span], k_ref[keys, span], allowed)
                out_ref[here, span] = jnp.dot(
                    probs.astype(BF16), v_ref[keys, span], preferred_element_type=F32
                ).astype(BF16)

    return pl.pallas_call(
        kernel,
        out_shape=[jax.ShapeDtypeStruct((count, width), BF16)] * 4
        + [jax.ShapeDtypeStruct((depth, 3 * width), BF16)],
        in_specs=[SMEM] * 2 + [VMEM] * 3 + [HBM] * len(pieces),
        out_specs=[VMEM] * 5,
        scratch_shapes=[pltpu.SemaphoreType.DMA((8,))],
        compiler_params=pltpu.CompilerParams(vmem_limit_bytes=48 << 20),
    )(ends, places, normal, cosine, sine, *pieces)


def attention_backward_heads(ends, queries, keys, values, grad_out, cosine, sine):
    count, width = queries.shape

    def kernel(ends_ref, q_ref, k_ref, v_ref, g_ref, cos_ref, sin_ref, out_ref, gk_ref, gv_ref):
        gk_ref[...] = jnp.zeros_like(gk_ref)
        gv_ref[...] = jnp.zeros_like(gv_ref)

        for block in range(count // BLOCK):
            here, keys = slice(block * BLOCK, (block + 1) * BLOCK), slice(0, (block + 1) * BLOCK)
            allowed = block_mask(ends_ref, block)
            for head in range(width // HEAD):
                span = slice(head * HEAD, (head + 1) * HEAD)
                q, g = q_ref[here, span], g_ref[here, span]
                probs = masked_probs(q, k_ref[keys, span], allowed)
                grad_probs = lax.dot_general(
                    g, v_ref[keys, span], (((1,), (1,)), ((), ())), preferred_element_type=F32
                )
                delta = jnp.sum(probs * grad_probs, axis=-1, keepdims=True)
                grad_scores = (probs * (grad_probs - delta)).astype(BF16)
                grad_query = jnp.dot(grad_scores, k_ref[keys, span], preferred_element_type=F32)
                out_ref[here, span] = turn(
                    grad_query * HEAD ** (-0.5), cos_ref[here, :], -sin_ref[here, :]
                ).astype(BF16)
                over_rows = (((0,), (0,)), ((), ()))
                gk_ref[keys, span] += lax.dot_general(grad_scores, q, over_rows, preferred_element_type=F32)
                gv_ref[keys, span] += lax.dot_general(
                    probs.astype(BF16), g, over_rows, preferred_element_type=F32
                )

        out_ref[:, 2 * width :] = gv_ref[...].astype(BF16)
        for head in range(width // HEAD):
            span = slice(head * HEAD, (head + 1) * HEAD)
            out_ref[:, width + head * HEAD : width + (head + 1) * HEAD] = turn(
                gk_ref[:, span] * HEAD ** (-0.5), cos_ref[...], -sin_ref[...]
            ).astype(BF16)

    return pl.pallas_call(
        kernel,
        out_shape=jax.ShapeDtypeStruct((count, 3 * width), BF16),
        in_specs=[SMEM] + [VMEM] * 6,
        out_specs=VMEM,
        scratch_shapes=[pltpu.VMEM((count, width), F32), pltpu.VMEM((count, width), F32)],
        compiler_params=pltpu.CompilerParams(vmem_limit_bytes=48 << 20),
    )(ends, queries, keys, values, grad_out, cosine, sine)


def norm_parts(values):
    centred = values - jnp.mean(values, axis=-1, keepdims=True)
    inverse = lax.rsqrt(jnp.mean(centred * centred, axis=-1, keepdims=True) + EPSILON)
    return centred * inverse, inverse


def norm_backward(values, scaled):
    normal, inverse = norm_parts(values)
    return inverse * (
        scaled
        - jnp.mean(scaled, axis=-1, keepdims=True)
        - normal * jnp.mean(scaled * normal, axis=-1, keepdims=True)
    )


ROWS = 64


def norm_of(values, gain):
    def kernel(values_ref, gain_ref, out_ref):
        out_ref[...] = (norm_parts(values_ref[...].astype(F32))[0] * gain_ref[...]).astype(BF16)

    count, width = values.shape
    return pl.pallas_call(
        kernel,
        grid=(count // ROWS,),
        out_shape=jax.ShapeDtypeStruct(values.shape, BF16),
        in_specs=[pl.BlockSpec((ROWS, width), lambda i: (i, 0)), pl.BlockSpec((1, width), lambda i: (0, 0))],
        out_specs=pl.BlockSpec((ROWS, width), lambda i: (i, 0)),
    )(values, gain)


def row_kernel(kernel, parts, arrays, gain, outs):
    rows, width = parts.shape[1:]
    whole = pl.BlockSpec((4, ROWS, width), lambda i: (0, i, 0))
    single = pl.BlockSpec((ROWS, width), lambda i: (i, 0))
    return pl.pallas_call(
        kernel,
        grid=(rows // ROWS,),
        out_shape=[jax.ShapeDtypeStruct((rows, width), kind) for kind in outs],
        in_specs=[whole] + [single] * len(arrays) + [pl.BlockSpec((1, width), lambda i: (0, 0))],
        out_specs=[single] * len(outs),
    )(parts, *arrays, gain)


def add_parts(parts_ref):
    total = parts_ref[0].astype(F32)
    for i in range(1, 4):
        total = total + parts_ref[i].astype(F32)
    return total


def middle_rows(parts, inputs, gain):
    def kernel(parts_ref, inputs_ref, gain_ref, middle_ref, normal_ref):
        middle = inputs_ref[...].astype(F32) + add_parts(parts_ref)
        middle_ref[...] = middle
        normal_ref[...] = (norm_parts(middle)[0] * gain_ref[...]).astype(BF16)

    return row_kernel(kernel, parts, [inputs], gain, [F32, BF16])


def grad_middle_rows(parts, middle, cotangent, gain):
    def kernel(parts_ref, middle_ref, cotangent_ref, gain_ref, grad_ref, branch_ref):
        grad = cotangent_ref[...].astype(F32) + norm_backward(middle_ref[...], add_parts(parts_ref) * gain_ref[...])
        grad_ref[...] = grad
        branch_ref[...] = grad.astype(BF16)

    return row_kernel(kernel, parts, [middle, cotangent], gain, [F32, BF16])


def token_grad_rows(parts, inputs, grad_middle, gain):
    def kernel(parts_ref, inputs_ref, middle_ref, gain_ref, grad_ref):
        grad = norm_backward(inputs_ref[...].astype(F32), add_parts(parts_ref) * gain_ref[...])
        grad_ref[...] = (middle_ref[...] + grad).astype(BF16)

    return row_kernel(kernel, parts, [inputs, grad_middle], gain, [BF16])[0]


def feed_forward(normal, grad_activation, places, pieces, piece_rows):
    count, width = normal.shape
    hidden_width = pieces[0].shape[1]
    step_rows = 256
    steps = count // step_rows

    def kernel(places_ref, normal_ref, grad_activation_ref, *rest):
        act_ref, grad_ref, up_out, up_ref, sems, out_sem = rest[len(pieces) :]
        step = pl.program_id(0)
        copies = row_copies(places_ref, rest[: len(pieces)], up_ref, sems, piece_rows)
        back = pltpu.make_async_copy(up_ref, up_out, out_sem)

        @pl.when(step == 0)
        def _():
            for copy in copies:
                copy.start()
            for copy in copies:
                copy.wait()
            back.start()

        hidden = jnp.dot(normal_ref[...], up_ref[...], preferred_element_type=F32)
        scale = math.sqrt(2.0 / math.pi)
        square = hidden * hidden
        tanh = jnp.tanh(scale * hidden * (1.0 + 0.044715 * square))
        act_ref[...] = (0.5 * hidden * (1.0 + tanh)).astype(BF16)
        slope = 0.5 * (1.0 + tanh) + (0.5 * scale) * hidden * (1.0 - tanh * tanh) * (
            1.0 + (3.0 * 0.044715) * square
        )
        grad_ref[...] = (grad_activation_ref[...] * slope).astype(BF16)

        @pl.when(step == steps - 1)
        def _():
            back.wait()

    row_spec = pl.BlockSpec((step_rows, width), lambda i: (i, 0))
    hidden_spec = pl.BlockSpec((step_rows, hidden_width), lambda i: (i, 0))
    return pl.pallas_call(
        kernel,
        grid=(steps,),
        out_shape=[jax.ShapeDtypeStruct((count, hidden_width), BF16)] * 2
        + [jax.ShapeDtypeStruct((width, hidden_width), BF16)],
        in_specs=[SMEM, row_spec, hidden_spec] + [HBM] * len(pieces),
        out_specs=[hidden_spec, hidden_spec, HBM],
        scratch_shapes=[
            pltpu.VMEM((width, hidden_width), BF16),
            pltpu.SemaphoreType.DMA((width // piece_rows,)),
            pltpu.SemaphoreType.DMA,
        ],
        compiler_params=pltpu.CompilerParams(vmem_limit_bytes=48 << 20),
    )(places, normal, grad_activation, *pieces)


def contract_rows(left, right):
    return lax.dot_general(left, right, (((0,), (0,)), ((), ())), preferred_element_type=F32)


def dot_transposed(left, right):
    return lax.dot_general(left, right, (((1,), (1,)), ((), ())), preferred_element_type=F32)


class Step:
    def __init__(self, function, *needs):
        self.function, self.needs, self.made = function, needs, None

    def get(self):
        if self.made is None:
            self.put(self.function(*[need.get() for need in self.needs]))
        return self.made[0]

    def put(self, value):
        self.made = (value,)


def grouped_body(
    tokens_own,
    triple_weight,
    output_weight,
    up_weight,
    down_weight,
    first_gain,
    second_gain,
    cotangent_own,
    frame_counts,
    text_counts,
    action_counts,
):
    rows, width = tokens_own.shape
    count = rows * MEMBERS
    dp, fsdp = lax.axis_index("dp"), lax.axis_index("fsdp")
    x, core = dp >> 1, dp & 1
    zh = fsdp >> 2

    counts = jnp.concatenate(
        [frame_counts.reshape(-1), text_counts.reshape(-1), action_counts.reshape(-1)]
    )
    counts = jnp.where(core == zh, counts, swap(counts, CORE))
    frames = counts[:2]
    slots = text_counts.shape[-1]
    texts = counts[2 : 2 + 2 * slots].reshape(2, slots)
    actions = counts[2 + 2 * slots :].reshape(2, slots)
    live = jnp.arange(slots, dtype=jnp.int32) < frames[:, None]
    lengths = jnp.sum(jnp.where(live, IMG + texts + actions, 0), axis=-1)
    first_end = lengths[0]
    second_end = lengths[0] + lengths[1]
    pack_ends = jnp.stack([first_end, second_end]).astype(jnp.int32)
    places = jnp.arange(count, dtype=jnp.int32)
    starts = jnp.where(places < first_end, 0, jnp.where(places < second_end, first_end, second_end))
    cosine_table, sine_table = rotary_tables(places - starts)
    cosine_table = jnp.concatenate([cosine_table[:, 0], cosine_table[:, 0]], axis=1)
    sine_table = jnp.concatenate([-sine_table[:, 0], sine_table[:, 0]], axis=1)

    sides = ((0, 0), (0, 1), (1, 0), (1, 1))
    rows_of_weight = triple_weight.shape[0]
    block = rows_of_weight * 4
    quarter = down_weight.shape[0] // 4
    hidden_width = up_weight.shape[1] // DEVICES
    triple_columns = lambda m: head_columns(m, width)
    up_columns = lambda m: hidden_columns(m, hidden_width)
    first_column = first_gain.astype(F32)[:, None]
    second_column = second_gain.astype(F32)[:, None]

    def places_of(pieces):
        return jnp.stack([place for a, b, parts in pieces for place in parts(x ^ a, zh ^ b)]).astype(jnp.int32)

    def column_places(*which):
        return lambda sx, sz: [sx * 4 + c * 2 + sz for c in which]

    def down_places(*which):
        return lambda sx, sz: [(sx * 2 + sz) * 4 + q for q in which]

    tokens, cotangent = Step(lambda: tokens_own), Step(lambda: cotangent_own)
    down_own, output_own = Step(lambda: down_weight), Step(lambda: output_weight)
    ends, cosine, sine = Step(lambda: pack_ends), Step(lambda: cosine_table), Step(lambda: sine_table)

    triple_dealt = Step(lambda: deal_columns(triple_weight, triple_columns, [first_gain[None], second_gain[None]]))
    triple_all = Step(lambda a: exchange(a, CORE, ZL, Y), triple_dealt)
    triple_own = Step(lambda a: a[:, :rows_of_weight].reshape(-1, a.shape[-1]), triple_all)
    triple_x = Step(lambda a: swap(a, X), triple_own)
    triple_half = [Step(lambda a, h=h: a[h * block : (h + 1) * block], triple_own) for h in range(2)]
    triple_zh = [Step(lambda a: swap(a, ZH), half) for half in triple_half]
    triple_xz = [Step(lambda a: swap(a, X), half) for half in triple_zh]
    inputs = Step(regroup, tokens)
    all_inputs = Step(lambda a: gather(a, CORE, ZL, Y), inputs)
    gains_own = Step(
        lambda a: jnp.concatenate(
            [a[:, rows_of_weight, i * HEAD : i * HEAD + rows_of_weight] for i in range(2)], axis=1
        ),
        triple_all,
    )
    gains_pair = Step(lambda a: pair_up(zh, a, swap(a, ZH)), gains_own)

    def whole_gains(pair):
        whole = pair_up(x, pair, swap(pair, X)).reshape(2, 2, 2, 4, 2, -1)
        return whole.transpose(4, 0, 2, 1, 3, 5).reshape(2, -1).astype(F32)

    gains = Step(whole_gains, gains_pair)
    normal = Step(lambda a, gains: norm_of(a, gains[:1]), all_inputs, gains)
    own_cotangent = Step(regroup, cotangent)
    all_cotangent = Step(lambda a: gather(a, CORE, ZL, Y), own_cotangent)
    turned = Step(lambda a: lax.ppermute(a, AXES, turn_pairs()), output_own)
    turned_zh = Step(lambda a: swap(a, ZH), turned)
    turned_pair = Step(lambda a, b: pair_up(zh, a, b), turned, turned_zh)
    turned_x = Step(lambda a: swap(a, X), turned_pair)

    def whole_output(pair, pair_x):
        whole = jnp.where(x == 0, jnp.stack([pair, pair_x], axis=1), jnp.stack([pair_x, pair], axis=1))
        return whole.reshape(-1, width)

    output = Step(whole_output, turned_pair, turned_x)
    down_x = Step(lambda a: swap(a, X), down_own)
    down_part = [Step(lambda a, q=q: a[q * quarter : (q + 1) * quarter], down_own) for q in range(4)]
    down_zh = [Step(lambda a: swap(a, ZH), part) for part in down_part]
    down_xz = [Step(lambda a: swap(a, X), part) for part in down_zh]

    def whole_down(own, own_x, *rest):
        places = [(0, 0, down_places(0, 1, 2, 3)), (1, 0, down_places(0, 1, 2, 3))]
        places += [(0, 1, down_places(q)) for q in range(4)] + [(1, 1, down_places(q)) for q in range(4)]
        return place_rows(places_of(places), [own, own_x, *rest], quarter)

    down = Step(whole_down, down_own, down_x, *down_zh, *down_xz)
    grad_activation = Step(dot_transposed, all_cotangent, down)
    up_dealt = Step(lambda: deal_columns(up_weight, up_columns))
    up_own = Step(lambda a: exchange(a, CORE, ZL, Y).reshape(-1, a.shape[-1]), up_dealt)
    up_x = Step(lambda a: swap(a, X), up_own)
    up_half = [Step(lambda a, h=h: a[h * block : (h + 1) * block], up_own) for h in range(2)]
    up_zh = [Step(lambda a: swap(a, ZH), half) for half in up_half]
    up_xz = [Step(lambda a: swap(a, X), half) for half in up_zh]

    halved = [(0, 0, column_places(0, 1)), (0, 1, column_places(0)), (0, 1, column_places(1))]
    halved += [(1, 0, column_places(0, 1)), (1, 1, column_places(0)), (1, 1, column_places(1))]

    def attend(ends, normal, cosine, sine, *pieces):
        return attention_forward(ends, places_of(halved), normal, list(pieces), cosine, sine)

    attention = Step(attend, ends, normal, cosine, sine, triple_own, *triple_zh, triple_x, *triple_xz)
    attended_partial = Step(lambda a, output: product_sums(core, a[3], output), attention, output)
    attended_sums = Step(collect, attended_partial)
    middle = Step(lambda a, inputs, gains: middle_rows(a, inputs, gains[1:]), attended_sums, inputs, gains)
    normal_two = Step(lambda a: gather(a[1], CORE, ZL, Y), middle)

    def feed(normal_two, grad_activation, *pieces):
        return feed_forward(normal_two, grad_activation, places_of(halved), list(pieces), block)

    forward = Step(feed, normal_two, grad_activation, up_own, *up_zh, up_x, *up_xz)

    def columns(left, right, start, stop, shape):
        return contract_rows(left, right[:, start:stop]).astype(BF16).reshape(*shape, -1, stop - start)

    class Reduction:
        def __init__(self, kept, one, two, sent=None, index=None):
            (side, bits), (other, other_bits) = one, two
            index = side if index is None else index
            self.kept = kept
            self.sent = sent or Step(lambda a: lax.dynamic_index_in_dim(a, 1 - side, 0, False), kept)
            self.came = Step(lambda a: swap(a, bits), self.sent)
            self.half = Step(lambda a, came: half_sum(index, 1 - other, a, came).astype(BF16), kept, self.came)
            self.far = Step(lambda a: swap(a, other_bits), self.half)
            self.total = Step(lambda a, came, far: keep_sum(index, other, a, came, far), kept, self.came, self.far)

    over_x, over_zh = (x, X), (zh, ZH)

    def x_first(left, right, pick, start, lanes, shape):
        def side(index):
            def product(a, b):
                whole, columns_of = pick(a, b)
                half = whole.shape[1] // 2
                own = lax.dynamic_slice_in_dim(whole, index * half, half, 1)
                return columns(own, columns_of, start * HEAD, (start + lanes) * HEAD, (1,) + shape)

            return product

        sent = Step(lambda a, b: side(1 - x)(a, b)[0], left, right)
        return Reduction(Step(side(x), left, right), over_x, over_zh, sent, 0)

    def zh_first(left, right, pick, start, lanes, shape):
        def product(a, b):
            return columns(*pick(a, b), start * HEAD, (start + lanes) * HEAD, (2,) + shape).swapaxes(0, 2)

        return Reduction(Step(product, left, right), over_zh, over_x)

    def slabs(parts):
        parts = [part.astype(BF16).reshape(MEMBERS, -1, part.shape[-1]) for part in parts]
        return exchange(jnp.concatenate(parts, axis=2), CORE, ZL, Y)

    hidden_partial = Step(lambda a: product_sums(core, a[1], a[2], True), forward)
    hidden_sums = Step(collect, hidden_partial)
    down_pick, down_shape = lambda a, b: (a[0], b), (1, 2)
    grad_down = [
        x_first(forward, all_cotangent, down_pick, 0, 12, down_shape),
        zh_first(forward, all_cotangent, down_pick, 12, 4, down_shape),
    ]
    down_out = Step(
        lambda *parts: jnp.concatenate([part[0] for part in parts], axis=1), *[part.total for part in grad_down]
    )
    up_pick, up_shape = lambda a, b: (a, b[1]), (2, 2)
    grad_up = [x_first(normal_two, forward, up_pick, start, 4, up_shape) for start in (0, 4)]
    up_slabs = Step(lambda *parts: slabs(parts), *[part.total for part in grad_up])
    up_out = Step(lambda a: place_columns([a], up_weight, second_column, up_columns), up_slabs)
    layer_partial = Step(lambda a, down: product_sums(core, a[0], down), forward, down)
    layer_sums = Step(collect, layer_partial)
    layer_rows = Step(
        lambda a, middle: (middle[0] + jnp.sum(a.astype(F32), axis=0)).astype(BF16), layer_sums, middle
    )
    layer_output = Step(regroup, layer_rows)
    grad_middle = Step(
        lambda a, middle, cot, gains: grad_middle_rows(a, middle[0], cot, gains[1:]),
        hidden_sums,
        middle,
        own_cotangent,
        gains,
    )
    grad_branch = Step(lambda a: gather(a[1], CORE, ZL, Y), grad_middle)
    grad_attended = Step(lambda a, output: dot_transposed(a, output).astype(BF16), grad_branch, output)
    grad_mixed = Step(
        lambda ends, a, grad, cosine, sine: attention_backward_heads(ends, a[0], a[1], a[2], grad, cosine, sine),
        ends,
        attention,
        grad_attended,
        cosine,
        sine,
    )
    output_term = Reduction(
        Step(
            lambda a, b: contract_rows(a[3], b).astype(BF16).reshape(2, 2, -1, width).swapaxes(0, 1)[:, None],
            attention,
            grad_branch,
        ),
        over_x,
        over_zh,
    )
    output_grad = Step(
        lambda a: lax.ppermute(a[0].astype(BF16), AXES, turn_pairs()).astype(F32), output_term.total
    )
    mixed_partial = Step(lambda a, b: product_sums(core, a, b[4], True), grad_mixed, attention)
    mixed_sums = Step(collect, mixed_partial)
    token_rows = Step(
        lambda a, inputs, middle, gains: token_grad_rows(a, inputs, middle[0], gains[:1]),
        mixed_sums,
        inputs,
        grad_middle,
        gains,
    )
    token_grad = Step(regroup, token_rows)
    grad_triple = [x_first(normal, grad_mixed, lambda a, b: (a, b), 0, 6, (2, 2))]
    triple_slabs = Step(lambda *parts: slabs(parts), *[part.total for part in grad_triple])
    triple_out = Step(lambda a: place_columns([a], triple_weight, first_column, triple_columns), triple_slabs)

    windows = [
        (
            [
                triple_own, triple_half[0], triple_half[1], gains_own, inputs, own_cotangent, down_x, turned,
                ends, down_part[0], down_part[1], down_part[2], down_part[3], up_dealt,
            ],
            [],
        ),
        (
            [all_inputs, triple_zh[0], triple_zh[1], triple_x, gains_pair, gains, cosine, sine],
            [down_part[0], turned],
        ),
        (
            [triple_xz[0], triple_xz[1], turned_zh, turned_pair, down_zh[0], normal],
            [
                cosine, down_part[1], down_part[2], ends, sine, triple_own, triple_x, triple_zh[0],
                triple_zh[1], up_dealt,
            ],
        ),
        (
            [up_own, up_half[0], up_half[1], turned_x, output, down_zh[1], down_zh[2], down_xz[0], attention],
            [down_part[3]],
        ),
        (
            [attended_partial, attended_sums, up_zh[0], up_x, down_zh[3], down_xz[1], down_xz[2]],
            [down_own, down_x, down_xz[0], down_zh[0], down_zh[1], down_zh[2], gains, inputs, up_half[1]],
        ),
        (
            [middle, normal_two, up_zh[1], up_xz[0], down_xz[3], up_xz[1], down, grad_activation],
            [up_own, up_x, up_zh[0]],
        ),
        (
            [forward],
            [all_cotangent],
        ),
        (
            [hidden_partial, grad_down[0].sent],
            [all_cotangent, forward, normal_two],
        ),
        (
            [
                hidden_sums, grad_down[1].kept, grad_down[0].came, grad_down[1].came, grad_up[0].sent,
                grad_down[0].kept,
            ],
            [down, forward, gains, middle, normal_two, own_cotangent],
        ),
        (
            [
                grad_middle, grad_branch, grad_up[0].came, grad_down[1].far, grad_down[0].far, grad_up[1].sent,
                grad_up[1].kept, layer_partial, grad_up[0].kept,
            ],
            [attention, cosine, ends, normal, output, sine],
        ),
        (
            [
                layer_sums, grad_up[1].came, grad_up[0].far, grad_attended, grad_mixed, mixed_partial,
                grad_triple[0].sent,
            ],
            [attention, grad_branch, normal],
        ),
        (
            [
                mixed_sums, grad_triple[0].came, grad_up[1].far, layer_output, grad_triple[0].kept,
                output_term.kept,
            ],
            [gains, grad_middle, inputs],
        ),
        (
            [grad_triple[0].far, output_term.came, token_rows, up_slabs],
            [],
        ),
    ]
    for made, held in windows:
        values = together(*[step.get() for step in made + held])
        for step, value in zip(made + held, values):
            step.put(value)
    return (
        layer_output.get(),
        token_grad.get(),
        triple_out.get()[0],
        output_grad.get(),
        up_out.get()[0],
        down_out.get(),
        triple_out.get()[1][:, 0],
        up_out.get()[1][:, 0],
    )


def solution(mesh):
    grouped = mesh.shape["dp"] * 2 == mesh.shape["fsdp"] == MEMBERS
    rows = P(AXES, None)
    return jax.shard_map(
        grouped_body if grouped else whole_rows_body,
        mesh=mesh,
        in_specs=(rows,) * 5 + (P(AXES),) * 2 + (rows, P("dp", None), P("dp", None, None), P("dp", None, None)),
        out_specs=(rows,) * 6 + (P(AXES),) * 2,
        check_vma=False,
    )
```

```python
import math

import jax
import jax.numpy as jnp
from jax import lax
from jax.experimental import pallas as pl
from jax.experimental.pallas import tpu as pltpu
from jax.sharding import PartitionSpec as P

HEADS = 16
HEAD = 128
IMG = 576


EPSILON = 1e-05
MASKED = -1e30


def clip_layout(frame_counts, text_counts, action_counts, pack_length):
    frame_slot = jnp.arange(text_counts.shape[-1], dtype=jnp.int32)
    frame_live = frame_slot < frame_counts[..., None]
    frame_sizes = jnp.where(frame_live, IMG + text_counts + action_counts, 0)
    clip_lengths = jnp.sum(frame_sizes, axis=-1)
    first_end = clip_lengths[..., 0:1]
    second_end = first_end + clip_lengths[..., 1:2]
    places = jnp.arange(pack_length, dtype=jnp.int32)
    segment = (places >= first_end).astype(jnp.int32) + (places >= second_end).astype(jnp.int32)
    starts = jnp.where(segment == 0, 0, jnp.where(segment == 1, first_end, second_end))
    return (segment, places - starts)


def rotary_tables(position):
    half_width = HEAD // 2
    frequency = jnp.exp(
        jnp.arange(half_width, dtype=jnp.float32) * (-2.0 * math.log(10000.0) / HEAD)
    )
    angles = position.astype(jnp.float32)[:, None] * frequency[None, :]
    return (jnp.cos(angles)[:, None, :], jnp.sin(angles)[:, None, :])


def rotate(vectors, cosine, sine_table):
    half_width = vectors.shape[-1] // 2
    former = vectors[..., :half_width]
    latter = vectors[..., half_width:]
    return jnp.concatenate(
        [former * cosine - latter * sine_table, latter * cosine + former * sine_table], axis=-1
    )


def unrotate(gradient, cosine, sine_table):
    half_width = gradient.shape[-1] // 2
    former = gradient[..., :half_width]
    latter = gradient[..., half_width:]
    return jnp.concatenate(
        [former * cosine + latter * sine_table, latter * cosine - former * sine_table], axis=-1
    )


def norm_rows(values, gain_vector):
    centred = values - jnp.mean(values, axis=-1, keepdims=True)
    variance = jnp.mean(centred * centred, axis=-1, keepdims=True)
    return centred * lax.rsqrt(variance + EPSILON) * gain_vector


def block_allowed(query_segment, query_places, key_segment, key_place):
    return (query_segment[:, None] == key_segment[None, :]) & (
        key_place[None, :] <= query_places[:, None]
    )


def block_scores(queries, key_block, allowed):
    scores = jnp.einsum(
        "qhd,khd->hqk", queries, key_block, preferred_element_type=jnp.float32
    ) * HEAD ** (-0.5)
    return jnp.where(allowed[None], scores, MASKED)


def block_probs(queries, key_block, allowed, row_max, row_sum):
    scores = block_scores(queries, key_block, allowed)
    return jnp.where(allowed[None], jnp.exp(scores - row_max[..., None]) / row_sum[..., None], 0.0)


def softmax_stats(queries, key_blocks, layout_parts):
    query_segment, query_places, key_segments, key_places = layout_parts
    row_count, head_count = (queries.shape[0], queries.shape[1])
    start_state = (
        jnp.full((head_count, row_count), MASKED, jnp.float32),
        jnp.zeros((head_count, row_count), jnp.float32),
    )

    def advance(state, block_inputs):
        key_block, key_segment, key_place = block_inputs
        allowed = block_allowed(query_segment, query_places, key_segment, key_place)

        def update(current):
            row_max, row_sum = current
            scores = block_scores(queries, key_block, allowed)
            new_max = jnp.maximum(row_max, jnp.max(scores, axis=-1))
            weights = jnp.where(allowed[None], jnp.exp(scores - new_max[..., None]), 0.0)
            return (new_max, row_sum * jnp.exp(row_max - new_max) + jnp.sum(weights, axis=-1))

        return (lax.cond(jnp.any(allowed), update, lambda current: current, state), None)

    final_state, unused = lax.scan(advance, start_state, (key_blocks, key_segments, key_places))
    return final_state


def attention_output(queries, key_blocks, value_blocks, layout_parts, row_max, row_sum):
    query_segment, query_places, key_segments, key_places = layout_parts

    def advance(accum, block_inputs):
        key_block, value_block, key_segment, key_place = block_inputs
        allowed = block_allowed(query_segment, query_places, key_segment, key_place)

        def update(current):
            probs = block_probs(queries, key_block, allowed, row_max, row_sum).astype(jnp.bfloat16)
            return current + jnp.einsum(
                "hqk,khd->qhd", probs, value_block, preferred_element_type=jnp.float32
            )

        return (lax.cond(jnp.any(allowed), update, lambda current: current, accum), None)

    attended, unused = lax.scan(
        advance,
        jnp.zeros(queries.shape, jnp.float32),
        (key_blocks, value_blocks, key_segments, key_places),
    )
    return attended


def attention_backward(
    queries, grad_attended, delta_rows, key_blocks, value_blocks, layout_parts, row_max, row_sum
):
    query_segment, query_places, key_segments, key_places = layout_parts
    score_scale = HEAD ** (-0.5)

    def advance(grad_query, block_inputs):
        key_block, value_block, key_segment, key_place = block_inputs
        allowed = block_allowed(query_segment, query_places, key_segment, key_place)

        def update(current):
            probs = block_probs(queries, key_block, allowed, row_max, row_sum)
            grad_probs = jnp.einsum(
                "qhd,khd->hqk", grad_attended, value_block, preferred_element_type=jnp.float32
            )
            grad_scores = (probs * (grad_probs - delta_rows[..., None])).astype(jnp.bfloat16)
            new_query = (
                current
                + jnp.einsum(
                    "hqk,khd->qhd", grad_scores, key_block, preferred_element_type=jnp.float32
                )
                * score_scale
            )
            return (new_query, ())

        def bypass(current):
            return (current, ())

        return lax.cond(jnp.any(allowed), update, bypass, grad_query)

    grad_query, terms = lax.scan(
        advance,
        jnp.zeros(queries.shape, jnp.float32),
        (key_blocks, value_blocks, key_segments, key_places),
    )
    return (grad_query, None, None)


def project_front(inputs, triple_full, gain_full, cosine, sine_table):
    row_count, width = inputs.shape
    normed = norm_rows(inputs, gain_full.astype(jnp.float32)).astype(jnp.bfloat16)
    mixed = jnp.dot(normed, triple_full, preferred_element_type=jnp.float32)
    queries = rotate(mixed[:, :width].reshape(row_count, HEADS, HEAD), cosine, sine_table).astype(
        jnp.bfloat16
    )
    keys_local = (
        rotate(mixed[:, width : 2 * width].reshape(row_count, HEADS, HEAD), cosine, sine_table)
        .astype(jnp.bfloat16)
        .reshape(row_count, width)
    )
    values_local = mixed[:, 2 * width :].astype(jnp.bfloat16)
    return (normed, queries, keys_local, values_local)


def run_attention(queries, gathered, layout_parts):
    block_count = layout_parts[2].shape[0]
    key_blocks = gathered[0].reshape(block_count, -1, HEADS, HEAD)
    value_blocks = gathered[1].reshape(block_count, -1, HEADS, HEAD)
    row_max, row_sum = softmax_stats(queries, key_blocks, layout_parts)
    attended = attention_output(queries, key_blocks, value_blocks, layout_parts, row_max, row_sum)
    return (attended, key_blocks, value_blocks, row_max, row_sum)


def finish_layer(inputs, attended, output_full, up_full, down_full, second_full):
    row_count, width = inputs.shape
    attended_low = attended.reshape(row_count, width).astype(jnp.bfloat16)
    middle = inputs + jnp.dot(attended_low, output_full, preferred_element_type=jnp.float32)
    normed_two = norm_rows(middle, second_full.astype(jnp.float32)).astype(jnp.bfloat16)
    hidden = jnp.dot(normed_two, up_full, preferred_element_type=jnp.float32)
    activation = jax.nn.gelu(hidden).astype(jnp.bfloat16)
    result = middle + jnp.dot(activation, down_full, preferred_element_type=jnp.float32)
    return (result, attended_low, middle, normed_two, hidden, activation)


def whole_rows_body(
    tokens,
    triple_weight,
    output_weight,
    up_weight,
    down_weight,
    first_gain,
    second_gain,
    cotangent,
    frame_counts,
    text_counts,
    action_counts,
):
    row_count, width = tokens.shape
    pack_length = row_count * lax.axis_size("fsdp")
    first_place = lax.axis_index("fsdp") * row_count
    segment, position = clip_layout(frame_counts[0], text_counts[0], action_counts[0], pack_length)
    block_rows = min(1024, pack_length)
    block_count = pack_length // block_rows
    query_places = first_place + jnp.arange(row_count, dtype=jnp.int32)
    own_segment = lax.dynamic_slice_in_dim(segment, first_place, row_count, 0)
    layout_parts = (
        own_segment,
        query_places,
        segment.reshape(block_count, block_rows),
        jnp.arange(pack_length, dtype=jnp.int32).reshape(block_count, block_rows),
    )
    cosine, sine_table = rotary_tables(
        lax.dynamic_slice_in_dim(position, first_place, row_count, 0)
    )
    inputs = tokens.astype(jnp.float32)
    attention_set = (
        lax.all_gather(triple_weight, ("dp", "fsdp"), axis=0, tiled=True),
        lax.all_gather(output_weight, ("dp", "fsdp"), axis=0, tiled=True),
        lax.all_gather(first_gain, ("dp", "fsdp"), axis=0, tiled=True),
    )
    normed, queries, keys_local, values_local = project_front(
        inputs, attention_set[0], attention_set[2], cosine, sine_table
    )
    gathered = (
        lax.all_gather(keys_local, "fsdp", axis=0, tiled=True),
        lax.all_gather(values_local, "fsdp", axis=0, tiled=True),
    )
    attended, key_blocks, value_blocks, row_max, row_sum = run_attention(
        queries, gathered, layout_parts
    )
    feedforward_set = (
        lax.all_gather(up_weight, ("dp", "fsdp"), axis=0, tiled=True),
        lax.all_gather(down_weight, ("dp", "fsdp"), axis=0, tiled=True),
        lax.all_gather(second_gain, ("dp", "fsdp"), axis=0, tiled=True),
    )
    kept_parts = finish_layer(
        inputs,
        attended,
        attention_set[1],
        feedforward_set[0],
        feedforward_set[1],
        feedforward_set[2],
    )
    layer_output = kept_parts[0].astype(jnp.bfloat16)
    attention_set = (
        lax.all_gather(triple_weight, ("dp", "fsdp"), axis=0, tiled=True),
        lax.all_gather(output_weight, ("dp", "fsdp"), axis=0, tiled=True),
        lax.all_gather(first_gain, ("dp", "fsdp"), axis=0, tiled=True),
    )
    normed, queries, keys_local, values_local = project_front(
        inputs, attention_set[0], attention_set[2], cosine, sine_table
    )
    gathered = (
        lax.all_gather(keys_local, "fsdp", axis=0, tiled=True),
        lax.all_gather(values_local, "fsdp", axis=0, tiled=True),
    )
    attended, key_blocks, value_blocks, row_max, row_sum = run_attention(
        queries, gathered, layout_parts
    )
    feedforward_set = (
        lax.all_gather(up_weight, ("dp", "fsdp"), axis=0, tiled=True),
        lax.all_gather(down_weight, ("dp", "fsdp"), axis=0, tiled=True),
        lax.all_gather(second_gain, ("dp", "fsdp"), axis=0, tiled=True),
    )
    kept_parts = finish_layer(
        inputs,
        attended,
        attention_set[1],
        feedforward_set[0],
        feedforward_set[1],
        feedforward_set[2],
    )
    unused_result, attended_low, middle, normed_two, hidden, activation = kept_parts
    down_term = jnp.einsum("rf,rd->fd", activation, cotangent, preferred_element_type=jnp.float32)
    grad_activation = jnp.einsum(
        "rd,fd->rf", cotangent, feedforward_set[1], preferred_element_type=jnp.float32
    )
    unused_gelu, gelu_pull = jax.vjp(jax.nn.gelu, hidden)
    grad_hidden = gelu_pull(grad_activation)[0].astype(jnp.bfloat16)
    up_term = jnp.einsum("rd,rf->df", normed_two, grad_hidden, preferred_element_type=jnp.float32)
    grad_normed_two = jnp.einsum(
        "rf,df->rd", grad_hidden, feedforward_set[0], preferred_element_type=jnp.float32
    )
    unused_second, second_pull = jax.vjp(norm_rows, middle, feedforward_set[2].astype(jnp.float32))
    grad_middle_norm, second_gain_term = second_pull(grad_normed_two)
    grad_middle = cotangent.astype(jnp.float32) + grad_middle_norm
    feedforward_sums = (
        lax.psum_scatter(up_term, ("dp", "fsdp"), scatter_dimension=0, tiled=True),
        lax.psum_scatter(down_term, ("dp", "fsdp"), scatter_dimension=0, tiled=True),
        lax.psum_scatter(second_gain_term, ("dp", "fsdp"), scatter_dimension=0, tiled=True),
    )
    grad_branch = grad_middle.astype(jnp.bfloat16)
    output_term = jnp.einsum(
        "rd,re->de", attended_low, grad_branch, preferred_element_type=jnp.float32
    )
    grad_attended = (
        jnp.einsum("re,de->rd", grad_branch, attention_set[1], preferred_element_type=jnp.float32)
        .astype(jnp.bfloat16)
        .reshape(row_count, HEADS, HEAD)
    )
    delta_rows = jnp.sum(grad_attended.astype(jnp.float32) * attended, axis=-1).T
    score_scale = HEAD ** (-0.5)
    grad_query = attention_backward(
        queries, grad_attended, delta_rows, key_blocks, value_blocks, layout_parts, row_max, row_sum
    )[0]
    pack_stats = (
        lax.all_gather(row_max.T, "fsdp", axis=0, tiled=True),
        lax.all_gather(row_sum.T, "fsdp", axis=0, tiled=True),
        lax.all_gather(delta_rows.T, "fsdp", axis=0, tiled=True),
    )
    own_keys = keys_local.reshape(row_count, HEADS, HEAD)
    own_values = values_local.reshape(row_count, HEADS, HEAD)
    empty_grads = jnp.zeros((row_count, HEADS, HEAD), jnp.float32)
    query_piece = lax.all_gather(queries, "fsdp", axis=0, tiled=True)
    grad_piece = lax.all_gather(grad_attended, "fsdp", axis=0, tiled=True)
    piece_rows = query_piece.shape[0]
    block_size = min(1024, piece_rows)
    block_total = piece_rows // block_size

    def advance(current, block_index):
        offset = block_index * block_size
        query_part = lax.dynamic_slice_in_dim(query_piece, offset, block_size, 0)
        grad_part = lax.dynamic_slice_in_dim(grad_piece, offset, block_size, 0)
        max_part = lax.dynamic_slice_in_dim(pack_stats[0], offset, block_size, 0).T
        sum_part = lax.dynamic_slice_in_dim(pack_stats[1], offset, block_size, 0).T
        delta_part = lax.dynamic_slice_in_dim(pack_stats[2], offset, block_size, 0).T
        part_segment = lax.dynamic_slice_in_dim(segment, offset, block_size, 0)
        part_places = offset + jnp.arange(block_size, dtype=jnp.int32)
        allowed = block_allowed(part_segment, part_places, own_segment, query_places)

        def update(pair):
            probs = block_probs(query_part, own_keys, allowed, max_part, sum_part)
            grad_probs = jnp.einsum(
                "qhd,khd->hqk", grad_part, own_values, preferred_element_type=jnp.float32
            )
            grad_scores = (probs * (grad_probs - delta_part[..., None])).astype(jnp.bfloat16)
            grad_key = (
                pair[0]
                + jnp.einsum(
                    "hqk,qhd->khd", grad_scores, query_part, preferred_element_type=jnp.float32
                )
                * score_scale
            )
            grad_value = pair[1] + jnp.einsum(
                "hqk,qhd->khd",
                probs.astype(jnp.bfloat16),
                grad_part,
                preferred_element_type=jnp.float32,
            )
            return (grad_key, grad_value)

        return (lax.cond(jnp.any(allowed), update, lambda pair: pair, current), None)

    result, unused = lax.scan(
        advance, (empty_grads, empty_grads), jnp.arange(block_total, dtype=jnp.int32)
    )
    key_grad_sum = result[0].reshape(row_count, width)
    value_grad_sum = result[1].reshape(row_count, width)
    grad_query_full = (
        unrotate(grad_query, cosine, sine_table).reshape(row_count, width).astype(jnp.bfloat16)
    )
    grad_key_full = (
        unrotate(key_grad_sum.reshape(row_count, HEADS, HEAD), cosine, sine_table)
        .reshape(row_count, width)
        .astype(jnp.bfloat16)
    )
    grad_value_full = value_grad_sum.astype(jnp.bfloat16)
    grad_mixed = jnp.concatenate([grad_query_full, grad_key_full, grad_value_full], axis=1)
    triple_term = jnp.einsum("rd,re->de", normed, grad_mixed, preferred_element_type=jnp.float32)
    grad_normed = jnp.einsum(
        "re,de->rd", grad_mixed, attention_set[0], preferred_element_type=jnp.float32
    )
    unused_first, first_pull = jax.vjp(norm_rows, inputs, attention_set[2].astype(jnp.float32))
    grad_input_norm, first_gain_term = first_pull(grad_normed)
    token_grad = (grad_middle + grad_input_norm).astype(jnp.bfloat16)
    attention_sums = (
        lax.psum_scatter(triple_term, ("dp", "fsdp"), scatter_dimension=0, tiled=True),
        lax.psum_scatter(output_term, ("dp", "fsdp"), scatter_dimension=0, tiled=True),
        lax.psum_scatter(first_gain_term, ("dp", "fsdp"), scatter_dimension=0, tiled=True),
    )
    return (
        layer_output,
        token_grad,
        attention_sums[0],
        attention_sums[1],
        feedforward_sums[0],
        feedforward_sums[1],
        attention_sums[2],
        feedforward_sums[2],
    )


AXES = ("dp", "fsdp")
DEVICES = 32
MEMBERS = 8
CORE, ZL, Y = 8, 2, 1
X, ZH = 16, 4
BF16 = jnp.bfloat16
F32 = jnp.float32
SMEM = pl.BlockSpec(memory_space=pltpu.SMEM)
VMEM = pl.BlockSpec(memory_space=pltpu.VMEM)
HBM = pl.BlockSpec(memory_space=pltpu.HBM)


def swap(array, bits):
    return lax.ppermute(array, AXES, [(i, i ^ bits) for i in range(DEVICES)])


def alike(*bits):
    groups = {}
    for i in range(DEVICES):
        groups.setdefault(i & ~sum(bits), []).append(i)
    return list(groups.values())


def exchange(array, *bits):
    return lax.all_to_all(array, AXES, 0, 0, tiled=True, axis_index_groups=alike(*bits))


def after(array, *others):
    return lax.optimization_barrier((array,) + others)[0]


def together(*arrays):
    return lax.optimization_barrier(arrays)


def regroup_pairs():
    def target(i):
        x, core, zh, low = i >> 4, (i >> 3) & 1, (i >> 2) & 1, i & 3
        return (x << 4) | (zh << 3) | (core << 2) | low

    return [(i, target(i)) for i in range(DEVICES)]


def regroup(array):
    return lax.ppermute(array, AXES, regroup_pairs())


def turn_pairs():
    return [(i, (i & 14) | (i & 1) << 4 | i >> 4) for i in range(DEVICES)]


def gather(own, *bits):
    return lax.all_gather(own, AXES, axis=0, tiled=True, axis_index_groups=alike(*bits))


def collect(parts):
    return exchange(parts.reshape(4, -1, parts.shape[1]), ZL, Y)


def row_product(half, left, right, transposed, came=None):
    count, depth = left.shape[0] // 2, left.shape[1]
    width = right.shape[0] if transposed else right.shape[1]
    tile = 512

    def kernel(half_ref, left_ref, right_ref, *rest):
        if transposed:
            total = dot_transposed(left_ref[...], right_ref[...])
        else:
            total = jnp.dot(left_ref[...], right_ref[...], preferred_element_type=F32)
        if came is not None:
            total = total + rest[0][...].astype(F32)
        rest[-1][...] = total.astype(BF16)

    columns = pl.BlockSpec((count, tile), lambda i, half_ref: (0, i))
    if transposed:
        right_spec = pl.BlockSpec((tile, depth), lambda i, half_ref: (i, 0))
    else:
        right_spec = pl.BlockSpec((depth, tile), lambda i, half_ref: (0, i))
    more = [] if came is None else [came]
    return pl.pallas_call(
        kernel,
        grid_spec=pltpu.PrefetchScalarGridSpec(
            num_scalar_prefetch=1,
            grid=(width // tile,),
            in_specs=[pl.BlockSpec((count, depth), lambda i, half_ref: (half_ref[0], 0)), right_spec]
            + [columns] * len(more),
            out_specs=columns,
        ),
        out_shape=jax.ShapeDtypeStruct((count, width), BF16),
        compiler_params=pltpu.CompilerParams(vmem_limit_bytes=32 << 20),
    )(half, left, right, *more)


def product_sums(core, rows, right, transposed=False):
    near, far = core.reshape(1), (1 - core).reshape(1)
    came = swap(row_product(far, rows, right, transposed), CORE)
    return row_product(near, rows, right, transposed, came)


def hidden_columns(member, width):
    core, zl, y = (member >> 2) & 1, (member >> 1) & 1, member & 1
    return [
        ((gx * X + core * CORE + gz * ZH + zl * ZL + y) * width, width)
        for gx in range(2)
        for gz in range(2)
    ]


def head_columns(member, width):
    core, zl, y = (member >> 2) & 1, (member >> 1) & 1, member & 1
    return [
        (part * width + ((y * 2 + core) * 4 + half * 2 + zl) * HEAD, HEAD)
        for part in range(3)
        for half in range(2)
    ]


def deal_columns(own, columns, extra=()):
    rows = own.shape[0]
    width = own.shape[1] // MEMBERS
    more = 16 if extra else 0

    def kernel(*refs):
        own_ref, slabs_ref = refs[0], refs[-1]
        for member in range(MEMBERS):
            start = 0
            for place, size in columns(member):
                slabs_ref[member, :rows, start : start + size] = own_ref[:, place : place + size]
                start += size
            if more:
                slabs_ref[member, rows:, :] = jnp.zeros((more, width), own.dtype)
                for i, extra_ref in enumerate(refs[1:-1]):
                    slabs_ref[member, rows:, i * HEAD : i * HEAD + rows] = jnp.broadcast_to(
                        extra_ref[...], (more, rows)
                    )

    arrays = [own, *extra]
    return pl.pallas_call(
        kernel,
        out_shape=jax.ShapeDtypeStruct((MEMBERS, rows + more, width), own.dtype),
        in_specs=[VMEM] * len(arrays),
        out_specs=VMEM,
    )(*arrays)


def pair_up(index, mine, theirs):
    return jnp.where(index == 0, jnp.stack([mine, theirs]), jnp.stack([theirs, mine]))


def row_copies(places_ref, pieces, whole_ref, sems, rows):
    sources = [(piece, start) for piece in pieces for start in range(0, piece.shape[0], rows)]
    return [
        pltpu.make_async_copy(
            piece.at[pl.ds(start, rows)],
            whole_ref.at[pl.ds(pl.multiple_of(places_ref[n] * rows, rows), rows)],
            sems.at[n],
        )
        for n, (piece, start) in enumerate(sources)
    ]


def place_rows(places, pieces, rows):
    count = sum(piece.shape[0] for piece in pieces)

    def kernel(places_ref, *rest):
        whole_ref, sems = rest[-2:]
        copies = row_copies(places_ref, rest[:-2], whole_ref, sems, rows)
        for copy in copies:
            copy.start()
        for copy in copies:
            copy.wait()

    return pl.pallas_call(
        kernel,
        out_shape=jax.ShapeDtypeStruct((count, pieces[0].shape[1]), BF16),
        in_specs=[SMEM] + [HBM] * len(pieces),
        out_specs=VMEM,
        scratch_shapes=[pltpu.SemaphoreType.DMA((count // rows,))],
        compiler_params=pltpu.CompilerParams(vmem_limit_bytes=16 << 20),
    )(places, *pieces)


def place_columns(slabs, own, gain, columns):
    rows = own.shape[0]
    sources = [(i, lane) for i, slab in enumerate(slabs) for lane in range(0, slab.shape[2], HEAD)]

    def kernel(*refs):
        slab_refs, (own_ref, gain_ref, whole_ref, sum_ref) = refs[: len(slabs)], refs[len(slabs) :]
        total = jnp.zeros((rows, HEAD), F32)
        for member in range(MEMBERS):
            places = [place + lane for place, size in columns(member) for lane in range(0, size, HEAD)]
            for place, (i, lane) in zip(places, sources):
                part = slab_refs[i][member, :, lane : lane + HEAD].astype(F32)
                whole_ref[:, place : place + HEAD] = part
                total = total + part * own_ref[:, place : place + HEAD].astype(F32)
        sum_ref[...] = jnp.sum(total, axis=1, keepdims=True) / gain_ref[...]

    return pl.pallas_call(
        kernel,
        out_shape=[jax.ShapeDtypeStruct(own.shape, F32), jax.ShapeDtypeStruct((rows, 1), F32)],
        in_specs=[VMEM] * (len(slabs) + 2),
        out_specs=[VMEM] * 2,
        compiler_params=pltpu.CompilerParams(vmem_limit_bytes=32 << 20),
    )(*slabs, own, gain)


def give(index, bits, grad):
    return swap(lax.dynamic_index_in_dim(grad, 1 - index, 0, False), bits)


def half_sum(first, second, grad, came):
    outer, inner, width = grad.shape[1], grad.shape[3], grad.shape[4]
    mine = lax.dynamic_slice(grad, (first, 0, second, 0, 0), (1, outer, 1, inner, width))
    theirs = lax.dynamic_slice(came, (0, second, 0, 0), (outer, 1, inner, width))
    shape = (outer, inner, width)
    return mine.reshape(shape).astype(F32) + theirs.reshape(shape).astype(F32)


def give_sum(first, second, bits, grad, came):
    return swap(half_sum(first, 1 - second, grad, came).astype(BF16), bits)


def keep_sum(first, second, grad, came, far):
    return half_sum(first, second, grad, came) + far.astype(F32)


def turn(vectors, cosine, sine):
    return vectors * cosine + pltpu.roll(vectors, HEAD // 2, 1) * sine


def block_mask(ends_ref, block):
    first_end, second_end = ends_ref[0], ends_ref[1]
    place = lax.broadcasted_iota(jnp.int32, (BLOCK, 1), 0) + block * BLOCK
    key_place = lax.broadcasted_iota(jnp.int32, (1, (block + 1) * BLOCK), 1)
    start = jnp.where(place < first_end, 0, jnp.where(place < second_end, first_end, second_end))
    return (key_place <= place) & (key_place >= start)


def masked_probs(queries, keys, allowed):
    scores = lax.dot_general(queries, keys, (((1,), (1,)), ((), ())), preferred_element_type=F32)
    scores = jnp.where(allowed, scores * HEAD ** (-0.5), MASKED)
    weights = jnp.exp(scores - jnp.max(scores, axis=-1, keepdims=True))
    return weights * (1.0 / jnp.sum(weights, axis=-1, keepdims=True))


BLOCK = 256


def attention_forward(ends, places, normal, pieces, cosine, sine):
    count, depth = normal.shape
    width = pieces[0].shape[1] // 3
    block_rows = depth // 8

    def kernel(ends_ref, places_ref, normal_ref, cos_ref, sin_ref, *rest):
        piece_refs, (q_ref, k_ref, v_ref, out_ref, weight_ref, sems) = rest[: len(pieces)], rest[len(pieces) :]
        copies = row_copies(places_ref, piece_refs, weight_ref, sems, block_rows)
        for copy in copies:
            copy.start()
        for copy in copies:
            copy.wait()

        @pl.loop(0, count // BLOCK)
        def _(block):
            here = pl.ds(pl.multiple_of(block * BLOCK, BLOCK), BLOCK)
            mixed = jnp.dot(normal_ref[here, :], weight_ref[...], preferred_element_type=F32)
            cos, sin = cos_ref[here, :], sin_ref[here, :]
            v_ref[here, :] = mixed[:, 2 * width :].astype(BF16)
            for head in range(width // HEAD):
                span = slice(head * HEAD, (head + 1) * HEAD)
                key_span = slice(width + head * HEAD, width + (head + 1) * HEAD)
                q_ref[here, span] = turn(mixed[:, span], cos, sin).astype(BF16)
                k_ref[here, span] = turn(mixed[:, key_span], cos, sin).astype(BF16)

        for block in range(count // BLOCK):
            here, keys = slice(block * BLOCK, (block + 1) * BLOCK), slice(0, (block + 1) * BLOCK)
            allowed = block_mask(ends_ref, block)
            for head in range(width // HEAD):
                span = slice(head * HEAD, (head + 1) * HEAD)
                probs = masked_probs(q_ref[here, span], k_ref[keys, span], allowed)
                out_ref[here, span] = jnp.dot(
                    probs.astype(BF16), v_ref[keys, span], preferred_element_type=F32
                ).astype(BF16)

    return pl.pallas_call(
        kernel,
        out_shape=[jax.ShapeDtypeStruct((count, width), BF16)] * 4
        + [jax.ShapeDtypeStruct((depth, 3 * width), BF16)],
        in_specs=[SMEM] * 2 + [VMEM] * 3 + [HBM] * len(pieces),
        out_specs=[VMEM] * 5,
        scratch_shapes=[pltpu.SemaphoreType.DMA((8,))],
        compiler_params=pltpu.CompilerParams(vmem_limit_bytes=48 << 20),
    )(ends, places, normal, cosine, sine, *pieces)


def attention_backward_heads(ends, queries, keys, values, grad_out, cosine, sine):
    count, width = queries.shape

    def kernel(ends_ref, q_ref, k_ref, v_ref, g_ref, cos_ref, sin_ref, out_ref, gk_ref, gv_ref):
        gk_ref[...] = jnp.zeros_like(gk_ref)
        gv_ref[...] = jnp.zeros_like(gv_ref)

        for block in range(count // BLOCK):
            here, keys = slice(block * BLOCK, (block + 1) * BLOCK), slice(0, (block + 1) * BLOCK)
            allowed = block_mask(ends_ref, block)
            for head in range(width // HEAD):
                span = slice(head * HEAD, (head + 1) * HEAD)
                q, g = q_ref[here, span], g_ref[here, span]
                probs = masked_probs(q, k_ref[keys, span], allowed)
                grad_probs = lax.dot_general(
                    g, v_ref[keys, span], (((1,), (1,)), ((), ())), preferred_element_type=F32
                )
                delta = jnp.sum(probs * grad_probs, axis=-1, keepdims=True)
                grad_scores = (probs * (grad_probs - delta)).astype(BF16)
                grad_query = jnp.dot(grad_scores, k_ref[keys, span], preferred_element_type=F32)
                out_ref[here, span] = turn(
                    grad_query * HEAD ** (-0.5), cos_ref[here, :], -sin_ref[here, :]
                ).astype(BF16)
                over_rows = (((0,), (0,)), ((), ()))
                gk_ref[keys, span] += lax.dot_general(grad_scores, q, over_rows, preferred_element_type=F32)
                gv_ref[keys, span] += lax.dot_general(
                    probs.astype(BF16), g, over_rows, preferred_element_type=F32
                )

        out_ref[:, 2 * width :] = gv_ref[...].astype(BF16)
        for head in range(width // HEAD):
            span = slice(head * HEAD, (head + 1) * HEAD)
            out_ref[:, width + head * HEAD : width + (head + 1) * HEAD] = turn(
                gk_ref[:, span] * HEAD ** (-0.5), cos_ref[...], -sin_ref[...]
            ).astype(BF16)

    return pl.pallas_call(
        kernel,
        out_shape=jax.ShapeDtypeStruct((count, 3 * width), BF16),
        in_specs=[SMEM] + [VMEM] * 6,
        out_specs=VMEM,
        scratch_shapes=[pltpu.VMEM((count, width), F32), pltpu.VMEM((count, width), F32)],
        compiler_params=pltpu.CompilerParams(vmem_limit_bytes=48 << 20),
    )(ends, queries, keys, values, grad_out, cosine, sine)


def norm_parts(values):
    centred = values - jnp.mean(values, axis=-1, keepdims=True)
    inverse = lax.rsqrt(jnp.mean(centred * centred, axis=-1, keepdims=True) + EPSILON)
    return centred * inverse, inverse


def norm_backward(values, scaled):
    normal, inverse = norm_parts(values)
    return inverse * (
        scaled
        - jnp.mean(scaled, axis=-1, keepdims=True)
        - normal * jnp.mean(scaled * normal, axis=-1, keepdims=True)
    )


ROWS = 64


def norm_of(values, gain):
    def kernel(values_ref, gain_ref, out_ref):
        out_ref[...] = (norm_parts(values_ref[...].astype(F32))[0] * gain_ref[...]).astype(BF16)

    count, width = values.shape
    return pl.pallas_call(
        kernel,
        grid=(count // ROWS,),
        out_shape=jax.ShapeDtypeStruct(values.shape, BF16),
        in_specs=[pl.BlockSpec((ROWS, width), lambda i: (i, 0)), pl.BlockSpec((1, width), lambda i: (0, 0))],
        out_specs=pl.BlockSpec((ROWS, width), lambda i: (i, 0)),
    )(values, gain)


def row_kernel(kernel, parts, arrays, gain, outs):
    rows, width = parts.shape[1:]
    whole = pl.BlockSpec((4, ROWS, width), lambda i: (0, i, 0))
    single = pl.BlockSpec((ROWS, width), lambda i: (i, 0))
    return pl.pallas_call(
        kernel,
        grid=(rows // ROWS,),
        out_shape=[jax.ShapeDtypeStruct((rows, width), kind) for kind in outs],
        in_specs=[whole] + [single] * len(arrays) + [pl.BlockSpec((1, width), lambda i: (0, 0))],
        out_specs=[single] * len(outs),
    )(parts, *arrays, gain)


def add_parts(parts_ref):
    total = parts_ref[0].astype(F32)
    for i in range(1, 4):
        total = total + parts_ref[i].astype(F32)
    return total


def middle_rows(parts, inputs, gain):
    def kernel(parts_ref, inputs_ref, gain_ref, middle_ref, normal_ref):
        middle = inputs_ref[...].astype(F32) + add_parts(parts_ref)
        middle_ref[...] = middle
        normal_ref[...] = (norm_parts(middle)[0] * gain_ref[...]).astype(BF16)

    return row_kernel(kernel, parts, [inputs], gain, [F32, BF16])


def grad_middle_rows(parts, middle, cotangent, gain):
    def kernel(parts_ref, middle_ref, cotangent_ref, gain_ref, grad_ref, branch_ref):
        grad = cotangent_ref[...].astype(F32) + norm_backward(middle_ref[...], add_parts(parts_ref) * gain_ref[...])
        grad_ref[...] = grad
        branch_ref[...] = grad.astype(BF16)

    return row_kernel(kernel, parts, [middle, cotangent], gain, [F32, BF16])


def token_grad_rows(parts, inputs, grad_middle, gain):
    def kernel(parts_ref, inputs_ref, middle_ref, gain_ref, grad_ref):
        grad = norm_backward(inputs_ref[...].astype(F32), add_parts(parts_ref) * gain_ref[...])
        grad_ref[...] = (middle_ref[...] + grad).astype(BF16)

    return row_kernel(kernel, parts, [inputs, grad_middle], gain, [BF16])[0]


def feed_forward(normal, grad_activation, places, pieces, piece_rows):
    count, width = normal.shape
    hidden_width = pieces[0].shape[1]
    step_rows = 256
    steps = count // step_rows

    def kernel(places_ref, normal_ref, grad_activation_ref, *rest):
        act_ref, grad_ref, up_out, up_ref, sems, out_sem = rest[len(pieces) :]
        step = pl.program_id(0)
        copies = row_copies(places_ref, rest[: len(pieces)], up_ref, sems, piece_rows)
        back = pltpu.make_async_copy(up_ref, up_out, out_sem)

        @pl.when(step == 0)
        def _():
            for copy in copies:
                copy.start()
            for copy in copies:
                copy.wait()
            back.start()

        hidden = jnp.dot(normal_ref[...], up_ref[...], preferred_element_type=F32)
        scale = math.sqrt(2.0 / math.pi)
        square = hidden * hidden
        tanh = jnp.tanh(scale * hidden * (1.0 + 0.044715 * square))
        act_ref[...] = (0.5 * hidden * (1.0 + tanh)).astype(BF16)
        slope = 0.5 * (1.0 + tanh) + (0.5 * scale) * hidden * (1.0 - tanh * tanh) * (
            1.0 + (3.0 * 0.044715) * square
        )
        grad_ref[...] = (grad_activation_ref[...] * slope).astype(BF16)

        @pl.when(step == steps - 1)
        def _():
            back.wait()

    row_spec = pl.BlockSpec((step_rows, width), lambda i: (i, 0))
    hidden_spec = pl.BlockSpec((step_rows, hidden_width), lambda i: (i, 0))
    return pl.pallas_call(
        kernel,
        grid=(steps,),
        out_shape=[jax.ShapeDtypeStruct((count, hidden_width), BF16)] * 2
        + [jax.ShapeDtypeStruct((width, hidden_width), BF16)],
        in_specs=[SMEM, row_spec, hidden_spec] + [HBM] * len(pieces),
        out_specs=[hidden_spec, hidden_spec, HBM],
        scratch_shapes=[
            pltpu.VMEM((width, hidden_width), BF16),
            pltpu.SemaphoreType.DMA((width // piece_rows,)),
            pltpu.SemaphoreType.DMA,
        ],
        compiler_params=pltpu.CompilerParams(vmem_limit_bytes=48 << 20),
    )(places, normal, grad_activation, *pieces)


def contract_rows(left, right):
    return lax.dot_general(left, right, (((0,), (0,)), ((), ())), preferred_element_type=F32)


def dot_transposed(left, right):
    return lax.dot_general(left, right, (((1,), (1,)), ((), ())), preferred_element_type=F32)


class Step:
    def __init__(self, function, *needs):
        self.function, self.needs, self.made = function, needs, None

    def get(self):
        if self.made is None:
            self.put(self.function(*[need.get() for need in self.needs]))
        return self.made[0]

    def put(self, value):
        self.made = (value,)


def grouped_body(
    tokens_own,
    triple_weight,
    output_weight,
    up_weight,
    down_weight,
    first_gain,
    second_gain,
    cotangent_own,
    frame_counts,
    text_counts,
    action_counts,
):
    rows, width = tokens_own.shape
    count = rows * MEMBERS
    dp, fsdp = lax.axis_index("dp"), lax.axis_index("fsdp")
    x, core = dp >> 1, dp & 1
    zh = fsdp >> 2

    counts = jnp.concatenate(
        [frame_counts.reshape(-1), text_counts.reshape(-1), action_counts.reshape(-1)]
    )
    counts = jnp.where(core == zh, counts, swap(counts, CORE))
    frames = counts[:2]
    slots = text_counts.shape[-1]
    texts = counts[2 : 2 + 2 * slots].reshape(2, slots)
    actions = counts[2 + 2 * slots :].reshape(2, slots)
    live = jnp.arange(slots, dtype=jnp.int32) < frames[:, None]
    lengths = jnp.sum(jnp.where(live, IMG + texts + actions, 0), axis=-1)
    first_end = lengths[0]
    second_end = lengths[0] + lengths[1]
    pack_ends = jnp.stack([first_end, second_end]).astype(jnp.int32)
    places = jnp.arange(count, dtype=jnp.int32)
    starts = jnp.where(places < first_end, 0, jnp.where(places < second_end, first_end, second_end))
    cosine_table, sine_table = rotary_tables(places - starts)
    cosine_table = jnp.concatenate([cosine_table[:, 0], cosine_table[:, 0]], axis=1)
    sine_table = jnp.concatenate([-sine_table[:, 0], sine_table[:, 0]], axis=1)

    sides = ((0, 0), (0, 1), (1, 0), (1, 1))
    rows_of_weight = triple_weight.shape[0]
    block = rows_of_weight * 4
    quarter = down_weight.shape[0] // 4
    hidden_width = up_weight.shape[1] // DEVICES
    triple_columns = lambda m: head_columns(m, width)
    up_columns = lambda m: hidden_columns(m, hidden_width)
    first_column = first_gain.astype(F32)[:, None]
    second_column = second_gain.astype(F32)[:, None]

    def places_of(pieces):
        return jnp.stack([place for a, b, parts in pieces for place in parts(x ^ a, zh ^ b)]).astype(jnp.int32)

    def column_places(*which):
        return lambda sx, sz: [sx * 4 + c * 2 + sz for c in which]

    def down_places(*which):
        return lambda sx, sz: [(sx * 2 + sz) * 4 + q for q in which]

    tokens, cotangent = Step(lambda: tokens_own), Step(lambda: cotangent_own)
    down_own, output_own = Step(lambda: down_weight), Step(lambda: output_weight)
    ends, cosine, sine = Step(lambda: pack_ends), Step(lambda: cosine_table), Step(lambda: sine_table)

    triple_dealt = Step(lambda: deal_columns(triple_weight, triple_columns, [first_gain[None], second_gain[None]]))
    triple_all = Step(lambda a: exchange(a, CORE, ZL, Y), triple_dealt)
    triple_own = Step(lambda a: a[:, :rows_of_weight].reshape(-1, a.shape[-1]), triple_all)
    triple_x = Step(lambda a: swap(a, X), triple_own)
    triple_half = [Step(lambda a, h=h: a[h * block : (h + 1) * block], triple_own) for h in range(2)]
    triple_zh = [Step(lambda a: swap(a, ZH), half) for half in triple_half]
    triple_xz = [Step(lambda a: swap(a, X), half) for half in triple_zh]
    inputs = Step(regroup, tokens)
    all_inputs = Step(lambda a: gather(a, CORE, ZL, Y), inputs)
    gains_own = Step(
        lambda a: jnp.concatenate(
            [a[:, rows_of_weight, i * HEAD : i * HEAD + rows_of_weight] for i in range(2)], axis=1
        ),
        triple_all,
    )
    gains_pair = Step(lambda a: pair_up(zh, a, swap(a, ZH)), gains_own)

    def whole_gains(pair):
        whole = pair_up(x, pair, swap(pair, X)).reshape(2, 2, 2, 4, 2, -1)
        return whole.transpose(4, 0, 2, 1, 3, 5).reshape(2, -1).astype(F32)

    gains = Step(whole_gains, gains_pair)
    normal = Step(lambda a, gains: norm_of(a, gains[:1]), all_inputs, gains)
    own_cotangent = Step(regroup, cotangent)
    all_cotangent = Step(lambda a: gather(a, CORE, ZL, Y), own_cotangent)
    turned = Step(lambda a: lax.ppermute(a, AXES, turn_pairs()), output_own)
    turned_zh = Step(lambda a: swap(a, ZH), turned)
    turned_pair = Step(lambda a, b: pair_up(zh, a, b), turned, turned_zh)
    turned_x = Step(lambda a: swap(a, X), turned_pair)

    def whole_output(pair, pair_x):
        whole = jnp.where(x == 0, jnp.stack([pair, pair_x], axis=1), jnp.stack([pair_x, pair], axis=1))
        return whole.reshape(-1, width)

    output = Step(whole_output, turned_pair, turned_x)
    down_x = Step(lambda a: swap(a, X), down_own)
    down_part = [Step(lambda a, q=q: a[q * quarter : (q + 1) * quarter], down_own) for q in range(4)]
    down_zh = [Step(lambda a: swap(a, ZH), part) for part in down_part]
    down_xz = [Step(lambda a: swap(a, X), part) for part in down_zh]

    def whole_down(own, own_x, *rest):
        places = [(0, 0, down_places(0, 1, 2, 3)), (1, 0, down_places(0, 1, 2, 3))]
        places += [(0, 1, down_places(q)) for q in range(4)] + [(1, 1, down_places(q)) for q in range(4)]
        return place_rows(places_of(places), [own, own_x, *rest], quarter)

    down = Step(whole_down, down_own, down_x, *down_zh, *down_xz)
    grad_activation = Step(dot_transposed, all_cotangent, down)
    up_dealt = Step(lambda: deal_columns(up_weight, up_columns))
    up_own = Step(lambda a: exchange(a, CORE, ZL, Y).reshape(-1, a.shape[-1]), up_dealt)
    up_x = Step(lambda a: swap(a, X), up_own)
    up_half = [Step(lambda a, h=h: a[h * block : (h + 1) * block], up_own) for h in range(2)]
    up_zh = [Step(lambda a: swap(a, ZH), half) for half in up_half]
    up_xz = [Step(lambda a: swap(a, X), half) for half in up_zh]

    halved = [(0, 0, column_places(0, 1)), (0, 1, column_places(0)), (0, 1, column_places(1))]
    halved += [(1, 0, column_places(0, 1)), (1, 1, column_places(0)), (1, 1, column_places(1))]

    def attend(ends, normal, cosine, sine, *pieces):
        return attention_forward(ends, places_of(halved), normal, list(pieces), cosine, sine)

    attention = Step(attend, ends, normal, cosine, sine, triple_own, *triple_zh, triple_x, *triple_xz)
    attended_partial = Step(lambda a, output: product_sums(core, a[3], output), attention, output)
    attended_sums = Step(collect, attended_partial)
    middle = Step(lambda a, inputs, gains: middle_rows(a, inputs, gains[1:]), attended_sums, inputs, gains)
    normal_two = Step(lambda a: gather(a[1], CORE, ZL, Y), middle)

    def feed(normal_two, grad_activation, *pieces):
        return feed_forward(normal_two, grad_activation, places_of(halved), list(pieces), block)

    forward = Step(feed, normal_two, grad_activation, up_own, *up_zh, up_x, *up_xz)

    def columns(left, right, start, stop, shape):
        return contract_rows(left, right[:, start:stop]).astype(BF16).reshape(*shape, -1, stop - start)

    class Reduction:
        def __init__(self, kept, one, two, sent=None, index=None):
            (side, bits), (other, other_bits) = one, two
            index = side if index is None else index
            self.kept = kept
            self.sent = sent or Step(lambda a: lax.dynamic_index_in_dim(a, 1 - side, 0, False), kept)
            self.came = Step(lambda a: swap(a, bits), self.sent)
            self.half = Step(lambda a, came: half_sum(index, 1 - other, a, came).astype(BF16), kept, self.came)
            self.far = Step(lambda a: swap(a, other_bits), self.half)
            self.total = Step(lambda a, came, far: keep_sum(index, other, a, came, far), kept, self.came, self.far)

    over_x, over_zh = (x, X), (zh, ZH)

    def x_first(left, right, pick, start, lanes, shape):
        def side(index):
            def product(a, b):
                whole, columns_of = pick(a, b)
                half = whole.shape[1] // 2
                own = lax.dynamic_slice_in_dim(whole, index * half, half, 1)
                return columns(own, columns_of, start * HEAD, (start + lanes) * HEAD, (1,) + shape)

            return product

        sent = Step(lambda a, b: side(1 - x)(a, b)[0], left, right)
        return Reduction(Step(side(x), left, right), over_x, over_zh, sent, 0)

    def zh_first(left, right, pick, start, lanes, shape):
        def product(a, b):
            return columns(*pick(a, b), start * HEAD, (start + lanes) * HEAD, (2,) + shape).swapaxes(0, 2)

        return Reduction(Step(product, left, right), over_zh, over_x)

    def slabs(parts):
        parts = [part.astype(BF16).reshape(MEMBERS, -1, part.shape[-1]) for part in parts]
        return exchange(jnp.concatenate(parts, axis=2), CORE, ZL, Y)

    hidden_partial = Step(lambda a: product_sums(core, a[1], a[2], True), forward)
    hidden_sums = Step(collect, hidden_partial)
    down_pick, down_shape = lambda a, b: (a[0], b), (1, 2)
    grad_down = [
        x_first(forward, all_cotangent, down_pick, 0, 12, down_shape),
        zh_first(forward, all_cotangent, down_pick, 12, 4, down_shape),
    ]
    down_out = Step(
        lambda *parts: jnp.concatenate([part[0] for part in parts], axis=1), *[part.total for part in grad_down]
    )
    up_pick, up_shape = lambda a, b: (a, b[1]), (2, 2)
    grad_up = [x_first(normal_two, forward, up_pick, start, 4, up_shape) for start in (0, 4)]
    up_slabs = Step(lambda *parts: slabs(parts), *[part.total for part in grad_up])
    up_out = Step(lambda a: place_columns([a], up_weight, second_column, up_columns), up_slabs)
    layer_partial = Step(lambda a, down: product_sums(core, a[0], down), forward, down)
    layer_sums = Step(collect, layer_partial)
    layer_rows = Step(
        lambda a, middle: (middle[0] + jnp.sum(a.astype(F32), axis=0)).astype(BF16), layer_sums, middle
    )
    layer_output = Step(regroup, layer_rows)
    grad_middle = Step(
        lambda a, middle, cot, gains: grad_middle_rows(a, middle[0], cot, gains[1:]),
        hidden_sums,
        middle,
        own_cotangent,
        gains,
    )
    grad_branch = Step(lambda a: gather(a[1], CORE, ZL, Y), grad_middle)
    grad_attended = Step(lambda a, output: dot_transposed(a, output).astype(BF16), grad_branch, output)
    grad_mixed = Step(
        lambda ends, a, grad, cosine, sine: attention_backward_heads(ends, a[0], a[1], a[2], grad, cosine, sine),
        ends,
        attention,
        grad_attended,
        cosine,
        sine,
    )
    output_term = Reduction(
        Step(
            lambda a, b: contract_rows(a[3], b).astype(BF16).reshape(2, 2, -1, width).swapaxes(0, 1)[:, None],
            attention,
            grad_branch,
        ),
        over_x,
        over_zh,
    )
    output_grad = Step(
        lambda a: lax.ppermute(a[0].astype(BF16), AXES, turn_pairs()).astype(F32), output_term.total
    )
    mixed_partial = Step(lambda a, b: product_sums(core, a, b[4], True), grad_mixed, attention)
    mixed_sums = Step(collect, mixed_partial)
    token_rows = Step(
        lambda a, inputs, middle, gains: token_grad_rows(a, inputs, middle[0], gains[:1]),
        mixed_sums,
        inputs,
        grad_middle,
        gains,
    )
    token_grad = Step(regroup, token_rows)
    grad_triple = [x_first(normal, grad_mixed, lambda a, b: (a, b), 0, 6, (2, 2))]
    triple_slabs = Step(lambda *parts: slabs(parts), *[part.total for part in grad_triple])
    triple_out = Step(lambda a: place_columns([a], triple_weight, first_column, triple_columns), triple_slabs)

    windows = [
        (
            [
                triple_own, triple_half[0], triple_half[1], gains_own, inputs, own_cotangent, down_x, turned,
                ends, down_part[0], down_part[1], down_part[2], down_part[3], up_dealt,
            ],
            [],
        ),
        (
            [all_inputs, triple_zh[0], triple_zh[1], triple_x, gains_pair, gains, cosine, sine],
            [down_part[0], turned],
        ),
        (
            [triple_xz[0], triple_xz[1], turned_zh, turned_pair, down_zh[0], normal],
            [
                cosine, down_part[1], down_part[2], ends, sine, triple_own, triple_x, triple_zh[0],
                triple_zh[1], up_dealt,
            ],
        ),
        (
            [up_own, up_half[0], up_half[1], turned_x, output, down_zh[1], down_zh[2], down_xz[0], attention],
            [down_part[3]],
        ),
        (
            [attended_partial, attended_sums, up_zh[0], up_x, down_zh[3], down_xz[1], down_xz[2]],
            [down_own, down_x, down_xz[0], down_zh[0], down_zh[1], down_zh[2], gains, inputs, up_half[1]],
        ),
        (
            [middle, normal_two, up_zh[1], up_xz[0], down_xz[3], up_xz[1], down, grad_activation],
            [up_own, up_x, up_zh[0]],
        ),
        (
            [forward],
            [all_cotangent, normal_two],
        ),
        (
            [
                hidden_partial, grad_down[0].sent, hidden_sums, grad_down[1].kept, grad_down[0].came,
                grad_down[1].came, grad_up[0].sent, grad_down[0].kept,
            ],
            [down, forward, gains, middle, normal_two, own_cotangent],
        ),
        (
            [
                grad_middle, grad_branch, grad_up[0].came, grad_down[1].far, grad_down[0].far, grad_up[1].sent,
                grad_up[1].kept, layer_partial, grad_up[0].kept,
            ],
            [attention, cosine, ends, normal, output, sine],
        ),
        (
            [
                layer_sums, grad_up[1].came, grad_up[0].far, grad_attended, grad_mixed, mixed_partial,
                grad_triple[0].sent,
            ],
            [attention, grad_branch, normal],
        ),
        (
            [
                mixed_sums, grad_triple[0].came, grad_up[1].far, layer_output, grad_triple[0].kept,
                output_term.kept,
            ],
            [gains, grad_middle, inputs],
        ),
        (
            [grad_triple[0].far, output_term.came, token_rows, up_slabs],
            [],
        ),
    ]
    for made, held in windows:
        values = together(*[step.get() for step in made + held])
        for step, value in zip(made + held, values):
            step.put(value)
    return (
        layer_output.get(),
        token_grad.get(),
        triple_out.get()[0],
        output_grad.get(),
        up_out.get()[0],
        down_out.get(),
        triple_out.get()[1][:, 0],
        up_out.get()[1][:, 0],
    )


def solution(mesh):
    grouped = mesh.shape["dp"] * 2 == mesh.shape["fsdp"] == MEMBERS
    rows = P(AXES, None)
    return jax.shard_map(
        grouped_body if grouped else whole_rows_body,
        mesh=mesh,
        in_specs=(rows,) * 5 + (P(AXES),) * 2 + (rows, P("dp", None), P("dp", None, None), P("dp", None, None)),
        out_specs=(rows,) * 6 + (P(AXES),) * 2,
        check_vma=False,
    )
```
